32 devices in a mesh: wide: 8 (over y, x, core), narrow: 4 (over z).
Axes of the slice: x: 2, y: 2, z: 4, core: 2. Of those that a mesh axis runs over, the one named last changes fastest.
Arguments:
- token_ids: int32 [4096], P(('wide', 'narrow')), may hold values from 0 to 50256
- lengths: int32 [32], P(('wide', 'narrow')), may hold values from 1 to 128, as said below
- top_ids: int32 [4096, 32], P(('wide', 'narrow')), may hold values from 0 to 32767, as said below
- aux_ids: int32 [4096, 512], P(('wide', 'narrow')), may hold values from 0 to 32767, as said below
- dead_set: int32 [32768], replicated, may hold values 0 or 1
- token_table: bfloat16 [50304, 768], P('wide'), may hold values from -6 to 6
- position_table: bfloat16 [1024, 768], replicated, may hold values from -4 to 4
- ln_gains: float32 [2, 768], replicated, may hold values from 0.5 to 1.5
- frozen_bias: float32 [8448], replicated, may hold values from -1.5 to 1.5
- w_qkv: bfloat16 [768, 2304], replicated, may hold values from -0.21875 to 0.21875
- w_proj: bfloat16 [768, 768], replicated, may hold values from -0.21875 to 0.21875
- w_fc: bfloat16 [768, 3072], replicated, may hold values from -0.21875 to 0.21875
- w_out: bfloat16 [3072, 768], replicated, may hold values from -0.109375 to 0.109375
- enc_weight: float32 [768, 32768], P('narrow', 'wide'), may hold values from -0.21875 to 0.21875
- enc_bias: float32 [32768], P(('wide', 'narrow')), may hold values from -4 to 4
- dec_weight: float32 [32768, 768], P('wide', 'narrow'), may hold values from -0.375 to 0.375
- decoder_bias: float32 [768], replicated, may hold values from -4 to 4
- enc_moment: float32 [768, 32768], P('narrow', 'wide'), may hold values from -0.25 to 0.25
- dec_moment: float32 [32768, 768], P('wide', 'narrow'), may hold values from -0.109375 to 0.109375
- encb_first: float32 [32768], P(('wide', 'narrow')), may hold values from -0.01953125 to 0.01953125
- encb_second: float32 [32768], P(('wide', 'narrow')), may hold values from 1.4322917e-07 to 5.729167e-07
- decb_first: float32 [768], replicated, may hold values from -0.375 to 0.375
- decb_second: float32 [768], replicated, may hold values from 5.953836e-05 to 0.00023815344
Outputs:
- token_loss: float32 [4096], P(('wide', 'narrow'))
- enc_new: float32 [768, 32768], P('narrow', 'wide')
- enc_moment_new: float32 [768, 32768], P('narrow', 'wide')
- enc_copy: bfloat16 [768, 32768], P('narrow', 'wide')
- dec_new: float32 [32768, 768], P('wide', 'narrow')
- dec_moment_new: float32 [32768, 768], P('wide', 'narrow')
- dec_copy: bfloat16 [32768, 768], P('wide', 'narrow')
- encb_new: float32 [32768], P(('wide', 'narrow'))
- encb_first_new: float32 [32768], P(('wide', 'narrow'))
- encb_second_new: float32 [32768], P(('wide', 'narrow'))
- decb_new: float32 [768], replicated
- decb_first_new: float32 [768], replicated
- decb_second_new: float32 [768], replicated
The draws below stay inside these ranges and needn't reach their ends.
Inputs may be any that keep to these rules, and one draw needn't show every extreme that they name: `lengths`: the last context has 128 counted tokens. Each row of top_ids and aux_ids together names 544 different latents. `aux_ids`: no aux id of a row equals a top id of that row.
All inputs are finite; a program needn't handle non-finite values.
Results may differ from the reference program's by a relative error of at most 0.014.
Values may be sent and summed in bfloat16 or wider, within the bound.
No kernel may reach another device: no remote copies, remote signals or barrier semaphores. Data moves between devices by JAX's collectives and lax.ppermute only.
A program may use at most 256 MiB of HBM per device.

```python
import math
import jax
import jax.numpy as jnp
import numpy as np
from jax import lax

D = 768
HEADS = 12
HEAD_DIM = 64
FF = 3072
POS = 1024
VOCAB = 50304
L = 32768
ACTIVE_LATENTS = 32
A = 512
NS_STEPS = 5
STEP = 10
TOK_DEV = 128
WIDE_DEVS = 8
NARROW_DEVS = 4
TOKENS = 4096


def draw_lengths(key, part):
    device_ids = jnp.arange(WIDE_DEVS * NARROW_DEVS, dtype=jnp.int32)
    wide_pos = device_ids // NARROW_DEVS
    narrow_pos = device_ids % NARROW_DEVS
    base_len = TOK_DEV * (WIDE_DEVS - 1 + 2 * wide_pos) * (NARROW_DEVS - 1 + 2 * narrow_pos) // (9 * (WIDE_DEVS - 1) * (NARROW_DEVS - 1))
    jitter = jax.random.randint(jax.random.fold_in(key, 3), device_ids.shape, 0, 1 + base_len // 5)
    last_one = device_ids == WIDE_DEVS * NARROW_DEVS - 1
    chosen = jnp.where(last_one, TOK_DEV, base_len - jitter)
    return jnp.maximum(chosen, 1).astype(jnp.int32)


def latent_lists(key):
    first_id = jax.random.randint(jax.random.fold_in(key, 11), (TOKENS, 1), 0, L)
    stride = 2 * jax.random.randint(jax.random.fold_in(key, 12), (TOKENS, 1), 0, L // 2) + 1
    slot_ids = jnp.arange(ACTIVE_LATENTS + A, dtype=jnp.int32)[None, :]
    return ((first_id + stride * slot_ids) % L).astype(jnp.int32)


def draw_top_ids(key, part):
    return latent_lists(key)[:, :ACTIVE_LATENTS]


def draw_aux_ids(key, part):
    return latent_lists(key)[:, ACTIVE_LATENTS:]


def place_ends(drawn, rng, smallest, high):
    spot = [jax.random.randint(jax.random.fold_in(rng, axis), (), 0, length) for axis, length in enumerate(drawn.shape)]
    widest = drawn.shape.index(max(drawn.shape))
    beside = spot[:widest] + [(spot[widest] + 1) % drawn.shape[widest]] + spot[widest + 1:]
    return drawn.at[tuple(spot)].set(smallest).at[tuple(beside)].set(high)


def level_of(rng, extent, cuts, least, top_value):
    level = 1.0
    for dim, parts in cuts:
        draws = jax.random.uniform(jax.random.fold_in(jax.random.fold_in(rng, 6), dim), (parts,), jnp.float32, least / len(cuts), top_value / len(cuts))
        level = level * jnp.repeat(jnp.exp(draws), extent[dim] // parts).reshape((-1,) + (1,) * (len(extent) - 1 - dim))
    return level


def rank_bounds(count, slope):
    portions = [(1 << 20) // math.isqrt(standing ** slope) + 1 for standing in range(1, count + 1)]
    width = 1 + sum(portions) // (1 << 30)
    return np.cumsum(np.array([max(1, weight // width) for weight in portions]))


def ranked_ids(stream_key, shape, amount, lean):
    table = rank_bounds(amount, lean)
    lot = jax.random.randint(jax.random.fold_in(stream_key, 1), shape, 0, int(table[amount - 1]))
    standing = jnp.searchsorted(jnp.asarray(table, jnp.int32), lot, side="right")
    return jax.random.permutation(jax.random.fold_in(stream_key, 2), amount)[standing].astype(jnp.int32)


def bell_draw(rng, extent, spread, most, cuts=(), held_as=jnp.bfloat16):
    factor_of = level_of(rng, extent, cuts, -0.22, 0.18) if cuts else 1.0
    array = jax.random.normal(rng, extent, jnp.float32) * spread * factor_of
    return jnp.minimum(jnp.maximum(array, -most), most).astype(held_as)


def setup_inputs(seed: int = 0) -> dict:
    arg_keys = jax.random.split(jax.random.key(seed), 24)
    token_ids = place_ends(ranked_ids(arg_keys[0], (TOKENS,), min(50257, VOCAB), 2), jax.random.fold_in(arg_keys[0], 3), 0, (min(50257, VOCAB)) - 1).astype(jnp.int32)
    lengths = draw_lengths(jax.random.fold_in(arg_keys[23], 71), 0)
    top_ids = draw_top_ids(jax.random.fold_in(arg_keys[23], 71), 0)
    aux_ids = draw_aux_ids(jax.random.fold_in(arg_keys[23], 71), 0)
    dead_set = place_ends((jax.random.randint(arg_keys[4], (L,), 0, 2) < 1).astype(jnp.int32), jax.random.fold_in(arg_keys[4], 1), 0, 1)
    token_table = bell_draw(arg_keys[5], (VOCAB, D), 1.0, 6.0, ((0, 8),))
    position_table = bell_draw(arg_keys[6], (POS, D), 0.3, 4.0)
    ln_gains = jnp.clip(1.0 + 0.1 * jax.random.normal(arg_keys[7], (2, D), jnp.float32), 0.5, 1.5)
    frozen_bias = bell_draw(arg_keys[8], (7 * D + FF,), 0.1, 1.5, (), jnp.float32)
    w_qkv = bell_draw(arg_keys[9], (D, 3 * D), D ** -0.5, 0.21875)
    w_proj = bell_draw(arg_keys[10], (D, D), D ** -0.5, 0.21875)
    w_fc = bell_draw(arg_keys[11], (D, FF), D ** -0.5, 0.21875)
    w_out = bell_draw(arg_keys[12], (FF, D), FF ** -0.5, 0.109375)
    enc_weight = bell_draw(arg_keys[13], (D, L), D ** -0.5, 0.21875, ((0, 4), (1, 8)), jnp.float32)
    enc_bias = bell_draw(arg_keys[14], (L,), 0.3, 4.0, ((0, 32),), jnp.float32)
    dec_weight = bell_draw(arg_keys[15], (L, D), (8 * ACTIVE_LATENTS) ** -0.5, 0.375, ((0, 8), (1, 4)), jnp.float32)
    decoder_bias = bell_draw(arg_keys[16], (D,), 0.3, 4.0, (), jnp.float32)
    enc_moment = bell_draw(arg_keys[17], (D, L), (0.4 / D ** 0.5 * (0.44 * TOKENS * ACTIVE_LATENTS / L) ** 0.5), 0.25, ((0, 4), (1, 8)), jnp.float32)
    dec_moment = bell_draw(arg_keys[18], (L, D), (4.5 / D * (0.44 * TOKENS * ACTIVE_LATENTS / L) ** 0.5), 0.109375, ((0, 8), (1, 4)), jnp.float32)
    encb_first = bell_draw(arg_keys[19], (L,), (0.03 / D ** 0.5 * (0.44 * TOKENS * ACTIVE_LATENTS / L) ** 0.5), 0.01953125, ((0, 32),), jnp.float32)
    encb_second = jnp.clip(jnp.exp(math.log(5.729166900891869e-07) - 1.3862944 * jax.random.uniform(arg_keys[20], (L,), jnp.float32) ** level_of(arg_keys[20], (L,), ((0, 32),), -0.2, 0.2)), 1.4322917252229672e-07, 5.729166900891869e-07)
    decb_first = bell_draw(arg_keys[21], (D,), (0.11 * (3.0 / D * (0.44 * TOKENS) ** 0.5 + 0.25 / D * (0.44 * TOKENS * ACTIVE_LATENTS) ** 0.5)), 0.375, (), jnp.float32)
    decb_second = jnp.clip(jnp.exp(jax.random.uniform(arg_keys[22], (D,), jnp.float32, math.log(5.9538360801525414e-05), math.log(0.00023815344))), 5.9538360801525414e-05, 0.00023815344)
    return {"token_ids": token_ids, "lengths": lengths, "top_ids": top_ids, "aux_ids": aux_ids, "dead_set": dead_set, "token_table": token_table, "position_table": position_table, "ln_gains": ln_gains, "frozen_bias": frozen_bias, "w_qkv": w_qkv, "w_proj": w_proj, "w_fc": w_fc, "w_out": w_out, "enc_weight": enc_weight, "enc_bias": enc_bias, "dec_weight": dec_weight, "decoder_bias": decoder_bias, "enc_moment": enc_moment, "dec_moment": dec_moment, "encb_first": encb_first, "encb_second": encb_second, "decb_first": decb_first, "decb_second": decb_second}


HIGH_PRECISION = lax.Precision.HIGHEST
AUX_COEF = 1.0 / 32.0
EPS_NORM = 1e-05
NS_EPS = 1e-07
QA = 3.4445
QB = -4.775
QC = 2.0315
MOMENTUM = 0.95
MUON_RATE = 0.1
DECAY = 0.1
BIAS_RATE = 0.3
BETA_ONE = 0.9
BETA_TWO = 0.999
ADAM_EPS = 1e-08

@jax.custom_vjp
def low(v):
    return lax.optimization_barrier(v.astype(jnp.bfloat16)).astype(jnp.float32)

@jax.custom_vjp
def lowered_pullback(v):
    return v

def low_keep(v):
    return (low(v), None)

def low_pass(kept, grad):
    return (grad,)

def back_keep(v):
    return (v, None)

def back_low(kept, grad):
    return (low(grad),)
low.defvjp(low_keep, low_pass)
lowered_pullback.defvjp(back_keep, back_low)

def layer_norm(value, gain, shift):
    row_mean = lax.optimization_barrier(jnp.mean(value, -1, keepdims=True))
    centred = value - row_mean
    row_var = lax.optimization_barrier(jnp.mean(centred * centred, -1, keepdims=True))
    return centred * lax.rsqrt(row_var + EPS_NORM) * gain + shift

def frozen_context(ids_row, ctx_length, token_table, position_table, ln_gains, frozen_bias, w_qkv, w_proj, w_fc, w_out):
    row_count = ids_row.shape[0]
    shifts = frozen_bias[:2 * D].reshape(2, D)
    b_qkv = frozen_bias[2 * D:5 * D]
    b_proj = frozen_bias[5 * D:6 * D]
    b_fc = frozen_bias[6 * D:6 * D + FF]
    b_out = frozen_bias[6 * D + FF:]
    start = jnp.take(token_table, ids_row, axis=0) + position_table[:row_count]
    normed = low(layer_norm(start, ln_gains[0], shifts[0]))
    qkv_rows = low(jnp.dot(normed, w_qkv, precision=HIGH_PRECISION) + b_qkv)
    head_split = qkv_rows.reshape(row_count, 3, HEADS, HEAD_DIM)
    scores = jnp.einsum('qhd,khd->hqk', head_split[:, 0], head_split[:, 1], precision=HIGH_PRECISION) * HEAD_DIM ** (-0.5)
    positions = jnp.arange(row_count)
    allowed = (positions[None, :] <= positions[:, None]) & (positions[None, :] < ctx_length)
    attn_probs = low(jax.nn.softmax(jnp.where(allowed[None], scores, -1e+30), axis=-1))
    mixed = low(jnp.einsum('hqk,khd->qhd', attn_probs, head_split[:, 2], precision=HIGH_PRECISION).reshape(row_count, D))
    hidden = start + jnp.dot(mixed, w_proj, precision=HIGH_PRECISION) + b_proj
    normed_two = low(layer_norm(hidden, ln_gains[1], shifts[1]))
    inner_acts = low(jax.nn.gelu(jnp.dot(normed_two, w_fc, precision=HIGH_PRECISION) + b_fc, approximate=True))
    return low(hidden + jnp.dot(inner_acts, w_out, precision=HIGH_PRECISION) + b_out)

def sae_losses(params, inputs, id_lists, gates, counted, error):
    enc_weight, enc_bias, dec_weight, decoder_bias = params
    enc = low(enc_weight)
    dec = low(dec_weight)
    bias_copy = low(enc_bias)
    block_rows = 128
    block_count = inputs.shape[0] // block_rows

    def one_block(packed):
        rows_in, ids, gate_rows, live, err_rows = packed
        enc_in = low(rows_in - decoder_bias)
        columns = jnp.take(enc, ids, axis=1)
        pre_acts = jnp.einsum('bd,dbk->bk', enc_in, columns, precision=HIGH_PRECISION) + jnp.take(bias_copy, ids)
        latent_activations = lowered_pullback(low(pre_acts) * gate_rows)
        selected_latents = jnp.take(dec, ids, axis=0)
        reconstructed_input = lowered_pullback(jnp.einsum('ay,ayp->ap', latent_activations[:, :ACTIVE_LATENTS], selected_latents[:, :ACTIVE_LATENTS], precision=HIGH_PRECISION) + decoder_bias)
        auxiliary_reconstruction = lowered_pullback(jnp.einsum('ay,ayp->ap', latent_activations[:, ACTIVE_LATENTS:], selected_latents[:, ACTIVE_LATENTS:], precision=HIGH_PRECISION))
        loss_rows = live * (lax.optimization_barrier(jnp.sum((reconstructed_input - rows_in) ** 2, 1)) + AUX_COEF * lax.optimization_barrier(jnp.sum((auxiliary_reconstruction - err_rows) ** 2, 1))) / D
        return (loss_rows, reconstructed_input)
    shaped = tuple((a.reshape((block_count, block_rows) + a.shape[1:]) for a in (inputs, id_lists, gates, counted, error)))
    loss_rows, reconstructed_input = lax.map(jax.checkpoint(one_block), shaped)
    return (loss_rows.reshape(-1), reconstructed_input.reshape(-1, D))

def orthogonalize(moment):
    gram_full = jnp.dot(moment, moment.T, precision=HIGH_PRECISION)
    norm_scale = 1.0 / (jnp.sqrt(jnp.trace(gram_full)) + NS_EPS)
    current = moment * norm_scale
    gram_full = gram_full * (norm_scale * norm_scale)
    for ns_step in range(NS_STEPS):
        if ns_step > 0:
            gram_full = jnp.dot(current, current.T, precision=HIGH_PRECISION)
        polynomial = QB * gram_full + QC * jnp.dot(gram_full, gram_full, precision=HIGH_PRECISION)
        current = QA * current + jnp.dot(polynomial, current, precision=HIGH_PRECISION)
    return current

def adam_update(param, grad, first, second):
    first = BETA_ONE * first + (1.0 - BETA_ONE) * grad
    second = BETA_TWO * second + (1.0 - BETA_TWO) * grad * grad
    denom = jnp.sqrt(second / (1.0 - BETA_TWO ** STEP)) + ADAM_EPS
    return (param - BIAS_RATE * (first / (1.0 - BETA_ONE ** STEP)) / denom, first, second)

def reference(token_ids, lengths, top_ids, aux_ids, dead_set, token_table, position_table, ln_gains, frozen_bias, w_qkv, w_proj, w_fc, w_out, enc_weight, enc_bias, dec_weight, decoder_bias, enc_moment, dec_moment, encb_first, encb_second, decb_first, decb_second):
    tables = tuple((a.astype(jnp.float32) for a in (token_table, position_table, w_qkv, w_proj, w_fc, w_out)))

    def one_context(carry, packed):
        ids_row, ctx_length = packed
        return (carry, frozen_context(ids_row, ctx_length, tables[0], tables[1], ln_gains, frozen_bias, tables[2], tables[3], tables[4], tables[5]))
    _, inputs = lax.scan(one_context, jnp.float32(0.0), (token_ids.reshape(-1, TOK_DEV), lengths))
    inputs = inputs.reshape(TOKENS, D)
    counted = (jnp.arange(TOK_DEV)[None, :] < lengths[:, None]).astype(jnp.float32).reshape(TOKENS)
    id_lists = jnp.concatenate([top_ids, aux_ids], 1)
    gates = jnp.concatenate([jnp.ones((TOKENS, ACTIVE_LATENTS), jnp.float32), jnp.take(dead_set, aux_ids).astype(jnp.float32)], 1)
    params = (enc_weight, enc_bias, dec_weight, decoder_bias)
    _, reconstructed_input = sae_losses(params, inputs, id_lists, gates, counted, jnp.zeros_like(inputs))
    error = inputs - reconstructed_input

    def total(p):
        return sae_losses(p, inputs, id_lists, gates, counted, error)[0]
    token_loss, pullback = jax.vjp(total, params)
    grads = pullback(jnp.ones_like(token_loss))[0]
    grad_enc, grad_encb, grad_dec, grad_decb = grads
    enc_next = MOMENTUM * enc_moment + grad_enc
    dec_next = MOMENTUM * dec_moment + grad_dec
    step_scale = MUON_RATE * 0.2 * math.sqrt(max(D, L))
    enc_new = enc_weight * (1.0 - MUON_RATE * DECAY) - step_scale * orthogonalize(enc_next)
    dec_new = dec_weight * (1.0 - MUON_RATE * DECAY) - step_scale * orthogonalize(dec_next.T).T
    encb_new, encb_one, encb_two = adam_update(enc_bias, grad_encb, encb_first, encb_second)
    decb_new, decb_one, decb_two = adam_update(decoder_bias, grad_decb, decb_first, decb_second)
    return (token_loss, enc_new, enc_next, enc_new.astype(jnp.bfloat16), dec_new, dec_next, dec_new.astype(jnp.bfloat16), encb_new, encb_one, encb_two, decb_new, decb_one, decb_two)
```

```python
import math

import jax
import jax.numpy as jnp
from jax import lax
from jax.sharding import PartitionSpec as P

D = 768
HEAD_DIM = 64
L = 32768
NS_STEPS = 5
STEP = 10


HIGH_PRECISION = lax.Precision.HIGHEST
AUX_COEF = 1.0 / 32.0
EPS_NORM = 1e-05
NS_EPS = 1e-07
QA = 3.4445
QB = -4.775
QC = 2.0315
MOMENTUM = 0.95
MUON_RATE = 0.1
DECAY = 0.1
BIAS_RATE = 0.3
BETA_ONE = 0.9
BETA_TWO = 0.999
ADAM_EPS = 1e-08


def layer_norm(value, gain, shift):
    row_mean = jnp.mean(value, -1, keepdims=True)
    centred = value - row_mean
    row_var = jnp.mean(centred * centred, -1, keepdims=True)
    return centred * lax.rsqrt(row_var + EPS_NORM) * gain + shift


def frozen_block(start, ctx_length, ln_gains, frozen_bias, w_qkv, w_proj, w_fc, w_out):
    row_count, model_width = start.shape
    head_count = model_width // HEAD_DIM
    ff_width = w_fc.shape[1]
    shifts = frozen_bias[: 2 * model_width].reshape(2, model_width)
    b_qkv = frozen_bias[2 * model_width : 5 * model_width]
    b_proj = frozen_bias[5 * model_width : 6 * model_width]
    b_fc = frozen_bias[6 * model_width : 6 * model_width + ff_width]
    b_out = frozen_bias[6 * model_width + ff_width :]
    normed = layer_norm(start, ln_gains[0], shifts[0]).astype(jnp.bfloat16)
    qkv_rows = (jnp.dot(normed, w_qkv, preferred_element_type=jnp.float32) + b_qkv).astype(
        jnp.bfloat16
    )
    head_split = qkv_rows.reshape(row_count, 3, head_count, HEAD_DIM)
    scores = jnp.einsum(
        "qhd,khd->hqk", head_split[:, 0], head_split[:, 1], preferred_element_type=jnp.float32
    ) * HEAD_DIM ** (-0.5)
    positions = jnp.arange(row_count)
    allowed = (positions[None, :] <= positions[:, None]) & (positions[None, :] < ctx_length)
    attn_probs = jax.nn.softmax(jnp.where(allowed[None], scores, -1e30), axis=-1).astype(
        jnp.bfloat16
    )
    mixed = jnp.einsum(
        "hqk,khd->qhd", attn_probs, head_split[:, 2], preferred_element_type=jnp.float32
    )
    mixed = mixed.reshape(row_count, model_width).astype(jnp.bfloat16)
    hidden = start + jnp.dot(mixed, w_proj, preferred_element_type=jnp.float32) + b_proj
    normed_two = layer_norm(hidden, ln_gains[1], shifts[1]).astype(jnp.bfloat16)
    inner_acts = jax.nn.gelu(
        jnp.dot(normed_two, w_fc, preferred_element_type=jnp.float32) + b_fc, approximate=True
    ).astype(jnp.bfloat16)
    return (hidden + jnp.dot(inner_acts, w_out, preferred_element_type=jnp.float32) + b_out).astype(
        jnp.bfloat16
    )


def kind_codes(id_lists, code_row, first_col, col_count):
    row_total, pick_count = id_lists.shape
    lane_width = min(128, col_count)
    group_count = col_count // lane_width
    block_rows = math.gcd(row_total, max(1, 8192 // group_count))
    offset_ids = id_lists - first_col
    high_ids = jnp.where(offset_ids >= 0, offset_ids // lane_width, -1)
    lane_ids = offset_ids % lane_width
    group_range = jnp.arange(group_count)
    lane_range = jnp.arange(lane_width)

    def one_block(packed):
        high_part, lane_part = packed
        high_hot = jnp.where(
            high_part[:, None, :] == group_range[None, :, None], code_row[None, None, :], 0.0
        ).astype(jnp.bfloat16)
        low_hot = (lane_part[:, :, None] == lane_range[None, None, :]).astype(jnp.bfloat16)
        placed = jnp.einsum("rhk,rkl->rhl", high_hot, low_hot, preferred_element_type=jnp.float32)
        return placed.reshape(high_part.shape[0], col_count)

    blocked = (
        high_ids.reshape(row_total // block_rows, block_rows, pick_count),
        lane_ids.reshape(row_total // block_rows, block_rows, pick_count),
    )
    return lax.map(one_block, blocked).reshape(row_total, col_count)


def gram_series(gram):
    trace_sum = jnp.trace(gram)
    norm_scale = 1.0 / (jnp.sqrt(trace_sum) + NS_EPS)
    gram = gram * (norm_scale * norm_scale)
    eye = jnp.eye(gram.shape[0], dtype=jnp.float32)
    product = None
    for ns_step in range(NS_STEPS):
        square = jnp.dot(gram, gram, precision=HIGH_PRECISION)
        poly = QA * eye + QB * gram + QC * square
        product = poly if product is None else jnp.dot(poly, product, precision=HIGH_PRECISION)
        if ns_step < NS_STEPS - 1:
            half = jnp.dot(gram, poly, precision=HIGH_PRECISION)
            gram = jnp.dot(poly, half, precision=HIGH_PRECISION)
    return product * norm_scale


def adam_update(param, grad, first, second):
    first = BETA_ONE * first + (1.0 - BETA_ONE) * grad
    second = BETA_TWO * second + (1.0 - BETA_TWO) * grad * grad
    denom = jnp.sqrt(second / (1.0 - BETA_TWO**STEP)) + ADAM_EPS
    return (param - BIAS_RATE * (first / (1.0 - BETA_ONE**STEP)) / denom, first, second)


def local(
    token_ids,
    lengths,
    top_ids,
    aux_ids,
    dead_set,
    token_table,
    position_table,
    ln_gains,
    frozen_bias,
    w_qkv,
    w_proj,
    w_fc,
    w_out,
    enc_weight,
    enc_bias,
    dec_weight,
    decoder_bias,
    enc_moment,
    dec_moment,
    encb_first,
    encb_second,
    decb_first,
    decb_second,
):
    wide_count = lax.axis_size("wide")
    narrow_count = lax.axis_size("narrow")
    wide_pos = lax.axis_index("wide")
    narrow_pos = lax.axis_index("narrow")
    both = ("wide", "narrow")
    row_count = token_ids.shape[0]
    model_width = token_table.shape[1]
    wide_latents = enc_weight.shape[1]
    own_latents = wide_latents // narrow_count

    def rows_to_latents(value):
        return lax.all_to_all(value, "narrow", split_axis=1, concat_axis=0, tiled=True)

    def cols_to_latents(value):
        return lax.all_to_all(value, "narrow", split_axis=0, concat_axis=1, tiled=True)

    enc_own = rows_to_latents(enc_weight.astype(jnp.bfloat16))
    dec_own = cols_to_latents(dec_weight.astype(jnp.bfloat16))
    enc_full = lax.all_gather(enc_own, "wide", axis=1, tiled=True)
    dec_full = lax.all_gather(dec_own, "wide", axis=0, tiled=True)
    bias_copy = lax.all_gather(enc_bias.astype(jnp.bfloat16), "wide", axis=0, tiled=True)
    latent_count = wide_count * own_latents

    vocab_dev = token_table.shape[0]
    every_ids = lax.all_gather(token_ids, "wide", axis=0, tiled=True)
    local_ids = every_ids - wide_pos * vocab_dev
    inside = (local_ids >= 0) & (local_ids < vocab_dev)
    looked = jnp.take(token_table, jnp.clip(local_ids, 0, vocab_dev - 1), axis=0)
    looked = jnp.where(inside[:, None], looked, jnp.zeros((), jnp.bfloat16))
    spread = lax.all_to_all(
        looked.reshape(wide_count, row_count, model_width), "wide", 0, 0, tiled=True
    )
    embedded = jnp.sum(spread.astype(jnp.float32), 0)
    start = embedded + position_table[:row_count].astype(jnp.float32)
    ctx_length = lengths[0]
    inputs = frozen_block(start, ctx_length, ln_gains, frozen_bias, w_qkv, w_proj, w_fc, w_out)
    counted = (jnp.arange(row_count) < ctx_length).astype(jnp.float32)

    top_count = top_ids.shape[1]
    id_lists = lax.all_gather(
        jnp.concatenate([top_ids, aux_ids], 1), "narrow", axis=0, tiled=True
    )
    within = id_lists % wide_latents
    column = (id_lists // wide_latents) * own_latents + within % own_latents
    column = jnp.where(within // own_latents == narrow_pos, column, -1)
    pick_total = id_lists.shape[1]
    code_row = jnp.where(jnp.arange(pick_total) < top_count, 1.0, 2.0).astype(jnp.float32)
    codes = kind_codes(column, code_row, 0, latent_count)
    dead_here = lax.dynamic_index_in_dim(
        dead_set.reshape(wide_count, narrow_count, own_latents), narrow_pos, 1, keepdims=False
    ).reshape(latent_count)
    top_mask = codes == 1.0
    aux_mask = (codes == 2.0) & (dead_here[None, :] == 1)

    all_inputs = lax.all_gather(inputs, "narrow", axis=0, tiled=True)
    encoder_in = (all_inputs.astype(jnp.float32) - decoder_bias).astype(jnp.bfloat16)
    pre_acts = (
        jnp.dot(encoder_in, enc_full, preferred_element_type=jnp.float32)
        + bias_copy.astype(jnp.float32)
    ).astype(jnp.bfloat16)
    zero_bf = jnp.zeros((), jnp.bfloat16)
    top_acts = jnp.where(top_mask, pre_acts, zero_bf)
    aux_acts = jnp.where(aux_mask, pre_acts, zero_bf)
    rebuilt_both = lax.psum_scatter(
        jnp.concatenate(
            [
                jnp.dot(top_acts, dec_full, preferred_element_type=jnp.float32),
                jnp.dot(aux_acts, dec_full, preferred_element_type=jnp.float32),
            ],
            1,
        ),
        "narrow",
        scatter_dimension=0,
        tiled=True,
    )
    target = inputs.astype(jnp.float32)
    reconstructed_input = rebuilt_both[:, :model_width] + decoder_bias
    auxiliary_reconstruction = rebuilt_both[:, model_width:]
    recon_error = target - reconstructed_input
    aux_gap = auxiliary_reconstruction - recon_error
    token_loss = (
        counted
        * (jnp.sum(recon_error * recon_error, 1) + AUX_COEF * jnp.sum(aux_gap * aux_gap, 1))
        / model_width
    )
    back_recon = 2.0 / model_width * counted[:, None] * (reconstructed_input - target)
    back_aux = 2.0 * AUX_COEF / model_width * counted[:, None] * aux_gap
    back_rows = jnp.concatenate([back_recon, back_aux], 1).astype(jnp.bfloat16)
    to_latents = (((1,), (1,)), ((), ()))
    over_rows = (((0,), (0,)), ((), ()))
    shard_rows = lax.all_gather(back_rows, "narrow", axis=0, tiled=True)
    recon_part = shard_rows[:, :model_width]
    aux_back = shard_rows[:, model_width:]
    grad_dec = lax.dot_general(top_acts, recon_part, over_rows, preferred_element_type=jnp.float32)
    grad_dec = grad_dec + lax.dot_general(
        aux_acts, aux_back, over_rows, preferred_element_type=jnp.float32
    )
    dec_grad = lax.psum_scatter(
        grad_dec.astype(jnp.bfloat16), "wide", scatter_dimension=0, tiled=True
    )
    back_top = lax.dot_general(recon_part, dec_full, to_latents, preferred_element_type=jnp.float32)
    back_side = lax.dot_general(aux_back, dec_full, to_latents, preferred_element_type=jnp.float32)
    latent_grad = jnp.where(top_mask, back_top, jnp.where(aux_mask, back_side, 0.0)).astype(
        jnp.bfloat16
    )
    grad_enc = lax.dot_general(
        encoder_in, latent_grad, over_rows, preferred_element_type=jnp.float32
    )
    enc_grad = lax.psum_scatter(
        grad_enc.astype(jnp.bfloat16), "wide", scatter_dimension=1, tiled=True
    )
    column_sum = jnp.sum(latent_grad, 0, dtype=jnp.float32)
    encb_grad = lax.psum_scatter(column_sum, "wide", scatter_dimension=0, tiled=True)
    bias_term = jnp.sum(back_rows[:, :model_width], 0, dtype=jnp.float32) - jnp.dot(
        enc_own.astype(jnp.float32), encb_grad, precision=HIGH_PRECISION
    )
    grad_decb = lax.psum(bias_term, both)

    def latents_to_rows(value):
        return lax.all_to_all(
            value.astype(jnp.bfloat16), "narrow", split_axis=0, concat_axis=1, tiled=True
        ).astype(jnp.float32)

    def latents_to_cols(value):
        return lax.all_to_all(
            value.astype(jnp.bfloat16), "narrow", split_axis=1, concat_axis=0, tiled=True
        ).astype(jnp.float32)

    enc_next = MOMENTUM * enc_moment + latents_to_rows(enc_grad)
    dec_next = MOMENTUM * dec_moment + latents_to_cols(dec_grad)
    enc_own_next = MOMENTUM * rows_to_latents(enc_moment.astype(jnp.bfloat16)).astype(
        jnp.float32
    ) + enc_grad.astype(jnp.float32)
    dec_own_next = MOMENTUM * cols_to_latents(dec_moment.astype(jnp.bfloat16)).astype(
        jnp.float32
    ) + dec_grad.astype(jnp.float32)
    split_next = enc_own_next.astype(jnp.bfloat16), dec_own_next.astype(jnp.bfloat16)
    enc_gram = lax.psum(
        lax.dot_general(
            split_next[0], split_next[0], to_latents, preferred_element_type=jnp.float32
        ),
        both,
    )
    dec_gram = lax.psum(
        lax.dot_general(
            split_next[1], split_next[1], over_rows, preferred_element_type=jnp.float32
        ),
        both,
    )
    enc_ortho = latents_to_rows(
        jnp.dot(
            gram_series(enc_gram).astype(jnp.bfloat16),
            split_next[0],
            preferred_element_type=jnp.float32,
        )
    )
    dec_ortho = latents_to_cols(
        jnp.dot(
            split_next[1],
            gram_series(dec_gram).astype(jnp.bfloat16),
            preferred_element_type=jnp.float32,
        )
    )
    step_scale = MUON_RATE * 0.2 * math.sqrt(max(D, L))
    enc_new = enc_weight * (1.0 - MUON_RATE * DECAY) - step_scale * enc_ortho
    dec_new = dec_weight * (1.0 - MUON_RATE * DECAY) - step_scale * dec_ortho
    encb_new, encb_one, encb_two = adam_update(enc_bias, encb_grad, encb_first, encb_second)
    decb_new, decb_one, decb_two = adam_update(decoder_bias, grad_decb, decb_first, decb_second)
    return (
        token_loss,
        enc_new,
        enc_next,
        enc_new.astype(jnp.bfloat16),
        dec_new,
        dec_next,
        dec_new.astype(jnp.bfloat16),
        encb_new,
        encb_one,
        encb_two,
        decb_new,
        decb_one,
        decb_two,
    )


def solution(mesh):
    placed = (
        P(("wide", "narrow")),
        P(("wide", "narrow")),
        P(("wide", "narrow"), None),
        P(("wide", "narrow"), None),
        P(),
        P("wide", None),
        P(),
        P(),
        P(),
        P(),
        P(),
        P(),
        P(),
        P("narrow", "wide"),
        P(("wide", "narrow")),
        P("wide", "narrow"),
        P(),
        P("narrow", "wide"),
        P("wide", "narrow"),
        P(("wide", "narrow")),
        P(("wide", "narrow")),
        P(),
        P(),
    )
    return jax.shard_map(
        local,
        mesh=mesh,
        in_specs=placed,
        out_specs=(
            P(("wide", "narrow")),
            P("narrow", "wide"),
            P("narrow", "wide"),
            P("narrow", "wide"),
            P("wide", "narrow"),
            P("wide", "narrow"),
            P("wide", "narrow"),
            P(("wide", "narrow")),
            P(("wide", "narrow")),
            P(("wide", "narrow")),
            P(),
            P(),
            P(),
        ),
        check_vma=False,
    )
```

```python
import math

import jax
import jax.numpy as jnp
from jax import lax
from jax.experimental import pallas as pl
from jax.experimental.pallas import tpu as pltpu
from jax.sharding import Mesh
from jax.sharding import PartitionSpec as P

D = 768
HEAD_DIM = 64
L = 32768
NS_STEPS = 5
STEP = 10


HIGH_PRECISION = lax.Precision.HIGHEST
AUX_COEF = 1.0 / 32.0
EPS_NORM = 1e-05
NS_EPS = 1e-07
QA = 3.4445
QB = -4.775
QC = 2.0315
MOMENTUM = 0.95
MUON_RATE = 0.1
DECAY = 0.1
BIAS_RATE = 0.3
BETA_ONE = 0.9
BETA_TWO = 0.999
ADAM_EPS = 1e-08


def layer_norm(value, gain, shift):
    row_mean = jnp.mean(value, -1, keepdims=True)
    centred = value - row_mean
    row_var = jnp.mean(centred * centred, -1, keepdims=True)
    return centred * lax.rsqrt(row_var + EPS_NORM) * gain + shift


def frozen_block(start, ctx_length, ln_gains, frozen_bias, w_qkv, w_proj, w_fc, w_out):
    row_count, model_width = start.shape
    head_count = model_width // HEAD_DIM
    ff_width = w_fc.shape[1]
    shifts = frozen_bias[: 2 * model_width].reshape(2, model_width)
    b_qkv = frozen_bias[2 * model_width : 5 * model_width]
    b_proj = frozen_bias[5 * model_width : 6 * model_width]
    b_fc = frozen_bias[6 * model_width : 6 * model_width + ff_width]
    b_out = frozen_bias[6 * model_width + ff_width :]
    normed = layer_norm(start, ln_gains[0], shifts[0]).astype(jnp.bfloat16)
    qkv_rows = (jnp.dot(normed, w_qkv, preferred_element_type=jnp.float32) + b_qkv).astype(
        jnp.bfloat16
    )
    head_split = qkv_rows.reshape(row_count, 3, head_count, HEAD_DIM)
    scores = jnp.einsum(
        "qhd,khd->hqk", head_split[:, 0], head_split[:, 1], preferred_element_type=jnp.float32
    ) * HEAD_DIM ** (-0.5)
    positions = jnp.arange(row_count)
    allowed = (positions[None, :] <= positions[:, None]) & (positions[None, :] < ctx_length)
    attn_probs = jax.nn.softmax(jnp.where(allowed[None], scores, -1e30), axis=-1).astype(
        jnp.bfloat16
    )
    mixed = jnp.einsum(
        "hqk,khd->qhd", attn_probs, head_split[:, 2], preferred_element_type=jnp.float32
    )
    mixed = mixed.reshape(row_count, model_width).astype(jnp.bfloat16)
    hidden = start + jnp.dot(mixed, w_proj, preferred_element_type=jnp.float32) + b_proj
    normed_two = layer_norm(hidden, ln_gains[1], shifts[1]).astype(jnp.bfloat16)
    inner_acts = jax.nn.gelu(
        jnp.dot(normed_two, w_fc, preferred_element_type=jnp.float32) + b_fc, approximate=True
    ).astype(jnp.bfloat16)
    return (hidden + jnp.dot(inner_acts, w_out, preferred_element_type=jnp.float32) + b_out).astype(
        jnp.bfloat16
    )


def split_bf(value):
    high = value.astype(jnp.bfloat16)
    return high, (value - high.astype(jnp.float32)).astype(jnp.bfloat16)


def series_kernel(
    place_ref, near_ref, far_ref, out_ref, gram, g_hi, g_lo, p_hi, p_lo, r_hi, r_lo, q_hi
):
    size = gram.shape[0]
    block = 256
    f32 = jnp.float32
    place = place_ref[0]
    chips, rows_each = near_ref.shape[:2]
    for chip in range(chips):
        for core, source in enumerate((near_ref, far_ref)):
            first = jnp.bitwise_xor(place, 2 * chip + core) * rows_each
            gram[pl.ds(pl.multiple_of(first, 8), rows_each), :] = source[chip].astype(f32)

    def dot(a, b):
        return jnp.dot(a, b, preferred_element_type=f32)

    def eye_rows(start):
        rows = lax.broadcasted_iota(jnp.int32, (block, size), 0) + start
        cols = lax.broadcasted_iota(jnp.int32, (block, size), 1)
        return (rows == cols).astype(f32)

    def row_blocks(body):
        def step(index, carry):
            body(pl.multiple_of(index * block, block))
            return carry

        lax.fori_loop(0, size // block, step, 0)

    def trace_part(index, total):
        start = pl.multiple_of(index * block, block)
        return total + jnp.sum(gram[pl.ds(start, block), :] * eye_rows(start))

    trace_sum = lax.fori_loop(0, size // block, trace_part, jnp.zeros((), f32))
    norm_scale = 1.0 / (jnp.sqrt(jnp.full((1, 1), trace_sum)) + NS_EPS)

    def store(ref_hi, ref_lo, rows, value):
        high, low = split_bf(value)
        ref_hi[rows, :] = high
        ref_lo[rows, :] = low

    def load_gram(start):
        rows = pl.ds(start, block)
        store(g_hi, g_lo, rows, gram[rows, :] * (norm_scale * norm_scale))

    row_blocks(load_gram)

    def three(a_hi, a_lo, b_hi, b_lo, rows):
        high, low = a_hi[rows, :], a_lo[rows, :]
        return dot(high, b_hi[...]) + (dot(high, b_lo[...]) + dot(low, b_hi[...]))

    def poly_rows(start):
        rows = pl.ds(start, block)
        here = g_hi[rows, :].astype(f32) + g_lo[rows, :].astype(f32)
        poly = QA * eye_rows(start) + QB * here + QC * three(g_hi, g_lo, g_hi, g_lo, rows)
        store(p_hi, p_lo, rows, poly)

    def half_rows(start):
        rows = pl.ds(start, block)
        store(r_hi, r_lo, rows, three(g_hi, g_lo, p_hi, p_lo, rows))

    def gram_rows(start):
        rows = pl.ds(start, block)
        store(g_hi, g_lo, rows, three(p_hi, p_lo, r_hi, r_lo, rows))

    def product_rows(start):
        rows = pl.ds(start, block)
        r_hi[rows, :] = dot(p_hi[rows, :], q_hi[...]).astype(jnp.bfloat16)

    def full_step(index, carry):
        row_blocks(poly_rows)
        row_blocks(half_rows)
        row_blocks(gram_rows)

        @pl.when(index == 0)
        def _():
            q_hi[...] = p_hi[...]

        @pl.when(index > 0)
        def _():
            row_blocks(product_rows)
            q_hi[...] = r_hi[...]

        return carry

    lax.fori_loop(0, NS_STEPS - 1, full_step, 0)
    row_blocks(poly_rows)

    def last_rows(start):
        rows = pl.ds(start, block)
        out_ref[rows, :] = (dot(p_hi[rows, :], q_hi[...]) * norm_scale).astype(out_ref.dtype)

    row_blocks(last_rows)


def gram_series(place, near, far):
    size = near.shape[2]
    whole = pl.BlockSpec(memory_space=pltpu.VMEM)
    return pl.pallas_call(
        series_kernel,
        out_shape=jax.ShapeDtypeStruct((size, size), jnp.bfloat16),
        in_specs=[pl.BlockSpec(memory_space=pltpu.SMEM), whole, whole],
        out_specs=whole,
        scratch_shapes=[pltpu.VMEM((size, size), jnp.float32)]
        + [pltpu.VMEM((size, size), jnp.bfloat16)] * 7,
        compiler_params=pltpu.CompilerParams(vmem_limit_bytes=40 * 2**20),
        cost_estimate=pl.CostEstimate(
            flops=43 * 2 * size**3, bytes_accessed=6 * size * size, transcendentals=0
        ),
    )(place, near, far)


def code_kernel(high_ref, low_ref, kind_ref, out_ref, stage):
    batch, groups = stage.shape[:2]
    picks = high_ref.shape[1]
    bf16, f32 = jnp.bfloat16, jnp.float32
    one, zero = jnp.ones((16, picks), bf16), jnp.zeros((16, picks), bf16)
    kinds = jnp.broadcast_to(kind_ref[...], (16, picks)).astype(bf16)
    steps = lax.broadcasted_iota(jnp.int32, (16, picks), 0).astype(f32).astype(bf16)

    def hot(row, count, value):
        row = jnp.broadcast_to(row, (16, picks)).astype(bf16)
        parts = [
            jnp.where(steps + jnp.asarray(16 * part, bf16) == row, value, zero)
            for part in range(max(1, count // 16))
        ]
        return jnp.concatenate(parts, 0).astype(jnp.float8_e4m3fn)

    def one_batch(index, carry):
        first = pl.multiple_of(index * batch, batch)
        for token in range(batch):
            row = pl.ds(first + token, 1)
            codes = lax.dot_general(
                hot(high_ref[row, :], groups, kinds),
                hot(low_ref[row, :], 128, one),
                (((1,), (1,)), ((), ())),
                preferred_element_type=f32,
            )
            stage[token] = codes[:groups]
        for group in range(groups):
            lanes = slice(group * 128, (group + 1) * 128)
            out_ref[pl.ds(first, batch), lanes] = stage[:, group, :].astype(bf16)
        return carry

    lax.fori_loop(0, high_ref.shape[0] // batch, one_batch, 0)


def kind_codes(column, code_row, latent_count):
    row_total, pick_total = column.shape
    groups = latent_count // 128
    rows = min(128, row_total)
    high = (column // 128).astype(jnp.float32)
    low = (column % 128).astype(jnp.float32)
    return pl.pallas_call(
        code_kernel,
        grid=(row_total // rows,),
        out_shape=jax.ShapeDtypeStruct((row_total, latent_count), jnp.bfloat16),
        in_specs=[
            pl.BlockSpec((rows, pick_total), lambda i: (i, 0)),
            pl.BlockSpec((rows, pick_total), lambda i: (i, 0)),
            pl.BlockSpec((1, pick_total), lambda i: (0, 0)),
        ],
        out_specs=pl.BlockSpec((rows, latent_count), lambda i: (i, 0)),
        scratch_shapes=[pltpu.VMEM((32, groups, 128), jnp.float32)],
        compiler_params=pltpu.CompilerParams(vmem_limit_bytes=40 * 2**20),
        cost_estimate=pl.CostEstimate(
            flops=40 * row_total * latent_count * 128,
            bytes_accessed=2 * row_total * latent_count,
            transcendentals=0,
        ),
    )(high, low, code_row[None, :])


def adam_update(param, grad, first, second):
    first = BETA_ONE * first + (1.0 - BETA_ONE) * grad
    second = BETA_TWO * second + (1.0 - BETA_TWO) * grad * grad
    denom = jnp.sqrt(second / (1.0 - BETA_TWO**STEP)) + ADAM_EPS
    return (param - BIAS_RATE * (first / (1.0 - BETA_ONE**STEP)) / denom, first, second)


def local(
    token_ids,
    lengths,
    top_ids,
    aux_ids,
    dead_set,
    token_table,
    position_table,
    ln_gains,
    frozen_bias,
    w_qkv,
    w_proj,
    w_fc,
    w_out,
    enc_weight,
    enc_bias,
    dec_weight,
    decoder_bias,
    enc_moment,
    dec_moment,
    encb_first,
    encb_second,
    decb_first,
    decb_second,
):
    chips = lax.axis_size("chip")
    narrow_count = lax.axis_size("narrow")
    wide_count = 2 * chips
    wide = ("chip", "core")
    chip_pos = lax.axis_index("chip")
    core_pos = lax.axis_index("core")
    wide_pos = 2 * chip_pos + core_pos
    narrow_pos = lax.axis_index("narrow")
    row_count = token_ids.shape[0]
    model_width = token_table.shape[1]
    wide_latents = enc_weight.shape[1]
    own_latents = wide_latents // narrow_count
    latent_count = chips * own_latents
    bf16, f32 = jnp.bfloat16, jnp.float32
    to_latents = (((1,), (1,)), ((), ()))
    over_rows = (((0,), (0,)), ((), ()))

    def swap(value, axis, offset):
        count = lax.axis_size(axis)
        return lax.ppermute(value, axis, [(place, place ^ offset) for place in range(count)])

    def spread(value):
        narrow_rows = jnp.concatenate(
            [value] + [swap(value, "narrow", k) for k in range(1, narrow_count)], 0
        )
        return jnp.concatenate([narrow_rows, swap(narrow_rows, "core", 1)], 0)

    def rows_to_latents(value):
        return lax.all_to_all(value, "narrow", split_axis=1, concat_axis=0, tiled=True)

    def cols_to_latents(value):
        return lax.all_to_all(value, "narrow", split_axis=0, concat_axis=1, tiled=True)

    def latents_to_rows(value):
        return lax.all_to_all(value, "narrow", split_axis=0, concat_axis=1, tiled=True)

    def latents_to_cols(value):
        return lax.all_to_all(value, "narrow", split_axis=1, concat_axis=0, tiled=True)

    vocab_dev = token_table.shape[0]
    every_ids = lax.all_gather(token_ids, wide, axis=0, tiled=True)
    pick_ids = spread(jnp.concatenate([top_ids, aux_ids], 1))
    enc_own = rows_to_latents(enc_weight.astype(bf16))
    dec_own = cols_to_latents(dec_weight.astype(bf16))
    bias_rows = jnp.concatenate(
        [enc_bias.astype(bf16)[None], jnp.zeros((15, own_latents), bf16)], 0
    )
    enc_biased = lax.all_gather(
        jnp.concatenate([enc_own, bias_rows], 0), "chip", axis=1, tiled=True
    )
    dec_full = lax.all_gather(dec_own, "chip", axis=0, tiled=True)
    enc_full = enc_biased[:model_width]
    bias_copy = enc_biased[model_width]

    local_ids = every_ids - wide_pos * vocab_dev
    inside = (local_ids >= 0) & (local_ids < vocab_dev)
    looked = jnp.take(token_table, jnp.clip(local_ids, 0, vocab_dev - 1), axis=0)
    looked = jnp.where(inside[:, None], looked, jnp.zeros((), bf16))
    pieces = lax.all_to_all(
        looked.reshape(wide_count, row_count, model_width), wide, 0, 0, tiled=True
    )
    start = jnp.sum(pieces.astype(f32), 0) + position_table[:row_count].astype(f32)
    ctx_length = lengths[0]
    inputs = frozen_block(start, ctx_length, ln_gains, frozen_bias, w_qkv, w_proj, w_fc, w_out)
    counted = (jnp.arange(row_count) < ctx_length).astype(f32)

    top_count = top_ids.shape[1]
    pick_total = pick_ids.shape[1]
    owner = pick_ids // wide_latents
    within = pick_ids % wide_latents
    column = (owner // 2) * own_latents + within % own_latents
    mine = (within // own_latents == narrow_pos) & (owner % 2 == core_pos)
    column = jnp.where(mine, column, -1)
    code_row = jnp.where(jnp.arange(pick_total) < top_count, 1.0, 2.0).astype(f32)
    codes = kind_codes(column, code_row, latent_count)
    dead_here = dead_set.reshape(chips, 2, narrow_count, own_latents)
    dead_here = lax.dynamic_slice(
        dead_here, (0, core_pos, narrow_pos, 0), (chips, 1, 1, own_latents)
    ).reshape(latent_count)
    top_mask = codes == 1.0
    aux_mask = (codes == 2.0) & (dead_here[None, :] == 1)

    all_inputs = spread(inputs)
    encoder_in = (all_inputs.astype(f32) - decoder_bias).astype(bf16)
    pre_acts = (
        jnp.dot(encoder_in, enc_full, preferred_element_type=f32) + bias_copy.astype(f32)
    ).astype(bf16)
    zero_bf = jnp.zeros((), bf16)
    top_acts = jnp.where(top_mask, pre_acts, zero_bf)
    aux_acts = jnp.where(aux_mask, pre_acts, zero_bf)
    core_rows = narrow_count * row_count

    def rebuild(acts):
        far = jnp.dot(acts[core_rows:], dec_full, preferred_element_type=f32).astype(bf16)
        near = jnp.dot(acts[:core_rows], dec_full, preferred_element_type=f32)
        total = near + swap(far, "core", 1).astype(f32)
        rounded = total.astype(bf16)
        result = total[:row_count]
        for k in range(1, narrow_count):
            part = rounded[k * row_count : (k + 1) * row_count]
            result = result + swap(part, "narrow", k).astype(f32)
        return result

    target = inputs.astype(f32)
    reconstructed_input = rebuild(top_acts) + decoder_bias
    auxiliary_reconstruction = rebuild(aux_acts)
    recon_error = target - reconstructed_input
    aux_gap = auxiliary_reconstruction - recon_error
    token_loss = (
        counted
        * (jnp.sum(recon_error * recon_error, 1) + AUX_COEF * jnp.sum(aux_gap * aux_gap, 1))
        / model_width
    )
    back_recon = 2.0 / model_width * counted[:, None] * (reconstructed_input - target)
    back_aux = 2.0 * AUX_COEF / model_width * counted[:, None] * aux_gap
    back_rows = jnp.concatenate([back_recon, back_aux], 1).astype(bf16)
    shard_rows = spread(back_rows)
    recon_part = shard_rows[:, :model_width]
    aux_back = shard_rows[:, model_width:]

    def scatter_chips(value, axis):
        def block(place):
            return lax.dynamic_slice_in_dim(value, place * own_latents, own_latents, axis)

        total = block(chip_pos).astype(f32)
        for k in range(1, chips):
            total = total + swap(block(chip_pos ^ k).astype(bf16), "chip", k).astype(f32)
        return total

    grad_dec = lax.dot_general(top_acts, recon_part, over_rows, preferred_element_type=f32)
    grad_dec = grad_dec + lax.dot_general(
        aux_acts, aux_back, over_rows, preferred_element_type=f32
    )
    dec_grad = scatter_chips(grad_dec, 0)
    back_top = lax.dot_general(recon_part, dec_full, to_latents, preferred_element_type=f32)
    back_side = lax.dot_general(aux_back, dec_full, to_latents, preferred_element_type=f32)
    latent_grad = jnp.where(top_mask, back_top, jnp.where(aux_mask, back_side, 0.0)).astype(bf16)
    grad_enc = lax.dot_general(encoder_in, latent_grad, over_rows, preferred_element_type=f32)
    own_moments = (
        rows_to_latents(enc_moment.astype(bf16)),
        cols_to_latents(dec_moment.astype(bf16)),
    )
    grad_enc, own_moments = lax.optimization_barrier((grad_enc, own_moments))
    enc_grad = scatter_chips(grad_enc, 1)
    column_sum = jnp.sum(latent_grad, 0, dtype=f32)
    encb_grad = jnp.sum(
        lax.all_to_all(column_sum.reshape(chips, own_latents), "chip", 0, 0, tiled=True), 0
    )
    bias_term = jnp.sum(back_rows[:, :model_width], 0, dtype=f32) - jnp.dot(
        enc_own.astype(f32), encb_grad, precision=HIGH_PRECISION
    )

    def sum_gram(part, extra):
        rows = model_width // wide_count
        spare = jnp.zeros((16, model_width), bf16)
        if extra is not None:
            spare = jnp.concatenate([*(half[None] for half in split_bf(extra)), spare[2:]], 0)
        chunks = jnp.concatenate(
            [
                part.reshape(wide_count, rows, model_width).astype(bf16),
                jnp.broadcast_to(spare[None], (wide_count, 16, model_width)),
            ],
            1,
        )
        chunks = lax.all_to_all(chunks, wide, 0, 0, tiled=True)
        total = jnp.sum(chunks.astype(f32), 0)
        vector = total[rows] + total[rows + 1]
        high, low = split_bf(vector)
        sent = jnp.concatenate(
            [total[:rows].astype(bf16), high[None], low[None], spare[2:]], 0
        )
        total = total[:rows]
        for k in range(1, narrow_count):
            got = swap(sent, "narrow", k).astype(f32)
            total = total + got[:rows]
            vector = vector + (got[rows] + got[rows + 1])
        near = jnp.stack([total] + [swap(total, "chip", k) for k in range(1, chips)])
        return near, swap(near, "core", 1), vector

    place = wide_pos.reshape(1)
    dec_own_next = (MOMENTUM * own_moments[1].astype(f32) + dec_grad).astype(bf16)
    dec_near, dec_far, _ = sum_gram(
        lax.dot_general(dec_own_next, dec_own_next, over_rows, preferred_element_type=f32), None
    )
    dec_rows_grad = latents_to_cols(dec_grad.astype(bf16))
    dec_factor = gram_series(place, dec_near, dec_far)
    dec_ortho = latents_to_cols(
        jnp.dot(dec_own_next, dec_factor, preferred_element_type=f32).astype(bf16)
    )
    enc_own_next = (MOMENTUM * own_moments[0].astype(f32) + enc_grad).astype(bf16)
    enc_near, enc_far, grad_decb = sum_gram(
        lax.dot_general(enc_own_next, enc_own_next, to_latents, preferred_element_type=f32),
        bias_term,
    )
    enc_rows_grad = latents_to_rows(enc_grad.astype(bf16))
    enc_factor = gram_series(place, enc_near, enc_far)
    enc_factor, enc_rows_grad, dec_rows_grad = lax.optimization_barrier(
        (enc_factor, enc_rows_grad, dec_rows_grad)
    )
    enc_ortho = latents_to_rows(
        jnp.dot(enc_factor, enc_own_next, preferred_element_type=f32).astype(bf16)
    )
    enc_next = MOMENTUM * enc_moment + enc_rows_grad.astype(f32)
    dec_next = MOMENTUM * dec_moment + dec_rows_grad.astype(f32)
    step_scale = MUON_RATE * 0.2 * math.sqrt(max(D, L))
    enc_new = enc_weight * (1.0 - MUON_RATE * DECAY) - step_scale * enc_ortho.astype(f32)
    dec_new = dec_weight * (1.0 - MUON_RATE * DECAY) - step_scale * dec_ortho.astype(f32)
    encb_new, encb_one, encb_two = adam_update(enc_bias, encb_grad, encb_first, encb_second)
    decb_new, decb_one, decb_two = adam_update(decoder_bias, grad_decb, decb_first, decb_second)
    return (
        token_loss,
        enc_new,
        enc_next,
        enc_new.astype(bf16),
        dec_new,
        dec_next,
        dec_new.astype(bf16),
        encb_new,
        encb_one,
        encb_two,
        decb_new,
        decb_one,
        decb_two,
    )


def solution(mesh):
    wide, narrow = mesh.devices.shape
    fine = Mesh(mesh.devices.reshape(wide // 2, 2, narrow), ("chip", "core", "narrow"))
    placed = (
        P(("chip", "core", "narrow")),
        P(("chip", "core", "narrow")),
        P(("chip", "core", "narrow"), None),
        P(("chip", "core", "narrow"), None),
        P(),
        P(("chip", "core"), None),
        P(),
        P(),
        P(),
        P(),
        P(),
        P(),
        P(),
        P("narrow", ("chip", "core")),
        P(("chip", "core", "narrow")),
        P(("chip", "core"), "narrow"),
        P(),
        P("narrow", ("chip", "core")),
        P(("chip", "core"), "narrow"),
        P(("chip", "core", "narrow")),
        P(("chip", "core", "narrow")),
        P(),
        P(),
    )
    return jax.shard_map(
        local,
        mesh=fine,
        in_specs=placed,
        out_specs=(
            P(("chip", "core", "narrow")),
            P("narrow", ("chip", "core")),
            P("narrow", ("chip", "core")),
            P("narrow", ("chip", "core")),
            P(("chip", "core"), "narrow"),
            P(("chip", "core"), "narrow"),
            P(("chip", "core"), "narrow"),
            P(("chip", "core", "narrow")),
            P(("chip", "core", "narrow")),
            P(("chip", "core", "narrow")),
            P(),
            P(),
            P(),
        ),
        check_vma=False,
    )
```

```python
import functools
import math

import jax
import jax.numpy as jnp
from jax import lax
from jax.experimental import pallas as pl
from jax.experimental.pallas import tpu as pltpu
from jax.sharding import Mesh
from jax.sharding import PartitionSpec as P

D = 768
HEAD_DIM = 64
L = 32768
NS_STEPS = 5
STEP = 10


HIGH_PRECISION = lax.Precision.HIGHEST
AUX_COEF = 1.0 / 32.0
EPS_NORM = 1e-05
NS_EPS = 1e-07
QA = 3.4445
QB = -4.775
QC = 2.0315
MOMENTUM = 0.95
MUON_RATE = 0.1
DECAY = 0.1
BIAS_RATE = 0.3
BETA_ONE = 0.9
BETA_TWO = 0.999
ADAM_EPS = 1e-08


def layer_norm(value, gain, shift):
    row_mean = jnp.mean(value, -1, keepdims=True)
    centred = value - row_mean
    row_var = jnp.mean(centred * centred, -1, keepdims=True)
    return centred * lax.rsqrt(row_var + EPS_NORM) * gain + shift


def frozen_block(start, ctx_length, ln_gains, frozen_bias, w_qkv, w_proj, w_fc, w_out):
    row_count, model_width = start.shape
    head_count = model_width // HEAD_DIM
    ff_width = w_fc.shape[1]
    shifts = frozen_bias[: 2 * model_width].reshape(2, model_width)
    b_qkv = frozen_bias[2 * model_width : 5 * model_width]
    b_proj = frozen_bias[5 * model_width : 6 * model_width]
    b_fc = frozen_bias[6 * model_width : 6 * model_width + ff_width]
    b_out = frozen_bias[6 * model_width + ff_width :]
    normed = layer_norm(start, ln_gains[0], shifts[0]).astype(jnp.bfloat16)
    qkv_rows = (jnp.dot(normed, w_qkv, preferred_element_type=jnp.float32) + b_qkv).astype(
        jnp.bfloat16
    )
    head_split = qkv_rows.reshape(row_count, 3, head_count, HEAD_DIM)
    scores = jnp.einsum(
        "qhd,khd->hqk", head_split[:, 0], head_split[:, 1], preferred_element_type=jnp.float32
    ) * HEAD_DIM ** (-0.5)
    positions = jnp.arange(row_count)
    allowed = (positions[None, :] <= positions[:, None]) & (positions[None, :] < ctx_length)
    attn_probs = jax.nn.softmax(jnp.where(allowed[None], scores, -1e30), axis=-1).astype(
        jnp.bfloat16
    )
    mixed = jnp.einsum(
        "hqk,khd->qhd", attn_probs, head_split[:, 2], preferred_element_type=jnp.float32
    )
    mixed = mixed.reshape(row_count, model_width).astype(jnp.bfloat16)
    hidden = start + jnp.dot(mixed, w_proj, preferred_element_type=jnp.float32) + b_proj
    normed_two = layer_norm(hidden, ln_gains[1], shifts[1]).astype(jnp.bfloat16)
    inner_acts = jax.nn.gelu(
        jnp.dot(normed_two, w_fc, preferred_element_type=jnp.float32) + b_fc, approximate=True
    ).astype(jnp.bfloat16)
    return (hidden + jnp.dot(inner_acts, w_out, preferred_element_type=jnp.float32) + b_out).astype(
        jnp.bfloat16
    )


def split_bf(value):
    high = value.astype(jnp.bfloat16)
    return high, (value - high.astype(jnp.float32)).astype(jnp.bfloat16)


def row_blocks(size, body):
    block = 256

    def step(index, carry):
        body(pl.ds(pl.multiple_of(index * block, block), block), index * block)
        return carry

    lax.fori_loop(0, size // block, step, 0)


def eye_rows(start, size):
    rows = lax.broadcasted_iota(jnp.int32, (256, size), 0) + start
    cols = lax.broadcasted_iota(jnp.int32, (256, size), 1)
    return (rows == cols).astype(jnp.float32)


def dot_f32(a, b):
    return jnp.dot(a, b, preferred_element_type=jnp.float32)


def store_split(pair, rows, value):
    pair[0][rows, :], pair[1][rows, :] = split_bf(value)


def three(left, right, rows):
    high, low = left[0][rows, :], left[1][rows, :]
    return dot_f32(high, right[0][...]) + (
        dot_f32(high, right[1][...]) + dot_f32(low, right[0][...])
    )


def series_step(gram, poly, half, out, old, new, step):
    size = gram[0].shape[0]
    last = step == NS_STEPS - 1
    exact_square = step >= 3

    def poly_rows(rows, start):
        here = gram[0][rows, :].astype(jnp.float32) + gram[1][rows, :].astype(jnp.float32)
        if exact_square:
            square = three(gram, gram, rows)
        else:
            square = dot_f32(gram[0][rows, :], gram[0][...])
        store_split(poly, rows, QA * eye_rows(start, size) + QB * here + QC * square)

    def half_rows(rows, start):
        store_split(half, rows, three(gram, poly, rows))

    def gram_rows(rows, start):
        store_split(out, rows, three(poly, half, rows))

    def product_rows(rows, start):
        new[rows, :] = dot_f32(poly[0][rows, :], old[...]).astype(jnp.bfloat16)

    row_blocks(size, poly_rows)
    if not last:
        row_blocks(size, half_rows)
        row_blocks(size, gram_rows)
    if step > 0:
        row_blocks(size, product_rows)


def first_kernel(place_ref, near_ref, far_ref, o_hi, o_lo, q_ref, total, *scratch):
    size = total.shape[0]
    chips, rows_each = near_ref.shape[:2]
    chip, core = place_ref[0], place_ref[1]
    gram, poly, half = scratch[:2], scratch[2:4], scratch[4:6]
    for offset in range(chips):
        for side, source in enumerate((near_ref, far_ref)):
            first = jnp.bitwise_xor(core, side) * (size // 2)
            first = first + jnp.bitwise_xor(chip, offset) * rows_each
            total[pl.ds(pl.multiple_of(first, 8), rows_each), :] = source[offset].astype(
                jnp.float32
            )

    def trace_part(index, value):
        start = pl.multiple_of(index * 256, 256)
        return value + jnp.sum(total[pl.ds(start, 256), :] * eye_rows(start, size))

    trace_sum = lax.fori_loop(0, size // 256, trace_part, jnp.zeros((), jnp.float32))
    scale = 1.0 / (jnp.sqrt(jnp.full((1, 1), trace_sum)) + NS_EPS)

    def load_rows(rows, start):
        store_split(gram, rows, total[rows, :] * (scale * scale))

    row_blocks(size, load_rows)
    series_step(gram, poly, half, (o_hi, o_lo), None, None, 0)

    def product_rows(rows, start):
        value = poly[0][rows, :].astype(jnp.float32) + poly[1][rows, :].astype(jnp.float32)
        q_ref[rows, :] = (value * scale).astype(jnp.bfloat16)

    row_blocks(size, product_rows)


def middle_kernel(step, g_hi, g_lo, q_ref, o_hi, o_lo, out_ref, *scratch):
    series_step(
        (g_hi, g_lo), scratch[:2], scratch[2:4], (o_hi, o_lo), q_ref, out_ref, step
    )


def last_kernel(g_hi, g_lo, q_ref, out_ref, *scratch):
    series_step((g_hi, g_lo), scratch[:2], None, None, q_ref, out_ref, NS_STEPS - 1)


def square_call(kernel, outs, scratch, passes, *operands):
    size = operands[-1].shape[-1]
    whole = pl.BlockSpec(memory_space=pltpu.VMEM)
    specs = [whole] * len(operands)
    if operands[0].ndim == 1:
        specs[0] = pl.BlockSpec(memory_space=pltpu.SMEM)
    square = jax.ShapeDtypeStruct((size, size), jnp.bfloat16)
    return pl.pallas_call(
        kernel,
        out_shape=[square] * outs,
        in_specs=specs,
        out_specs=[whole] * outs,
        scratch_shapes=[pltpu.VMEM((size, size), kind) for kind in scratch],
        compiler_params=pltpu.CompilerParams(vmem_limit_bytes=40 * 2**20),
        cost_estimate=pl.CostEstimate(
            flops=passes * 2 * size**3, bytes_accessed=12 * size * size, transcendentals=0
        ),
    )(*operands)


def series_start(place, near, far):
    bf16 = jnp.bfloat16
    return square_call(first_kernel, 3, [jnp.float32] + [bf16] * 6, 8, place, near, far)


def series_finish(state):
    bf16 = jnp.bfloat16
    for step in range(1, NS_STEPS - 1):
        kernel = functools.partial(middle_kernel, step)
        state = square_call(kernel, 3, [bf16] * 4, 8 if step < 3 else 10, *state)
    return square_call(last_kernel, 1, [bf16] * 2, 4, *state)[0]


def code_kernel(shifts, place_ref, ids_ref, dead_ref, out_ref, high, low, stage):
    wide_shift, own_shift, top_count = shifts
    batch, groups = stage.shape[:2]
    rows, picks = ids_ref.shape
    bf16, f32 = jnp.bfloat16, jnp.float32
    chip, core, narrow = place_ref[0], place_ref[1], place_ref[2]
    latent_count = dead_ref.shape[1]
    half_shift = own_shift - 1

    ids = ids_ref[...]
    owner = lax.shift_right_logical(ids, wide_shift)
    within = jnp.bitwise_and(ids, (1 << wide_shift) - 1)
    mine = (lax.shift_right_logical(within, own_shift) == narrow) & (
        jnp.bitwise_and(owner, 1) == core
    )
    inner = jnp.bitwise_and(within, (1 << own_shift) - 1)
    offset = jnp.bitwise_xor(lax.shift_right_logical(owner, 1), chip)
    column = (
        lax.shift_right_logical(inner, half_shift) * (latent_count // 2)
        + lax.shift_left(offset, half_shift)
        + jnp.bitwise_and(inner, (1 << half_shift) - 1)
    )
    high[...] = jnp.where(mine, lax.shift_right_logical(column, 7), -1).astype(f32)
    low[...] = jnp.bitwise_and(column, 127).astype(f32)

    one, zero = jnp.ones((16, picks), bf16), jnp.zeros((16, picks), bf16)
    places = lax.broadcasted_iota(jnp.int32, (16, picks), 1)
    kinds = jnp.where(places < top_count, 1.0, 2.0).astype(bf16)
    steps = lax.broadcasted_iota(jnp.int32, (16, picks), 0).astype(f32).astype(bf16)

    def hot(row, count, value):
        row = jnp.broadcast_to(row, (16, picks)).astype(bf16)
        parts = [
            jnp.where(steps + jnp.asarray(16 * part, bf16) == row, value, zero)
            for part in range(max(1, count // 16))
        ]
        return jnp.concatenate(parts, 0).astype(jnp.float8_e4m3fn)

    def one_batch(index, carry):
        first = pl.multiple_of(index * batch, batch)
        for token in range(batch):
            row = pl.ds(first + token, 1)
            codes = lax.dot_general(
                hot(high[row, :], groups, kinds),
                hot(low[row, :], 128, one),
                (((1,), (1,)), ((), ())),
                preferred_element_type=f32,
            )
            stage[token] = codes[:groups]
        for group in range(groups):
            lanes = slice(group * 128, (group + 1) * 128)
            codes = stage[:, group, :]
            live = (codes != 2.0) | (dead_ref[:, lanes] == 1)
            out_ref[pl.ds(first, batch), lanes] = jnp.where(live, codes, 0.0).astype(bf16)
        return carry

    lax.fori_loop(0, rows // batch, one_batch, 0)


def kind_codes(place, ids, dead_here, wide_latents, own_latents, top_count):
    row_total, pick_total = ids.shape
    latent_count = dead_here.shape[1]
    rows = min(128, row_total)
    shifts = (wide_latents.bit_length() - 1, own_latents.bit_length() - 1, top_count)
    return pl.pallas_call(
        functools.partial(code_kernel, shifts),
        grid=(row_total // rows,),
        out_shape=jax.ShapeDtypeStruct((row_total, latent_count), jnp.bfloat16),
        in_specs=[
            pl.BlockSpec(memory_space=pltpu.SMEM),
            pl.BlockSpec((rows, pick_total), lambda i: (i, 0)),
            pl.BlockSpec((1, latent_count), lambda i: (0, 0)),
        ],
        out_specs=pl.BlockSpec((rows, latent_count), lambda i: (i, 0)),
        scratch_shapes=[
            pltpu.VMEM((rows, pick_total), jnp.float32),
            pltpu.VMEM((rows, pick_total), jnp.float32),
            pltpu.VMEM((32, latent_count // 128, 128), jnp.float32),
        ],
        compiler_params=pltpu.CompilerParams(vmem_limit_bytes=40 * 2**20),
        cost_estimate=pl.CostEstimate(
            flops=40 * row_total * latent_count * 128,
            bytes_accessed=2 * row_total * latent_count,
            transcendentals=0,
        ),
    )(place, ids, dead_here)


def adam_update(param, grad, first, second):
    first = BETA_ONE * first + (1.0 - BETA_ONE) * grad
    second = BETA_TWO * second + (1.0 - BETA_TWO) * grad * grad
    denom = jnp.sqrt(second / (1.0 - BETA_TWO**STEP)) + ADAM_EPS
    return (param - BIAS_RATE * (first / (1.0 - BETA_ONE**STEP)) / denom, first, second)


def local(
    token_ids,
    lengths,
    top_ids,
    aux_ids,
    dead_set,
    token_table,
    position_table,
    ln_gains,
    frozen_bias,
    w_qkv,
    w_proj,
    w_fc,
    w_out,
    enc_weight,
    enc_bias,
    dec_weight,
    decoder_bias,
    enc_moment,
    dec_moment,
    encb_first,
    encb_second,
    decb_first,
    decb_second,
):
    chips = lax.axis_size("chip")
    narrow_count = lax.axis_size("narrow")
    wide_count = 2 * chips
    wide = ("chip", "core")
    chip_pos = lax.axis_index("chip")
    core_pos = lax.axis_index("core")
    wide_pos = 2 * chip_pos + core_pos
    narrow_pos = lax.axis_index("narrow")
    row_count = token_ids.shape[0]
    model_width = token_table.shape[1]
    wide_latents = enc_weight.shape[1]
    own_latents = wide_latents // narrow_count
    half_latents = own_latents // 2
    latent_count = chips * own_latents
    core_rows = narrow_count * row_count
    bf16, f32 = jnp.bfloat16, jnp.float32
    to_latents = (((1,), (1,)), ((), ()))
    over_rows = (((0,), (0,)), ((), ()))
    place = jnp.stack([chip_pos, core_pos, narrow_pos]).astype(jnp.int32)
    bits = [1 << bit for bit in range(chips.bit_length() - 1)]
    orders = (bits, bits[::-1])

    def after(value, *others):
        return lax.optimization_barrier((value, others))[0]

    def swap(value, axis, offset):
        count = lax.axis_size(axis)
        return lax.ppermute(value, axis, [(spot, spot ^ offset) for spot in range(count)])

    def spread_narrow(value):
        parts = [value] + [swap(value, "narrow", k) for k in range(1, narrow_count)]
        return jnp.concatenate(parts, 0)

    def rows_to_latents(value):
        return lax.all_to_all(value, "narrow", split_axis=1, concat_axis=0, tiled=True)

    def cols_to_latents(value):
        return lax.all_to_all(value, "narrow", split_axis=0, concat_axis=1, tiled=True)

    def latents_to_rows(value):
        return lax.all_to_all(value, "narrow", split_axis=0, concat_axis=1, tiled=True)

    def latents_to_cols(value):
        return lax.all_to_all(value, "narrow", split_axis=1, concat_axis=0, tiled=True)

    def gather_chips(own, axis):
        pieces = []
        for part, order in enumerate(orders):
            first = lax.slice_in_dim(own, part * half_latents, (part + 1) * half_latents, axis=axis)
            held = {0: first}
            for bit in order:
                offsets = sorted(held)
                sent = [held[offset] for offset in offsets]
                sent = sent[0] if len(sent) == 1 else jnp.concatenate(sent, axis)
                got = jnp.split(swap(sent, "chip", bit), len(offsets), axis)
                held.update({offset ^ bit: piece for offset, piece in zip(offsets, got)})
            pieces += [held[offset] for offset in range(chips)]
        return jnp.concatenate(pieces, axis)

    def scatter_chips(value, axis, extra=None):
        results, extras = [], []
        for part, order in enumerate(orders):
            base = part * chips * half_latents
            held, added = {}, {}
            for offset in range(chips):
                start = base + offset * half_latents
                held[offset] = lax.slice_in_dim(value, start, start + half_latents, axis=axis)
                if extra is not None:
                    added[offset] = lax.slice_in_dim(extra, start, start + half_latents, axis=0)
            for bit in reversed(order):
                keep = sorted(offset for offset in held if not offset & bit)
                sent = jnp.concatenate([held[offset | bit].astype(bf16) for offset in keep], axis)
                if extra is not None:
                    vector = jnp.concatenate([added[offset | bit] for offset in keep])
                    lines = jnp.stack(split_bf(vector))
                    lines = jnp.concatenate([lines, jnp.zeros((14, lines.shape[1]), bf16)], 0)
                    sent = jnp.concatenate([sent, lines], 0)
                got = swap(sent, "chip", bit).astype(f32)
                if extra is not None:
                    vector = got[model_width] + got[model_width + 1]
                    got = got[:model_width]
                    added = {
                        offset: added[offset] + piece
                        for offset, piece in zip(keep, jnp.split(vector, len(keep)))
                    }
                got = jnp.split(got, len(keep), axis)
                held = {offset: held[offset] + piece for offset, piece in zip(keep, got)}
            results.append(held[0])
            if extra is not None:
                extras.append(added[0])
        result = jnp.concatenate(results, axis)
        return result if extra is None else (result, jnp.concatenate(extras))

    vocab_dev = token_table.shape[0]
    every_ids = lax.all_gather(token_ids, wide, axis=0, tiled=False).reshape(wide_count, row_count)
    every_ids = jnp.concatenate(
        [
            lax.dynamic_slice_in_dim(every_ids, wide_pos ^ offset, 1, 0)
            for offset in range(wide_count)
        ],
        1,
    )[0]
    local_ids = every_ids - wide_pos * vocab_dev
    inside = (local_ids >= 0) & (local_ids < vocab_dev)
    looked = jnp.take(token_table, jnp.clip(local_ids, 0, vocab_dev - 1), axis=0)
    looked = jnp.where(inside[:, None], looked, jnp.zeros((), bf16))
    enc_own = rows_to_latents(enc_weight.astype(bf16))
    near_picks = spread_narrow(jnp.concatenate([top_ids, aux_ids], 1))
    far_picks = swap(near_picks, "core", 1)

    looked = looked.reshape(chips, 2, row_count, model_width)
    looked = looked[:, 0] + swap(looked[:, 1], "core", 1)
    embedded = looked[0].astype(f32)
    for k in range(1, chips):
        embedded = embedded + swap(looked[k], "chip", k).astype(f32)

    enc_own = after(enc_own, looked)
    dec_own = cols_to_latents(after(dec_weight, enc_own).astype(bf16))
    bias_rows = jnp.concatenate(
        [enc_bias.astype(bf16)[None], jnp.zeros((15, own_latents), bf16)], 0
    )
    enc_biased = gather_chips(jnp.concatenate([enc_own, bias_rows], 0), 1)
    enc_full = enc_biased[:model_width]
    bias_copy = enc_biased[model_width]

    dead_here = jnp.stack(
        [
            lax.dynamic_slice_in_dim(
                dead_set,
                (2 * (chip_pos ^ offset) + core_pos) * wide_latents + narrow_pos * own_latents,
                own_latents,
            )
            for offset in range(chips)
        ]
    )
    dead_here = dead_here.reshape(chips, 2, half_latents).transpose(1, 0, 2)
    dead_here = dead_here.reshape(1, latent_count)
    sizes = (wide_latents, own_latents, top_ids.shape[1])
    near_codes = kind_codes(place, near_picks, dead_here, *sizes)

    start = after(embedded, near_codes) + position_table[:row_count].astype(f32)
    ctx_length = lengths[0]
    inputs = frozen_block(start, ctx_length, ln_gains, frozen_bias, w_qkv, w_proj, w_fc, w_out)
    counted = (jnp.arange(row_count) < ctx_length).astype(f32)
    dec_full = gather_chips(after(dec_own, inputs), 0)
    far_codes = kind_codes(place, after(far_picks, inputs), dead_here, *sizes)

    near_inputs = spread_narrow(inputs)
    far_inputs = swap(near_inputs, "core", 1)
    zero_bf = jnp.zeros((), bf16)

    def encode(tokens, codes):
        encoder_in = (tokens.astype(f32) - decoder_bias).astype(bf16)
        pre_acts = (
            jnp.dot(encoder_in, enc_full, preferred_element_type=f32) + bias_copy.astype(f32)
        ).astype(bf16)
        top_acts = jnp.where(codes == 1.0, pre_acts, zero_bf)
        return encoder_in, top_acts, jnp.where(codes == 2.0, pre_acts, zero_bf)

    all_inputs = jnp.concatenate([near_inputs, far_inputs], 0)
    codes = jnp.concatenate([near_codes, far_codes], 0)
    encoder_in, top_acts, aux_acts = encode(all_inputs, codes)

    def rebuild(acts):
        far = jnp.dot(acts[core_rows:], dec_full, preferred_element_type=f32).astype(bf16)
        near = jnp.dot(acts[:core_rows], dec_full, preferred_element_type=f32)
        total = near + swap(far, "core", 1).astype(f32)
        rounded = total.astype(bf16)
        result = total[:row_count]
        for k in range(1, narrow_count):
            part = rounded[k * row_count : (k + 1) * row_count]
            result = result + swap(part, "narrow", k).astype(f32)
        return result

    target = inputs.astype(f32)
    reconstructed_input = rebuild(top_acts) + decoder_bias
    auxiliary_reconstruction = rebuild(aux_acts)
    recon_error = target - reconstructed_input
    aux_gap = auxiliary_reconstruction - recon_error
    token_loss = (
        counted
        * (jnp.sum(recon_error * recon_error, 1) + AUX_COEF * jnp.sum(aux_gap * aux_gap, 1))
        / model_width
    )
    back_recon = 2.0 / model_width * counted[:, None] * (reconstructed_input - target)
    back_aux = 2.0 * AUX_COEF / model_width * counted[:, None] * aux_gap
    back_rows = jnp.concatenate([back_recon, back_aux], 1).astype(bf16)
    near_back = spread_narrow(back_rows)
    shard_rows = jnp.concatenate([near_back, swap(near_back, "core", 1)], 0)
    recon_part = shard_rows[:, :model_width]
    aux_back = shard_rows[:, model_width:]

    grad_dec = lax.dot_general(top_acts, recon_part, over_rows, preferred_element_type=f32)
    grad_dec = grad_dec + lax.dot_general(
        aux_acts, aux_back, over_rows, preferred_element_type=f32
    )
    grad_dec, recon_part, aux_back = lax.optimization_barrier((grad_dec, recon_part, aux_back))
    dec_grad = scatter_chips(grad_dec, 0)
    back_top = lax.dot_general(recon_part, dec_full, to_latents, preferred_element_type=f32)
    back_side = lax.dot_general(aux_back, dec_full, to_latents, preferred_element_type=f32)
    latent_grad = jnp.where(codes == 1.0, back_top, jnp.where(codes == 2.0, back_side, 0.0))
    latent_grad = latent_grad.astype(bf16)
    grad_enc = lax.dot_general(encoder_in, latent_grad, over_rows, preferred_element_type=f32)
    column_sum = jnp.sum(latent_grad, 0, dtype=f32)
    enc_grad, encb_grad = scatter_chips(grad_enc, 1, column_sum)
    bias_term = jnp.sum(back_rows[:, :model_width], 0, dtype=f32) - jnp.dot(
        enc_own.astype(f32), encb_grad, precision=HIGH_PRECISION
    )
    dec_moment_own = cols_to_latents(after(dec_moment, back_rows).astype(bf16))
    enc_moment_own = rows_to_latents(after(enc_moment, dec_moment_own).astype(bf16))

    def sum_gram(part, extra):
        half = model_width // 2
        rows = half // chips
        spare = jnp.zeros((14, model_width), bf16)

        def pack(block, vector):
            lines = [line[None] for line in split_bf(vector)]
            return jnp.concatenate([block.astype(bf16), *lines, spare], 0)

        def unpack(got):
            got = got.astype(f32)
            return got[:-16], got[-16] + got[-15]

        def block_of(value, index, count):
            return lax.dynamic_slice_in_dim(value, index * count, count, 0)

        vector = extra
        got, more = unpack(swap(pack(block_of(part, 1 - core_pos, half), vector), "core", 1))
        part, vector = block_of(part, core_pos, half) + got, vector + more
        total, sent_vector = block_of(part, chip_pos, rows), vector
        for k in range(1, chips):
            sent = pack(block_of(part, chip_pos ^ k, rows), sent_vector)
            got, more = unpack(swap(sent, "chip", k))
            total, vector = total + got, vector + more
        sent = pack(total, vector)
        for k in range(1, narrow_count):
            got, more = unpack(swap(sent, "narrow", k))
            total, vector = total + got, vector + more
        near = jnp.stack([total] + [swap(total, "chip", k) for k in range(1, chips)])
        return near, swap(near, "core", 1), vector

    dec_own_next = (MOMENTUM * dec_moment_own.astype(f32) + dec_grad).astype(bf16)
    dec_near, dec_far, _ = sum_gram(
        lax.dot_general(dec_own_next, dec_own_next, over_rows, preferred_element_type=f32),
        jnp.zeros((model_width,), f32),
    )
    dec_state = series_start(place, dec_near, dec_far)
    dec_rows_grad = latents_to_cols(after(dec_grad, enc_moment_own).astype(bf16))
    enc_own_next = (MOMENTUM * enc_moment_own.astype(f32) + enc_grad).astype(bf16)
    enc_near, enc_far, grad_decb = sum_gram(
        lax.dot_general(enc_own_next, enc_own_next, to_latents, preferred_element_type=f32),
        bias_term,
    )
    dec_factor = series_finish(dec_state)
    dec_ortho = latents_to_cols(
        jnp.dot(dec_own_next, dec_factor, preferred_element_type=f32).astype(bf16)
    )
    enc_rows_grad = latents_to_rows(after(enc_grad, dec_rows_grad).astype(bf16))
    enc_state = series_start(place, after(enc_near, dec_factor, dec_rows_grad), enc_far)
    enc_factor = series_finish(enc_state)
    enc_factor = after(enc_factor, enc_rows_grad)
    enc_ortho = latents_to_rows(
        jnp.dot(enc_factor, enc_own_next, preferred_element_type=f32).astype(bf16)
    )
    enc_next = MOMENTUM * enc_moment + enc_rows_grad.astype(f32)
    dec_next = MOMENTUM * dec_moment + dec_rows_grad.astype(f32)
    step_scale = MUON_RATE * 0.2 * math.sqrt(max(D, L))
    enc_new = enc_weight * (1.0 - MUON_RATE * DECAY) - step_scale * enc_ortho.astype(f32)
    dec_new = dec_weight * (1.0 - MUON_RATE * DECAY) - step_scale * dec_ortho.astype(f32)
    encb_new, encb_one, encb_two = adam_update(enc_bias, encb_grad, encb_first, encb_second)
    decb_new, decb_one, decb_two = adam_update(decoder_bias, grad_decb, decb_first, decb_second)
    return (
        token_loss,
        enc_new,
        enc_next,
        enc_new.astype(bf16),
        dec_new,
        dec_next,
        dec_new.astype(bf16),
        encb_new,
        encb_one,
        encb_two,
        decb_new,
        decb_one,
        decb_two,
    )


def solution(mesh):
    wide, narrow = mesh.devices.shape
    fine = Mesh(mesh.devices.reshape(wide // 2, 2, narrow), ("chip", "core", "narrow"))
    placed = (
        P(("chip", "core", "narrow")),
        P(("chip", "core", "narrow")),
        P(("chip", "core", "narrow"), None),
        P(("chip", "core", "narrow"), None),
        P(),
        P(("chip", "core"), None),
        P(),
        P(),
        P(),
        P(),
        P(),
        P(),
        P(),
        P("narrow", ("chip", "core")),
        P(("chip", "core", "narrow")),
        P(("chip", "core"), "narrow"),
        P(),
        P("narrow", ("chip", "core")),
        P(("chip", "core"), "narrow"),
        P(("chip", "core", "narrow")),
        P(("chip", "core", "narrow")),
        P(),
        P(),
    )
    return jax.shard_map(
        local,
        mesh=fine,
        in_specs=placed,
        out_specs=(
            P(("chip", "core", "narrow")),
            P("narrow", ("chip", "core")),
            P("narrow", ("chip", "core")),
            P("narrow", ("chip", "core")),
            P(("chip", "core"), "narrow"),
            P(("chip", "core"), "narrow"),
            P(("chip", "core"), "narrow"),
            P(("chip", "core", "narrow")),
            P(("chip", "core", "narrow")),
            P(("chip", "core", "narrow")),
            P(),
            P(),
            P(),
        ),
        check_vma=False,
    )
```

```python
import functools
import math

import jax
import jax.numpy as jnp
from jax import lax
from jax.experimental import pallas as pl
from jax.experimental.pallas import tpu as pltpu
from jax.sharding import Mesh
from jax.sharding import PartitionSpec as P

D = 768
HEAD_DIM = 64
L = 32768
NS_STEPS = 5
STEP = 10


HIGH_PRECISION = lax.Precision.HIGHEST
AUX_COEF = 1.0 / 32.0
EPS_NORM = 1e-05
NS_EPS = 1e-07
QA = 3.4445
QB = -4.775
QC = 2.0315
MOMENTUM = 0.95
MUON_RATE = 0.1
DECAY = 0.1
BIAS_RATE = 0.3
BETA_ONE = 0.9
BETA_TWO = 0.999
ADAM_EPS = 1e-08


def layer_norm(value, gain, shift):
    row_mean = jnp.mean(value, -1, keepdims=True)
    centred = value - row_mean
    row_var = jnp.mean(centred * centred, -1, keepdims=True)
    return centred * lax.rsqrt(row_var + EPS_NORM) * gain + shift


def frozen_block(start, ctx_length, ln_gains, frozen_bias, w_qkv, w_proj, w_fc, w_out):
    row_count, model_width = start.shape
    head_count = model_width // HEAD_DIM
    ff_width = w_fc.shape[1]
    shifts = frozen_bias[: 2 * model_width].reshape(2, model_width)
    b_qkv = frozen_bias[2 * model_width : 5 * model_width]
    b_proj = frozen_bias[5 * model_width : 6 * model_width]
    b_fc = frozen_bias[6 * model_width : 6 * model_width + ff_width]
    b_out = frozen_bias[6 * model_width + ff_width :]
    normed = layer_norm(start, ln_gains[0], shifts[0]).astype(jnp.bfloat16)
    qkv_rows = (jnp.dot(normed, w_qkv, preferred_element_type=jnp.float32) + b_qkv).astype(
        jnp.bfloat16
    )
    head_split = qkv_rows.reshape(row_count, 3, head_count, HEAD_DIM)
    scores = jnp.einsum(
        "qhd,khd->hqk", head_split[:, 0], head_split[:, 1], preferred_element_type=jnp.float32
    ) * HEAD_DIM ** (-0.5)
    positions = jnp.arange(row_count)
    allowed = (positions[None, :] <= positions[:, None]) & (positions[None, :] < ctx_length)
    attn_probs = jax.nn.softmax(jnp.where(allowed[None], scores, -1e30), axis=-1).astype(
        jnp.bfloat16
    )
    mixed = jnp.einsum(
        "hqk,khd->qhd", attn_probs, head_split[:, 2], preferred_element_type=jnp.float32
    )
    mixed = mixed.reshape(row_count, model_width).astype(jnp.bfloat16)
    hidden = start + jnp.dot(mixed, w_proj, preferred_element_type=jnp.float32) + b_proj
    normed_two = layer_norm(hidden, ln_gains[1], shifts[1]).astype(jnp.bfloat16)
    inner_acts = jax.nn.gelu(
        jnp.dot(normed_two, w_fc, preferred_element_type=jnp.float32) + b_fc, approximate=True
    ).astype(jnp.bfloat16)
    return (hidden + jnp.dot(inner_acts, w_out, preferred_element_type=jnp.float32) + b_out).astype(
        jnp.bfloat16
    )


def split_bf(value):
    high = value.astype(jnp.bfloat16)
    return high, (value - high.astype(jnp.float32)).astype(jnp.bfloat16)


def row_blocks(size, body):
    block = 256

    def step(index, carry):
        body(pl.ds(pl.multiple_of(index * block, block), block), index * block)
        return carry

    lax.fori_loop(0, size // block, step, 0)


def eye_rows(start, size):
    rows = lax.broadcasted_iota(jnp.int32, (256, size), 0) + start
    cols = lax.broadcasted_iota(jnp.int32, (256, size), 1)
    return (rows == cols).astype(jnp.float32)


def dot_f32(a, b):
    return jnp.dot(a, b, preferred_element_type=jnp.float32)


def store_split(pair, rows, value):
    pair[0][rows, :], pair[1][rows, :] = split_bf(value)


def three(left, right, rows):
    high, low = left[0][rows, :], left[1][rows, :]
    return dot_f32(high, right[0][...]) + (
        dot_f32(high, right[1][...]) + dot_f32(low, right[0][...])
    )


def series_step(gram, poly, half, out, old, new, step):
    size = gram[0].shape[0]
    last = step == NS_STEPS - 1
    exact_square = step >= 3

    def poly_rows(rows, start):
        here = gram[0][rows, :].astype(jnp.float32) + gram[1][rows, :].astype(jnp.float32)
        if exact_square:
            square = three(gram, gram, rows)
        else:
            square = dot_f32(gram[0][rows, :], gram[0][...])
        store_split(poly, rows, QA * eye_rows(start, size) + QB * here + QC * square)

    def half_rows(rows, start):
        store_split(half, rows, three(gram, poly, rows))

    def gram_rows(rows, start):
        store_split(out, rows, three(poly, half, rows))

    def product_rows(rows, start):
        new[rows, :] = dot_f32(poly[0][rows, :], old[...]).astype(jnp.bfloat16)

    row_blocks(size, poly_rows)
    if not last:
        row_blocks(size, half_rows)
        row_blocks(size, gram_rows)
    if step > 0:
        row_blocks(size, product_rows)


def first_kernel(place_ref, near_ref, far_ref, o_hi, o_lo, q_ref, total, *scratch):
    size = total.shape[0]
    chips, rows_each = near_ref.shape[:2]
    chip, core = place_ref[0], place_ref[1]
    gram, poly, half = scratch[:2], scratch[2:4], scratch[4:6]
    for offset in range(chips):
        for side, source in enumerate((near_ref, far_ref)):
            first = jnp.bitwise_xor(core, side) * (size // 2)
            first = first + jnp.bitwise_xor(chip, offset) * rows_each
            total[pl.ds(pl.multiple_of(first, 8), rows_each), :] = source[offset].astype(
                jnp.float32
            )

    def trace_part(index, value):
        start = pl.multiple_of(index * 256, 256)
        return value + jnp.sum(total[pl.ds(start, 256), :] * eye_rows(start, size))

    trace_sum = lax.fori_loop(0, size // 256, trace_part, jnp.zeros((), jnp.float32))
    scale = 1.0 / (jnp.sqrt(jnp.full((1, 1), trace_sum)) + NS_EPS)

    def load_rows(rows, start):
        store_split(gram, rows, total[rows, :] * (scale * scale))

    row_blocks(size, load_rows)
    series_step(gram, poly, half, (o_hi, o_lo), None, None, 0)

    def product_rows(rows, start):
        value = poly[0][rows, :].astype(jnp.float32) + poly[1][rows, :].astype(jnp.float32)
        q_ref[rows, :] = (value * scale).astype(jnp.bfloat16)

    row_blocks(size, product_rows)


def middle_kernel(step, g_hi, g_lo, q_ref, o_hi, o_lo, out_ref, *scratch):
    series_step(
        (g_hi, g_lo), scratch[:2], scratch[2:4], (o_hi, o_lo), q_ref, out_ref, step
    )


def last_kernel(g_hi, g_lo, q_ref, out_ref, *scratch):
    series_step((g_hi, g_lo), scratch[:2], None, None, q_ref, out_ref, NS_STEPS - 1)


def square_call(kernel, outs, scratch, passes, *operands):
    size = operands[-1].shape[-1]
    whole = pl.BlockSpec(memory_space=pltpu.VMEM)
    specs = [whole] * len(operands)
    if operands[0].ndim == 1:
        specs[0] = pl.BlockSpec(memory_space=pltpu.SMEM)
    square = jax.ShapeDtypeStruct((size, size), jnp.bfloat16)
    return pl.pallas_call(
        kernel,
        out_shape=[square] * outs,
        in_specs=specs,
        out_specs=[whole] * outs,
        scratch_shapes=[pltpu.VMEM((size, size), kind) for kind in scratch],
        compiler_params=pltpu.CompilerParams(vmem_limit_bytes=40 * 2**20),
        cost_estimate=pl.CostEstimate(
            flops=passes * 2 * size**3, bytes_accessed=12 * size * size, transcendentals=0
        ),
    )(*operands)


def series_start(place, near, far):
    bf16 = jnp.bfloat16
    return square_call(first_kernel, 3, [jnp.float32] + [bf16] * 6, 8, place, near, far)


def series_next(step, state):
    bf16 = jnp.bfloat16
    if step == NS_STEPS - 1:
        return square_call(last_kernel, 1, [bf16] * 2, 4, *state)
    kernel = functools.partial(middle_kernel, step)
    return square_call(kernel, 3, [bf16] * 4, 8 if step < 3 else 10, *state)


def code_kernel(shifts, place_ref, ids_ref, dead_ref, out_ref, high, low, stage):
    wide_shift, own_shift, top_count, orders = shifts
    batch, groups = stage.shape[:2]
    rows, picks = ids_ref.shape
    bf16, f32 = jnp.bfloat16, jnp.float32
    chip, core, narrow = place_ref[0], place_ref[1], place_ref[2]
    latent_count = dead_ref.shape[1]
    half_shift = own_shift - 1

    ids = ids_ref[...]
    owner = lax.shift_right_logical(ids, wide_shift)
    within = jnp.bitwise_and(ids, (1 << wide_shift) - 1)
    mine = (lax.shift_right_logical(within, own_shift) == narrow) & (
        jnp.bitwise_and(owner, 1) == core
    )
    inner = jnp.bitwise_and(within, (1 << own_shift) - 1)
    offset = jnp.bitwise_xor(lax.shift_right_logical(owner, 1), chip)
    half = lax.shift_right_logical(inner, half_shift)
    spots = []
    for order in orders:
        spot = jnp.zeros_like(offset)
        for index, bit in enumerate(order[:-1]):
            spot = spot + jnp.where(jnp.bitwise_and(offset, bit) != 0, 1 << index, 0)
        sent = jnp.where(jnp.bitwise_and(offset, order[-1]) != 0, latent_count // 4, 0)
        spots.append(sent + lax.shift_left(spot, half_shift))
    column = (
        half * (latent_count // 2)
        + jnp.where(half == 0, spots[0], spots[1])
        + jnp.bitwise_and(inner, (1 << half_shift) - 1)
    )
    high[...] = jnp.where(mine, lax.shift_right_logical(column, 7), -1).astype(f32)
    low[...] = jnp.bitwise_and(column, 127).astype(f32)

    one, zero = jnp.ones((16, picks), bf16), jnp.zeros((16, picks), bf16)
    places = lax.broadcasted_iota(jnp.int32, (16, picks), 1)
    kinds = jnp.where(places < top_count, 1.0, 2.0).astype(bf16)
    steps = lax.broadcasted_iota(jnp.int32, (16, picks), 0).astype(f32).astype(bf16)

    def hot(row, count, value):
        row = jnp.broadcast_to(row, (16, picks)).astype(bf16)
        parts = [
            jnp.where(steps + jnp.asarray(16 * part, bf16) == row, value, zero)
            for part in range(max(1, count // 16))
        ]
        return jnp.concatenate(parts, 0).astype(jnp.float8_e4m3fn)

    def one_batch(index, carry):
        first = pl.multiple_of(index * batch, batch)
        for token in range(batch):
            row = pl.ds(first + token, 1)
            codes = lax.dot_general(
                hot(high[row, :], groups, kinds),
                hot(low[row, :], 128, one),
                (((1,), (1,)), ((), ())),
                preferred_element_type=f32,
            )
            stage[token] = codes[:groups]
        for group in range(groups):
            lanes = slice(group * 128, (group + 1) * 128)
            codes = stage[:, group, :]
            live = (codes != 2.0) | (dead_ref[:, lanes] == 1)
            out_ref[pl.ds(first, batch), lanes] = jnp.where(live, codes, 0.0).astype(bf16)
        return carry

    lax.fori_loop(0, rows // batch, one_batch, 0)


def kind_codes(place, ids, dead_here, wide_latents, own_latents, top_count, orders):
    row_total, pick_total = ids.shape
    latent_count = dead_here.shape[1]
    rows = min(128, row_total)
    shifts = (wide_latents.bit_length() - 1, own_latents.bit_length() - 1, top_count, orders)
    return pl.pallas_call(
        functools.partial(code_kernel, shifts),
        grid=(row_total // rows,),
        out_shape=jax.ShapeDtypeStruct((row_total, latent_count), jnp.bfloat16),
        in_specs=[
            pl.BlockSpec(memory_space=pltpu.SMEM),
            pl.BlockSpec((rows, pick_total), lambda i: (i, 0)),
            pl.BlockSpec((1, latent_count), lambda i: (0, 0)),
        ],
        out_specs=pl.BlockSpec((rows, latent_count), lambda i: (i, 0)),
        scratch_shapes=[
            pltpu.VMEM((rows, pick_total), jnp.float32),
            pltpu.VMEM((rows, pick_total), jnp.float32),
            pltpu.VMEM((32, latent_count // 128, 128), jnp.float32),
        ],
        compiler_params=pltpu.CompilerParams(vmem_limit_bytes=40 * 2**20),
        cost_estimate=pl.CostEstimate(
            flops=40 * row_total * latent_count * 128,
            bytes_accessed=2 * row_total * latent_count,
            transcendentals=0,
        ),
    )(place, ids, dead_here)


def pick_copy(step, count, sources, target):
    for index, source in enumerate(sources):

        @pl.when(step // count == index)
        def _(source=source):
            target[...] = source[...]


def forward_kernel(count, x_ref, codes_ref, *refs):
    encs, decs = refs[:4], refs[4:8]
    top_ref, aux_ref, far_ref, near_ref = refs[8:12]
    enc, dec, acc_top, acc_aux = refs[12:]
    step = pl.program_id(0)
    rows_all, width = x_ref.shape
    block = min(1024, rows_all)
    pick_copy(step, count, encs, enc)
    pick_copy(step, count, decs, dec)

    @pl.when(step == 0)
    def _():
        acc_top[...] = jnp.zeros_like(acc_top)
        acc_aux[...] = jnp.zeros_like(acc_aux)

    bias = enc[pl.ds(width, 16), :].astype(jnp.float32)[:1]

    def one(index, carry):
        rows = pl.ds(pl.multiple_of(index * block, block), block)
        pre = (dot_f32(x_ref[rows, :], enc[pl.ds(0, width), :]) + bias).astype(jnp.bfloat16)
        codes = codes_ref[rows, :]
        zero = jnp.zeros_like(pre)
        top = jnp.where(codes == 1.0, pre, zero)
        aux = jnp.where(codes == 2.0, pre, zero)
        top_ref[rows, :] = top
        aux_ref[rows, :] = aux
        acc_top[rows, :] += dot_f32(top, dec[...])
        acc_aux[rows, :] += dot_f32(aux, dec[...])
        return carry

    lax.fori_loop(0, rows_all // block, one, 0)

    @pl.when(step == pl.num_programs(0) - 1)
    def _():
        half = rows_all // 2
        for first, acc in ((0, acc_top), (width, acc_aux)):
            near_ref[:, first : first + width] = acc[pl.ds(0, half), :]
            far_ref[:, first : first + width] = acc[pl.ds(half, half), :].astype(jnp.bfloat16)


def part_specs(shape, axis, block, count, starts):
    specs = []
    for index, first in enumerate(starts):

        def place(step, index=index, first=first):
            spot = jnp.clip(step - index * count, 0, count - 1)
            return (spot + first, 0) if axis == 0 else (0, spot + first)

        size = (block, shape[1]) if axis == 0 else (shape[0], block)
        specs.append(pl.BlockSpec(size, place))
    return specs


def forward(x, codes, encs, decs):
    rows, width = x.shape
    quarter = encs[0].shape[1]
    block = min(512, quarter)
    count = quarter // block
    lanes = pl.BlockSpec((rows, block), lambda step: (0, step))
    fixed = lambda shape: pl.BlockSpec(shape, lambda step: (0, 0))
    bf16, f32 = jnp.bfloat16, jnp.float32
    half_shape = (rows // 2, 2 * width)
    return pl.pallas_call(
        functools.partial(forward_kernel, count),
        grid=(4 * count,),
        out_shape=[
            jax.ShapeDtypeStruct(codes.shape, bf16),
            jax.ShapeDtypeStruct(codes.shape, bf16),
            jax.ShapeDtypeStruct(half_shape, bf16),
            jax.ShapeDtypeStruct(half_shape, f32),
        ],
        in_specs=[fixed(x.shape), lanes]
        + part_specs(encs[0].shape, 1, block, count, (0, 0, 0, 0))
        + part_specs(decs[0].shape, 0, block, count, (0, 0, 0, 0)),
        out_specs=[lanes, lanes, fixed(half_shape), fixed(half_shape)],
        scratch_shapes=[
            pltpu.VMEM((encs[0].shape[0], block), bf16),
            pltpu.VMEM((block, width), bf16),
            pltpu.VMEM((rows, width), f32),
            pltpu.VMEM((rows, width), f32),
        ],
        compiler_params=pltpu.CompilerParams(vmem_limit_bytes=58 * 2**20),
        cost_estimate=pl.CostEstimate(
            flops=6 * rows * width * codes.shape[1],
            bytes_accessed=6 * rows * codes.shape[1],
            transcendentals=0,
        ),
    )(x, codes, *encs, *decs)


def store_part(count, refs, rows, value):
    step = pl.program_id(0)
    for index, ref in enumerate(refs):

        @pl.when(step // count == index)
        def _(ref=ref):
            ref[rows, :] = value.astype(ref.dtype)


def dec_grad_kernel(count, recon_ref, aux_back_ref, top_ref, aux_ref, *outs):
    def one(index, carry):
        rows = pl.ds(pl.multiple_of(index * 384, 384), 384)
        value = dot_f32(recon_ref[rows, :], top_ref[...]) + dot_f32(
            aux_back_ref[rows, :], aux_ref[...]
        )
        store_part(count, outs, rows, value)
        return carry

    lax.fori_loop(0, recon_ref.shape[0] // 384, one, 0)


def dec_grads(back_t, top_acts, aux_acts, quarters, kind):
    width = back_t.shape[0] // 2
    rows, latents = top_acts.shape
    quarter = latents // 4
    block = min(512, quarter)
    count = quarter // block

    def lanes(step):
        return (0, jnp.where(step < count, quarters[0], quarters[1] - 1) * count + step)

    acts = pl.BlockSpec((rows, block), lanes)
    shape = (width, quarter)
    return pl.pallas_call(
        functools.partial(dec_grad_kernel, count),
        grid=(2 * count,),
        out_shape=[jax.ShapeDtypeStruct(shape, kind)] * 2,
        in_specs=[
            pl.BlockSpec((width, rows), lambda step: (0, 0)),
            pl.BlockSpec((width, rows), lambda step: (1, 0)),
            acts,
            acts,
        ],
        out_specs=part_specs(shape, 1, block, count, (0, 0)),
        compiler_params=pltpu.CompilerParams(vmem_limit_bytes=58 * 2**20),
        cost_estimate=pl.CostEstimate(
            flops=8 * rows * width * quarter, bytes_accessed=8 * rows * quarter, transcendentals=0
        ),
    )(back_t, back_t, top_acts, aux_acts)


def enc_grad_kernel(count, x_ref, back_ref, codes_ref, dec_a, dec_b, out_a, out_b, dec, grads):
    step = pl.program_id(0)
    pick_copy(step, count, (dec_a, dec_b), dec)
    width = x_ref.shape[0]
    block = min(1024, back_ref.shape[0])
    to_latents = (((1,), (1,)), ((), ()))

    def one(index, total):
        rows = pl.ds(pl.multiple_of(index * block, block), block)
        codes = codes_ref[rows, :].astype(jnp.float32)
        top = lax.dot_general(
            back_ref[rows, :width], dec[...], to_latents, preferred_element_type=jnp.float32
        )
        aux = lax.dot_general(
            back_ref[rows, width:], dec[...], to_latents, preferred_element_type=jnp.float32
        )
        value = jnp.where(codes == 1.0, top, jnp.where(codes == 2.0, aux, 0.0))
        value = value.astype(jnp.bfloat16)
        grads[rows, :] = value
        return total + jnp.sum(value.astype(jnp.float32), 0, keepdims=True)

    total = lax.fori_loop(
        0, back_ref.shape[0] // block, one, jnp.zeros((1, dec.shape[0]), jnp.float32)
    )

    def two(index, carry):
        rows = pl.ds(pl.multiple_of(index * 384, 384), 384)
        store_part(count, (out_a, out_b), rows, dot_f32(x_ref[rows, :], grads[...]))
        return carry

    lax.fori_loop(0, width // 384, two, 0)
    lines = lax.broadcasted_iota(jnp.int32, (16, dec.shape[0]), 0)
    if out_a.dtype == jnp.bfloat16:
        high = total.astype(jnp.bfloat16).astype(jnp.float32)
        lines = jnp.where(lines == 0, high, jnp.where(lines == 1, total - high, 0.0))
    else:
        lines = jnp.where(lines == 0, total, 0.0)
    store_part(count, (out_a, out_b), pl.ds(width, 16), lines)


def enc_grads(x_t, back, codes, decs, quarters, kind):
    width, rows = x_t.shape
    quarter = codes.shape[1] // 4
    block = min(512, quarter)
    count = quarter // block

    def lanes(step):
        return (0, jnp.where(step < count, quarters[0], quarters[1] - 1) * count + step)

    shape = (width + 16, quarter)
    return pl.pallas_call(
        functools.partial(enc_grad_kernel, count),
        grid=(2 * count,),
        out_shape=[jax.ShapeDtypeStruct(shape, kind)] * 2,
        in_specs=[
            pl.BlockSpec(x_t.shape, lambda step: (0, 0)),
            pl.BlockSpec(back.shape, lambda step: (0, 0)),
            pl.BlockSpec((rows, block), lanes),
        ]
        + part_specs(decs[0].shape, 0, block, count, (0, 0)),
        out_specs=part_specs(shape, 1, block, count, (0, 0)),
        scratch_shapes=[
            pltpu.VMEM((block, width), jnp.bfloat16),
            pltpu.VMEM((rows, block), jnp.bfloat16),
        ],
        compiler_params=pltpu.CompilerParams(vmem_limit_bytes=58 * 2**20),
        cost_estimate=pl.CostEstimate(
            flops=12 * rows * width * quarter, bytes_accessed=8 * rows * quarter, transcendentals=0
        ),
    )(x_t, back, codes, *decs)


def adam_update(param, grad, first, second):
    first = BETA_ONE * first + (1.0 - BETA_ONE) * grad
    second = BETA_TWO * second + (1.0 - BETA_TWO) * grad * grad
    denom = jnp.sqrt(second / (1.0 - BETA_TWO**STEP)) + ADAM_EPS
    return (param - BIAS_RATE * (first / (1.0 - BETA_ONE**STEP)) / denom, first, second)


def local(
    token_ids,
    lengths,
    top_ids,
    aux_ids,
    dead_set,
    token_table,
    position_table,
    ln_gains,
    frozen_bias,
    w_qkv,
    w_proj,
    w_fc,
    w_out,
    enc_weight,
    enc_bias,
    dec_weight,
    decoder_bias,
    enc_moment,
    dec_moment,
    encb_first,
    encb_second,
    decb_first,
    decb_second,
):
    chips = lax.axis_size("chip")
    narrow_count = lax.axis_size("narrow")
    wide_count = 2 * chips
    wide = ("chip", "core")
    chip_pos = lax.axis_index("chip")
    core_pos = lax.axis_index("core")
    wide_pos = 2 * chip_pos + core_pos
    narrow_pos = lax.axis_index("narrow")
    row_count = token_ids.shape[0]
    model_width = token_table.shape[1]
    wide_latents = enc_weight.shape[1]
    own_latents = wide_latents // narrow_count
    half_latents = own_latents // 2
    latent_count = chips * own_latents
    core_rows = narrow_count * row_count
    bf16, f32 = jnp.bfloat16, jnp.float32
    to_latents = (((1,), (1,)), ((), ()))
    over_rows = (((0,), (0,)), ((), ()))
    place = jnp.stack([chip_pos, core_pos, narrow_pos]).astype(jnp.int32)
    bits = [1 << bit for bit in range(chips.bit_length() - 1)]
    orders = (bits, bits[::-1])

    def after(value, *others):
        return lax.optimization_barrier((value, others))[0]

    def swap(value, axis, offset):
        count = lax.axis_size(axis)
        return lax.ppermute(value, axis, [(spot, spot ^ offset) for spot in range(count)])

    def spread_narrow(value):
        parts = [value] + [swap(value, "narrow", k) for k in range(1, narrow_count)]
        return jnp.concatenate(parts, 0)

    def rows_to_latents(value):
        return lax.all_to_all(value, "narrow", split_axis=1, concat_axis=0, tiled=True)

    def cols_to_latents(value):
        return lax.all_to_all(value, "narrow", split_axis=0, concat_axis=1, tiled=True)

    def latents_to_rows(value):
        return lax.all_to_all(value, "narrow", split_axis=0, concat_axis=1, tiled=True)

    def latents_to_cols(value):
        return lax.all_to_all(value, "narrow", split_axis=1, concat_axis=0, tiled=True)

    def gather_chips(own, axis):
        pieces = []
        for part, order in enumerate(orders):
            held = lax.slice_in_dim(own, part * half_latents, (part + 1) * half_latents, axis=axis)
            for bit in order[:-1]:
                held = jnp.concatenate([held, swap(held, "chip", bit)], axis)
            pieces += [held, swap(held, "chip", order[-1])]
        return pieces

    def scatter_chips(keeps, sents):
        results, sums = [], []
        for order, held, sent in zip(orders, keeps, sents):
            held = held + swap(sent, "chip", order[-1]).astype(f32)
            for bit in reversed(order[:-1]):
                lower, upper = jnp.split(held, 2, 1)
                sent = upper[:model_width].astype(bf16)
                if held.shape[0] > model_width:
                    lines = split_bf(upper[model_width] + upper[model_width + 1])
                    spare = jnp.zeros((14, upper.shape[1]), bf16)
                    sent = jnp.concatenate([sent, *(line[None] for line in lines), spare], 0)
                held = lower + swap(sent, "chip", bit).astype(f32)
            results.append(held[:model_width])
            if held.shape[0] > model_width:
                sums.append(held[model_width] + held[model_width + 1])
        return jnp.concatenate(results, 1), jnp.concatenate(sums) if sums else None

    vocab_dev = token_table.shape[0]
    every_ids = lax.all_gather(token_ids, wide, axis=0, tiled=False).reshape(wide_count, row_count)
    every_ids = jnp.concatenate(
        [
            lax.dynamic_slice_in_dim(every_ids, wide_pos ^ offset, 1, 0)
            for offset in range(wide_count)
        ],
        1,
    )[0]
    local_ids = every_ids - wide_pos * vocab_dev
    inside = (local_ids >= 0) & (local_ids < vocab_dev)
    looked = jnp.take(token_table, jnp.clip(local_ids, 0, vocab_dev - 1), axis=0)
    looked = jnp.where(inside[:, None], looked, jnp.zeros((), bf16))
    enc_own = rows_to_latents(enc_weight.astype(bf16))
    picks = after(jnp.concatenate([top_ids, aux_ids], 1), every_ids)
    near_picks = spread_narrow(picks)
    far_picks = swap(near_picks, "core", 1)

    looked = looked.reshape(chips, 2, row_count, model_width)
    looked = looked[:, 0] + swap(looked[:, 1], "core", 1)
    embedded = looked[0].astype(f32)
    for k in range(1, chips):
        embedded = embedded + swap(looked[k], "chip", k).astype(f32)

    bias_rows = jnp.concatenate(
        [enc_bias.astype(bf16)[None], jnp.zeros((15, own_latents), bf16)], 0
    )
    enc_biased = jnp.concatenate([enc_own, bias_rows], 0)
    enc_parts = gather_chips(enc_biased, 1)
    dec_own = cols_to_latents(after(dec_weight, enc_own).astype(bf16))

    dead_here = jnp.stack(
        [
            lax.dynamic_slice_in_dim(
                dead_set,
                (2 * (chip_pos ^ offset) + core_pos) * wide_latents + narrow_pos * own_latents,
                own_latents,
            )
            for offset in range(chips)
        ]
    )
    places = [0]
    dead_parts = []
    for part, order in enumerate(orders):
        places = [0]
        for bit in order:
            places = places + [spot ^ bit for spot in places]
        for spot in places:
            dead_parts.append(dead_here[spot, part * half_latents : (part + 1) * half_latents])
    dead_here = jnp.concatenate(dead_parts)[None]
    sizes = (wide_latents, own_latents, top_ids.shape[1], orders)
    near_codes = kind_codes(place, after(near_picks, enc_biased), dead_here, *sizes)

    start = after(embedded, near_codes) + position_table[:row_count].astype(f32)
    ctx_length = lengths[0]
    inputs = frozen_block(start, ctx_length, ln_gains, frozen_bias, w_qkv, w_proj, w_fc, w_out)
    counted = (jnp.arange(row_count) < ctx_length).astype(f32)
    dec_own = after(dec_own, inputs)
    dec_parts = gather_chips(dec_own, 0)
    near_inputs = spread_narrow(after(inputs, dec_own))
    far_codes = kind_codes(place, after(far_picks, inputs), dead_here, *sizes)
    near_inputs = after(near_inputs, far_codes)
    far_inputs = swap(near_inputs, "core", 1)
    codes = jnp.concatenate([near_codes, far_codes], 0)
    all_inputs = jnp.concatenate([near_inputs, far_inputs], 0)
    encoder_in = (all_inputs.astype(f32) - decoder_bias).astype(bf16)
    top_acts, aux_acts, far, near = forward(encoder_in, codes, enc_parts, dec_parts)
    encoder_t = encoder_in.T
    rebuilt = near + swap(far, "core", 1).astype(f32)
    rounded = rebuilt.astype(bf16)
    rebuilt = rebuilt[:row_count]
    for k in range(1, narrow_count):
        part = rounded[k * row_count : (k + 1) * row_count]
        rebuilt = rebuilt + swap(part, "narrow", k).astype(f32)
    target = inputs.astype(f32)
    reconstructed_input = rebuilt[:, :model_width] + decoder_bias
    auxiliary_reconstruction = rebuilt[:, model_width:]
    recon_error = target - reconstructed_input
    aux_gap = auxiliary_reconstruction - recon_error
    token_loss = (
        counted
        * (jnp.sum(recon_error * recon_error, 1) + AUX_COEF * jnp.sum(aux_gap * aux_gap, 1))
        / model_width
    )
    back_recon = 2.0 / model_width * counted[:, None] * (reconstructed_input - target)
    back_aux = 2.0 * AUX_COEF / model_width * counted[:, None] * aux_gap
    back_rows = jnp.concatenate([back_recon, back_aux], 1).astype(bf16)
    near_back = spread_narrow(back_rows)
    shard_rows = jnp.concatenate([near_back, swap(near_back, "core", 1)], 0)
    back_t = shard_rows.T
    dec_sent = dec_grads(back_t, top_acts, aux_acts, (1, 3), bf16)
    shard_rows, top_acts, dec_sent = lax.optimization_barrier((shard_rows, top_acts, dec_sent))
    dec_keep = dec_grads(back_t, top_acts, aux_acts, (0, 2), f32)
    shard_rows, dec_keep = lax.optimization_barrier((shard_rows, dec_keep))
    enc_sent = enc_grads(encoder_t, shard_rows, codes, dec_parts[1::2], (1, 3), bf16)
    shard_rows, enc_sent = lax.optimization_barrier((shard_rows, enc_sent))
    enc_keep = enc_grads(encoder_t, shard_rows, codes, dec_parts[::2], (0, 2), f32)
    dec_moment_own = rows_to_latents(after(dec_moment, back_rows).astype(bf16).T)
    enc_moment_own = rows_to_latents(after(enc_moment, dec_moment_own).astype(bf16))
    dec_grad, _ = scatter_chips(dec_keep, dec_sent)
    enc_grad, encb_grad = scatter_chips(enc_keep, enc_sent)
    bias_term = jnp.sum(back_rows[:, :model_width], 0, dtype=f32) - jnp.dot(
        enc_own.astype(f32), encb_grad, precision=HIGH_PRECISION
    )

    def sum_gram(part, vector, fill):
        half = model_width // 2
        rows = half // chips
        spare = jnp.zeros((14, model_width), bf16)

        def pack(block, vector):
            lines = [line[None] for line in split_bf(vector)]
            return jnp.concatenate([block.astype(bf16), *lines, spare], 0)

        def unpack(got):
            got = got.astype(f32)
            return got[:-16], got[-16] + got[-15]

        def block_of(value, index, count):
            return lax.dynamic_slice_in_dim(value, index * count, count, 0)

        def exchange(sents, axis):
            got = [swap(sent, axis, k + 1) for k, sent in enumerate(sents)]
            return fill(sents, got)

        sent = pack(block_of(part, 1 - core_pos, half), vector)
        (got,) = exchange([sent], "core")
        got, more = unpack(got)
        part, vector = block_of(part, core_pos, half) + got, vector + more
        total = block_of(part, chip_pos, rows)
        sents = [pack(block_of(part, chip_pos ^ k, rows), vector) for k in range(1, chips)]
        for got in exchange(sents, "chip"):
            got, more = unpack(got)
            total, vector = total + got, vector + more
        for got in exchange([pack(total, vector)] * (narrow_count - 1), "narrow"):
            got, more = unpack(got)
            total, vector = total + got, vector + more
        near = jnp.stack([total, *exchange([total] * (chips - 1), "chip")])
        (far,) = exchange([near], "core")
        return near, far, vector

    dec_own_next = (MOMENTUM * dec_moment_own.astype(f32) + dec_grad).astype(bf16)
    dec_own_next, enc_keep = lax.optimization_barrier((dec_own_next, enc_keep))
    dec_near, dec_far, _ = sum_gram(
        lax.dot_general(dec_own_next, dec_own_next, to_latents, preferred_element_type=f32),
        jnp.zeros((model_width,), f32),
        lambda sents, got: got,
    )
    enc_own_next = (MOMENTUM * enc_moment_own.astype(f32) + enc_grad).astype(bf16)
    enc_gram = lax.dot_general(
        enc_own_next, enc_own_next, to_latents, preferred_element_type=f32
    )
    enc_gram, dec_near = lax.optimization_barrier((enc_gram, dec_near))
    progress = []

    def dec_fill(sents, got):
        step = len(progress)
        if step == 0:
            state = series_start(after(place, sents), dec_near, dec_far)
        else:
            state = series_next(step, after(progress[-1], sents))
        got, state = lax.optimization_barrier((got, state))
        progress.append(state)
        return got

    enc_near, enc_far, grad_decb = sum_gram(enc_gram, bias_term, dec_fill)
    dec_factor = progress[-1][0]
    dec_rows_grad = latents_to_rows(after(dec_grad, enc_gram).astype(bf16))
    dec_ortho = latents_to_rows(
        jnp.dot(
            after(dec_factor, dec_rows_grad), dec_own_next, preferred_element_type=f32
        ).astype(bf16)
    )
    state = series_start(place, after(enc_near, dec_factor, dec_rows_grad), enc_far)
    for step in range(1, NS_STEPS - 1):
        state = series_next(step, state)
    state = after(state, dec_ortho)
    enc_rows_grad = latents_to_rows(after(enc_grad, dec_ortho).astype(bf16))
    enc_factor = series_next(NS_STEPS - 1, state)[0]
    enc_factor = after(enc_factor, enc_rows_grad)
    enc_ortho = latents_to_rows(
        jnp.dot(enc_factor, enc_own_next, preferred_element_type=f32).astype(bf16)
    )
    dec_ortho = dec_ortho.T
    dec_rows_grad = dec_rows_grad.T
    enc_next = MOMENTUM * enc_moment + enc_rows_grad.astype(f32)
    dec_next = MOMENTUM * dec_moment + dec_rows_grad.astype(f32)
    step_scale = MUON_RATE * 0.2 * math.sqrt(max(D, L))
    enc_new = enc_weight * (1.0 - MUON_RATE * DECAY) - step_scale * enc_ortho.astype(f32)
    dec_new = dec_weight * (1.0 - MUON_RATE * DECAY) - step_scale * dec_ortho.astype(f32)
    encb_new, encb_one, encb_two = adam_update(enc_bias, encb_grad, encb_first, encb_second)
    decb_new, decb_one, decb_two = adam_update(decoder_bias, grad_decb, decb_first, decb_second)
    return (
        token_loss,
        enc_new,
        enc_next,
        enc_new.astype(bf16),
        dec_new,
        dec_next,
        dec_new.astype(bf16),
        encb_new,
        encb_one,
        encb_two,
        decb_new,
        decb_one,
        decb_two,
    )


def solution(mesh):
    wide, narrow = mesh.devices.shape
    fine = Mesh(mesh.devices.reshape(wide // 2, 2, narrow), ("chip", "core", "narrow"))
    placed = (
        P(("chip", "core", "narrow")),
        P(("chip", "core", "narrow")),
        P(("chip", "core", "narrow"), None),
        P(("chip", "core", "narrow"), None),
        P(),
        P(("chip", "core"), None),
        P(),
        P(),
        P(),
        P(),
        P(),
        P(),
        P(),
        P("narrow", ("chip", "core")),
        P(("chip", "core", "narrow")),
        P(("chip", "core"), "narrow"),
        P(),
        P("narrow", ("chip", "core")),
        P(("chip", "core"), "narrow"),
        P(("chip", "core", "narrow")),
        P(("chip", "core", "narrow")),
        P(),
        P(),
    )
    return jax.shard_map(
        local,
        mesh=fine,
        in_specs=placed,
        out_specs=(
            P(("chip", "core", "narrow")),
            P("narrow", ("chip", "core")),
            P("narrow", ("chip", "core")),
            P("narrow", ("chip", "core")),
            P(("chip", "core"), "narrow"),
            P(("chip", "core"), "narrow"),
            P(("chip", "core"), "narrow"),
            P(("chip", "core", "narrow")),
            P(("chip", "core", "narrow")),
            P(("chip", "core", "narrow")),
            P(),
            P(),
            P(),
        ),
        check_vma=False,
    )
```

```python
import functools
import math

import jax
import jax.numpy as jnp
from jax import lax
from jax.experimental import pallas as pl
from jax.experimental.pallas import tpu as pltpu
from jax.sharding import Mesh
from jax.sharding import PartitionSpec as P

D = 768
HEAD_DIM = 64
L = 32768
NS_STEPS = 5
STEP = 10


HIGH_PRECISION = lax.Precision.HIGHEST
AUX_COEF = 1.0 / 32.0
EPS_NORM = 1e-05
NS_EPS = 1e-07
QA = 3.4445
QB = -4.775
QC = 2.0315
MOMENTUM = 0.95
MUON_RATE = 0.1
DECAY = 0.1
BIAS_RATE = 0.3
BETA_ONE = 0.9
BETA_TWO = 0.999
ADAM_EPS = 1e-08


def layer_norm(value, gain, shift):
    row_mean = jnp.mean(value, -1, keepdims=True)
    centred = value - row_mean
    row_var = jnp.mean(centred * centred, -1, keepdims=True)
    return centred * lax.rsqrt(row_var + EPS_NORM) * gain + shift


def frozen_block(start, ctx_length, ln_gains, frozen_bias, w_qkv, w_proj, w_fc, w_out):
    row_count, model_width = start.shape
    head_count = model_width // HEAD_DIM
    ff_width = w_fc.shape[1]
    shifts = frozen_bias[: 2 * model_width].reshape(2, model_width)
    b_qkv = frozen_bias[2 * model_width : 5 * model_width]
    b_proj = frozen_bias[5 * model_width : 6 * model_width]
    b_fc = frozen_bias[6 * model_width : 6 * model_width + ff_width]
    b_out = frozen_bias[6 * model_width + ff_width :]
    normed = layer_norm(start, ln_gains[0], shifts[0]).astype(jnp.bfloat16)
    qkv_rows = (jnp.dot(normed, w_qkv, preferred_element_type=jnp.float32) + b_qkv).astype(
        jnp.bfloat16
    )
    head_split = qkv_rows.reshape(row_count, 3, head_count, HEAD_DIM)
    scores = jnp.einsum(
        "qhd,khd->hqk", head_split[:, 0], head_split[:, 1], preferred_element_type=jnp.float32
    ) * HEAD_DIM ** (-0.5)
    positions = jnp.arange(row_count)
    allowed = (positions[None, :] <= positions[:, None]) & (positions[None, :] < ctx_length)
    attn_probs = jax.nn.softmax(jnp.where(allowed[None], scores, -1e30), axis=-1).astype(
        jnp.bfloat16
    )
    mixed = jnp.einsum(
        "hqk,khd->qhd", attn_probs, head_split[:, 2], preferred_element_type=jnp.float32
    )
    mixed = mixed.reshape(row_count, model_width).astype(jnp.bfloat16)
    hidden = start + jnp.dot(mixed, w_proj, preferred_element_type=jnp.float32) + b_proj
    normed_two = layer_norm(hidden, ln_gains[1], shifts[1]).astype(jnp.bfloat16)
    inner_acts = jax.nn.gelu(
        jnp.dot(normed_two, w_fc, preferred_element_type=jnp.float32) + b_fc, approximate=True
    ).astype(jnp.bfloat16)
    return (hidden + jnp.dot(inner_acts, w_out, preferred_element_type=jnp.float32) + b_out).astype(
        jnp.bfloat16
    )


def split_bf(value):
    high = value.astype(jnp.bfloat16)
    return high, (value - high.astype(jnp.float32)).astype(jnp.bfloat16)


def row_blocks(size, body):
    block = 256

    def step(index, carry):
        body(pl.ds(pl.multiple_of(index * block, block), block), index * block)
        return carry

    lax.fori_loop(0, size // block, step, 0)


def eye_rows(start, size):
    rows = lax.broadcasted_iota(jnp.int32, (256, size), 0) + start
    cols = lax.broadcasted_iota(jnp.int32, (256, size), 1)
    return (rows == cols).astype(jnp.float32)


def dot_f32(a, b):
    return jnp.dot(a, b, preferred_element_type=jnp.float32)


def store_split(pair, rows, value):
    pair[0][rows, :], pair[1][rows, :] = split_bf(value)


def three(left, right, rows):
    high, low = left[0][rows, :], left[1][rows, :]
    return dot_f32(high, right[0][...]) + (
        dot_f32(high, right[1][...]) + dot_f32(low, right[0][...])
    )


def series_step(gram, poly, half, out, old, new, step):
    size = gram[0].shape[0]
    last = step == NS_STEPS - 1
    exact_square = step >= 3

    def poly_rows(rows, start):
        here = gram[0][rows, :].astype(jnp.float32) + gram[1][rows, :].astype(jnp.float32)
        if exact_square:
            square = three(gram, gram, rows)
        else:
            square = dot_f32(gram[0][rows, :], gram[0][...])
        store_split(poly, rows, QA * eye_rows(start, size) + QB * here + QC * square)

    def half_rows(rows, start):
        store_split(half, rows, three(gram, poly, rows))

    def gram_rows(rows, start):
        store_split(out, rows, three(poly, half, rows))

    def product_rows(rows, start):
        new[rows, :] = dot_f32(poly[0][rows, :], old[...]).astype(jnp.bfloat16)

    row_blocks(size, poly_rows)
    if not last:
        row_blocks(size, half_rows)
        row_blocks(size, gram_rows)
    if step > 0:
        row_blocks(size, product_rows)


def first_kernel(place_ref, near_ref, far_ref, o_hi, o_lo, q_ref, total, *scratch):
    size = total.shape[0]
    chips, rows_each = near_ref.shape[:2]
    chip, core = place_ref[0], place_ref[1]
    gram, poly, half = scratch[:2], scratch[2:4], scratch[4:6]
    for offset in range(chips):
        for side, source in enumerate((near_ref, far_ref)):
            first = jnp.bitwise_xor(core, side) * (size // 2)
            first = first + jnp.bitwise_xor(chip, offset) * rows_each
            total[pl.ds(pl.multiple_of(first, 8), rows_each), :] = source[offset].astype(
                jnp.float32
            )

    def trace_part(index, value):
        start = pl.multiple_of(index * 256, 256)
        return value + jnp.sum(total[pl.ds(start, 256), :] * eye_rows(start, size))

    trace_sum = lax.fori_loop(0, size // 256, trace_part, jnp.zeros((), jnp.float32))
    scale = 1.0 / (jnp.sqrt(jnp.full((1, 1), trace_sum)) + NS_EPS)

    def load_rows(rows, start):
        store_split(gram, rows, total[rows, :] * (scale * scale))

    row_blocks(size, load_rows)
    series_step(gram, poly, half, (o_hi, o_lo), None, None, 0)

    def product_rows(rows, start):
        value = poly[0][rows, :].astype(jnp.float32) + poly[1][rows, :].astype(jnp.float32)
        q_ref[rows, :] = (value * scale).astype(jnp.bfloat16)

    row_blocks(size, product_rows)


def middle_kernel(step, g_hi, g_lo, q_ref, o_hi, o_lo, out_ref, *scratch):
    series_step(
        (g_hi, g_lo), scratch[:2], scratch[2:4], (o_hi, o_lo), q_ref, out_ref, step
    )


def last_kernel(g_hi, g_lo, q_ref, out_ref, *scratch):
    series_step((g_hi, g_lo), scratch[:2], None, None, q_ref, out_ref, NS_STEPS - 1)


def square_call(kernel, outs, scratch, passes, *operands):
    size = operands[-1].shape[-1]
    whole = pl.BlockSpec(memory_space=pltpu.VMEM)
    specs = [whole] * len(operands)
    if operands[0].ndim == 1:
        specs[0] = pl.BlockSpec(memory_space=pltpu.SMEM)
    square = jax.ShapeDtypeStruct((size, size), jnp.bfloat16)
    return pl.pallas_call(
        kernel,
        out_shape=[square] * outs,
        in_specs=specs,
        out_specs=[whole] * outs,
        scratch_shapes=[pltpu.VMEM((size, size), kind) for kind in scratch],
        compiler_params=pltpu.CompilerParams(vmem_limit_bytes=40 * 2**20),
        cost_estimate=pl.CostEstimate(
            flops=passes * size**3 // 16, bytes_accessed=size * size // 2, transcendentals=0
        ),
    )(*operands)


def series_start(place, near, far):
    bf16 = jnp.bfloat16
    return square_call(first_kernel, 3, [jnp.float32] + [bf16] * 6, 8, place, near, far)


def series_next(step, state):
    bf16 = jnp.bfloat16
    if step == NS_STEPS - 1:
        return square_call(last_kernel, 1, [bf16] * 2, 4, *state)
    kernel = functools.partial(middle_kernel, step)
    return square_call(kernel, 3, [bf16] * 4, 8 if step < 3 else 10, *state)


def code_kernel(shifts, place_ref, ids_ref, dead_ref, out_ref, high, low, stage):
    wide_shift, own_shift, top_count, orders = shifts
    batch, groups = stage.shape[:2]
    rows, picks = ids_ref.shape
    bf16, f32 = jnp.bfloat16, jnp.float32
    chip, core, narrow = place_ref[0], place_ref[1], place_ref[2]
    latent_count = dead_ref.shape[1]
    half_shift = own_shift - 1

    ids = ids_ref[...]
    owner = lax.shift_right_logical(ids, wide_shift)
    within = jnp.bitwise_and(ids, (1 << wide_shift) - 1)
    mine = (lax.shift_right_logical(within, own_shift) == narrow) & (
        jnp.bitwise_and(owner, 1) == core
    )
    inner = jnp.bitwise_and(within, (1 << own_shift) - 1)
    offset = jnp.bitwise_xor(lax.shift_right_logical(owner, 1), chip)
    half = lax.shift_right_logical(inner, half_shift)
    spots = []
    for order in orders:
        spot = jnp.zeros_like(offset)
        for index, bit in enumerate(order[:-1]):
            spot = spot + jnp.where(jnp.bitwise_and(offset, bit) != 0, 1 << index, 0)
        sent = jnp.where(jnp.bitwise_and(offset, order[-1]) != 0, latent_count // 4, 0)
        spots.append(sent + lax.shift_left(spot, half_shift))
    column = (
        half * (latent_count // 2)
        + jnp.where(half == 0, spots[0], spots[1])
        + jnp.bitwise_and(inner, (1 << half_shift) - 1)
    )
    high[...] = jnp.where(mine, lax.shift_right_logical(column, 7), -1).astype(f32)
    low[...] = jnp.bitwise_and(column, 127).astype(f32)

    one, zero = jnp.ones((16, picks), bf16), jnp.zeros((16, picks), bf16)
    places = lax.broadcasted_iota(jnp.int32, (16, picks), 1)
    kinds = jnp.where(places < top_count, 1.0, 2.0).astype(bf16)
    steps = lax.broadcasted_iota(jnp.int32, (16, picks), 0).astype(f32).astype(bf16)

    def hot(row, count, value):
        row = jnp.broadcast_to(row, (16, picks)).astype(bf16)
        parts = [
            jnp.where(steps + jnp.asarray(16 * part, bf16) == row, value, zero)
            for part in range(max(1, count // 16))
        ]
        return jnp.concatenate(parts, 0).astype(jnp.float8_e4m3fn)

    def one_batch(index, carry):
        first = pl.multiple_of(index * batch, batch)
        for token in range(batch):
            row = pl.ds(first + token, 1)
            codes = lax.dot_general(
                hot(high[row, :], groups, kinds),
                hot(low[row, :], 128, one),
                (((1,), (1,)), ((), ())),
                preferred_element_type=f32,
            )
            stage[token] = codes[:groups]
        for group in range(groups):
            lanes = slice(group * 128, (group + 1) * 128)
            codes = stage[:, group, :]
            live = (codes != 2.0) | (dead_ref[:, lanes] == 1)
            out_ref[pl.ds(first, batch), lanes] = jnp.where(live, codes, 0.0).astype(bf16)
        return carry

    lax.fori_loop(0, rows // batch, one_batch, 0)


def kind_codes(place, ids, dead_here, sizes, part, parts, held=None):
    wide_latents, own_latents, top_count, orders = sizes
    row_total, pick_total = ids.shape
    latent_count = dead_here.shape[1]
    rows = min(128, row_total)
    first = part * (row_total // rows)
    shifts = (wide_latents.bit_length() - 1, own_latents.bit_length() - 1, top_count, orders)
    kernel = functools.partial(code_kernel, shifts)
    operands, specs, aliases = [place, ids, dead_here], [], {}
    if held is not None:
        operands, specs, aliases = operands + [held], [pl.BlockSpec(memory_space=pl.ANY)], {3: 0}

    def body(place_ref, ids_ref, dead_ref, *refs):
        kernel(place_ref, ids_ref, dead_ref, *refs[len(specs) :])

    return pl.pallas_call(
        body,
        grid=(row_total // rows,),
        out_shape=jax.ShapeDtypeStruct((parts * row_total, latent_count), jnp.bfloat16),
        in_specs=[
            pl.BlockSpec(memory_space=pltpu.SMEM),
            pl.BlockSpec((rows, pick_total), lambda i: (i, 0)),
            pl.BlockSpec((1, latent_count), lambda i: (0, 0)),
        ]
        + specs,
        out_specs=pl.BlockSpec((rows, latent_count), lambda i: (i + first, 0)),
        input_output_aliases=aliases,
        scratch_shapes=[
            pltpu.VMEM((rows, pick_total), jnp.float32),
            pltpu.VMEM((rows, pick_total), jnp.float32),
            pltpu.VMEM((32, latent_count // 128, 128), jnp.float32),
        ],
        compiler_params=pltpu.CompilerParams(vmem_limit_bytes=40 * 2**20),
        cost_estimate=pl.CostEstimate(
            flops=row_total * latent_count,
            bytes_accessed=row_total * pick_total,
            transcendentals=0,
        ),
    )(*operands)


def pick_copy(step, count, sources, target):
    for index, source in enumerate(sources):

        @pl.when(step // count == index)
        def _(source=source):
            target[...] = source[...]


def forward_kernel(count, x_ref, codes_ref, *refs):
    encs, decs = refs[:4], refs[4:8]
    top_ref, aux_ref, far_ref, near_ref = refs[8:12]
    enc, dec, acc_top, acc_aux = refs[12:]
    step = pl.program_id(0)
    rows_all, width = x_ref.shape
    block = min(1024, rows_all)
    pick_copy(step, count, encs, enc)
    pick_copy(step, count, decs, dec)

    @pl.when(step == 0)
    def _():
        acc_top[...] = jnp.zeros_like(acc_top)
        acc_aux[...] = jnp.zeros_like(acc_aux)

    bias = enc[pl.ds(width, 16), :].astype(jnp.float32)[:1]
    to_features = (((1,), (1,)), ((), ()))

    def one(index, carry):
        rows = pl.ds(pl.multiple_of(index * block, block), block)
        pre = (dot_f32(x_ref[rows, :], enc[pl.ds(0, width), :]) + bias).astype(jnp.bfloat16)
        codes = codes_ref[rows, :]
        zero = jnp.zeros_like(pre)
        top = jnp.where(codes == 1.0, pre, zero)
        aux = jnp.where(codes == 2.0, pre, zero)
        top_ref[rows, :] = top
        aux_ref[rows, :] = aux
        acc_top[rows, :] += lax.dot_general(
            top, dec[...], to_features, preferred_element_type=jnp.float32
        )
        acc_aux[rows, :] += lax.dot_general(
            aux, dec[...], to_features, preferred_element_type=jnp.float32
        )
        return carry

    lax.fori_loop(0, rows_all // block, one, 0)

    @pl.when(step == pl.num_programs(0) - 1)
    def _():
        half = rows_all // 2
        for first, acc in ((0, acc_top), (width, acc_aux)):
            near_ref[:, first : first + width] = acc[pl.ds(0, half), :]
            far_ref[:, first : first + width] = acc[pl.ds(half, half), :].astype(jnp.bfloat16)


def part_specs(shape, axis, block, count, starts):
    specs = []
    for index, first in enumerate(starts):

        def place(step, index=index, first=first):
            spot = jnp.clip(step - index * count, 0, count - 1)
            return (spot + first, 0) if axis == 0 else (0, spot + first)

        size = (block, shape[1]) if axis == 0 else (shape[0], block)
        specs.append(pl.BlockSpec(size, place))
    return specs


def forward(x, codes, encs, decs):
    rows, width = x.shape
    quarter = encs[0].shape[1]
    block = min(512, quarter)
    count = quarter // block
    lanes = pl.BlockSpec((rows, block), lambda step: (0, step))
    fixed = lambda shape: pl.BlockSpec(shape, lambda step: (0, 0))
    bf16, f32 = jnp.bfloat16, jnp.float32
    half_shape = (rows // 2, 2 * width)
    return pl.pallas_call(
        functools.partial(forward_kernel, count),
        grid=(4 * count,),
        out_shape=[
            jax.ShapeDtypeStruct(codes.shape, bf16),
            jax.ShapeDtypeStruct(codes.shape, bf16),
            jax.ShapeDtypeStruct(half_shape, bf16),
            jax.ShapeDtypeStruct(half_shape, f32),
        ],
        in_specs=[fixed(x.shape), lanes]
        + part_specs(encs[0].shape, 1, block, count, (0, 0, 0, 0))
        + part_specs(decs[0].shape, 1, block, count, (0, 0, 0, 0)),
        out_specs=[lanes, lanes, fixed(half_shape), fixed(half_shape)],
        scratch_shapes=[
            pltpu.VMEM((width + 16, block), bf16),
            pltpu.VMEM((width, block), bf16),
            pltpu.VMEM((rows, width), f32),
            pltpu.VMEM((rows, width), f32),
        ],
        compiler_params=pltpu.CompilerParams(vmem_limit_bytes=58 * 2**20),
        cost_estimate=pl.CostEstimate(
            flops=2 * rows * width * codes.shape[1],
            bytes_accessed=6 * rows * codes.shape[1],
            transcendentals=0,
        ),
    )(x, codes, *encs, *decs)


def store_part(count, refs, rows, value):
    step = pl.program_id(0)
    for index, ref in enumerate(refs):

        @pl.when(step // count == index)
        def _(ref=ref):
            ref[rows, :] = value.astype(ref.dtype)


def dec_grad_kernel(count, recon_ref, aux_back_ref, top_ref, aux_ref, *outs):
    def one(index, carry):
        rows = pl.ds(pl.multiple_of(index * 384, 384), 384)
        value = dot_f32(recon_ref[rows, :], top_ref[...]) + dot_f32(
            aux_back_ref[rows, :], aux_ref[...]
        )
        store_part(count, outs, rows, value)
        return carry

    lax.fori_loop(0, recon_ref.shape[0] // 384, one, 0)


def dec_grads(back_t, top_acts, aux_acts, quarters, kind):
    width = back_t.shape[0] // 2
    rows, latents = top_acts.shape
    quarter = latents // 4
    block = min(512, quarter)
    count = quarter // block

    def lanes(step):
        return (0, jnp.where(step < count, quarters[0], quarters[1] - 1) * count + step)

    acts = pl.BlockSpec((rows, block), lanes)
    shape = (width, quarter)
    return pl.pallas_call(
        functools.partial(dec_grad_kernel, count),
        grid=(2 * count,),
        out_shape=[jax.ShapeDtypeStruct(shape, kind)] * 2,
        in_specs=[
            pl.BlockSpec((width, rows), lambda step: (0, 0)),
            pl.BlockSpec((width, rows), lambda step: (1, 0)),
            acts,
            acts,
        ],
        out_specs=part_specs(shape, 1, block, count, (0, 0)),
        compiler_params=pltpu.CompilerParams(vmem_limit_bytes=58 * 2**20),
        cost_estimate=pl.CostEstimate(
            flops=rows * width * quarter // 8, bytes_accessed=rows * quarter // 4, transcendentals=0
        ),
    )(back_t, back_t, top_acts, aux_acts)


def enc_grad_kernel(count, x_ref, back_ref, codes_ref, dec_a, dec_b, out_a, out_b, dec, grads):
    step = pl.program_id(0)
    pick_copy(step, count, (dec_a, dec_b), dec)
    width, latents = dec.shape
    block = min(1024, back_ref.shape[0])

    def one(index, total):
        rows = pl.ds(pl.multiple_of(index * block, block), block)
        codes = codes_ref[rows, :].astype(jnp.float32)
        top = dot_f32(back_ref[rows, :width], dec[...])
        aux = dot_f32(back_ref[rows, width:], dec[...])
        value = jnp.where(codes == 1.0, top, jnp.where(codes == 2.0, aux, 0.0))
        value = value.astype(jnp.bfloat16)
        grads[rows, :] = value
        return total + jnp.sum(value.astype(jnp.float32), 0, keepdims=True)

    total = lax.fori_loop(
        0, back_ref.shape[0] // block, one, jnp.zeros((1, latents), jnp.float32)
    )

    def two(index, carry):
        rows = pl.ds(pl.multiple_of(index * 384, 384), 384)
        store_part(count, (out_a, out_b), rows, dot_f32(x_ref[rows, :], grads[...]))
        return carry

    lax.fori_loop(0, width // 384, two, 0)
    lines = lax.broadcasted_iota(jnp.int32, (16, latents), 0)
    if out_a.dtype == jnp.bfloat16:
        high = total.astype(jnp.bfloat16).astype(jnp.float32)
        lines = jnp.where(lines == 0, high, jnp.where(lines == 1, total - high, 0.0))
    else:
        lines = jnp.where(lines == 0, total, 0.0)
    store_part(count, (out_a, out_b), pl.ds(width, 16), lines)


def enc_grads(x_t, back, codes, parts, quarters, kind):
    width, rows = x_t.shape
    quarter = codes.shape[1] // 4
    block = min(512, quarter)
    count = quarter // block

    def lanes(step):
        return (0, jnp.where(step < count, quarters[0], quarters[1] - 1) * count + step)

    shape = (width + 16, quarter)
    return pl.pallas_call(
        functools.partial(enc_grad_kernel, count),
        grid=(2 * count,),
        out_shape=[jax.ShapeDtypeStruct(shape, kind)] * 2,
        in_specs=[
            pl.BlockSpec(x_t.shape, lambda step: (0, 0)),
            pl.BlockSpec(back.shape, lambda step: (0, 0)),
            pl.BlockSpec((rows, block), lanes),
        ]
        + part_specs(parts[0].shape, 1, block, count, (0, 0)),
        out_specs=part_specs(shape, 1, block, count, (0, 0)),
        scratch_shapes=[
            pltpu.VMEM((width, block), jnp.bfloat16),
            pltpu.VMEM((rows, block), jnp.bfloat16),
        ],
        compiler_params=pltpu.CompilerParams(vmem_limit_bytes=58 * 2**20),
        cost_estimate=pl.CostEstimate(
            flops=rows * width * quarter // 8, bytes_accessed=rows * quarter // 4, transcendentals=0
        ),
    )(x_t, back, codes, *parts)


def finish_kernel(place_ref, factor_ref, momentum_ref, weight_ref, *outs):
    new_ref, next_ref, copy_ref = outs
    rows = factor_ref.shape[0]
    f32 = jnp.float32
    momentum = momentum_ref[0]
    kept = momentum_ref[0, pl.ds(pl.multiple_of(place_ref[2] * rows, 16), rows), :].astype(f32)
    ortho = dot_f32(factor_ref[...], momentum)
    next_ref[...] = kept
    step_scale = MUON_RATE * 0.2 * math.sqrt(max(D, L))
    value = weight_ref[...] * (1.0 - MUON_RATE * DECAY) - step_scale * ortho
    new_ref[...] = value
    copy_ref[...] = value.astype(jnp.bfloat16)


def finish(place, factor, momenta, weight):
    count, width, block = momenta.shape
    rows = weight.shape[0]
    part = pl.BlockSpec((rows, block), lambda step, place: (0, step))
    return pl.pallas_call(
        finish_kernel,
        grid_spec=pltpu.PrefetchScalarGridSpec(
            num_scalar_prefetch=1,
            grid=(count,),
            in_specs=[
                pl.BlockSpec((rows, width), lambda step, place: (place[2], 0)),
                pl.BlockSpec((1, width, block), lambda step, place: (step, 0, 0)),
                part,
            ],
            out_specs=[part] * 3,
        ),
        out_shape=[
            jax.ShapeDtypeStruct(weight.shape, jnp.float32),
            jax.ShapeDtypeStruct(weight.shape, jnp.float32),
            jax.ShapeDtypeStruct(weight.shape, jnp.bfloat16),
        ],
        compiler_params=pltpu.CompilerParams(vmem_limit_bytes=58 * 2**20),
        cost_estimate=pl.CostEstimate(
            flops=2 * rows * width * block * count,
            bytes_accessed=8 * rows * block * count,
            transcendentals=0,
        ),
    )(place, factor, momenta, weight)


def adam_update(param, grad, first, second):
    first = BETA_ONE * first + (1.0 - BETA_ONE) * grad
    second = BETA_TWO * second + (1.0 - BETA_TWO) * grad * grad
    denom = jnp.sqrt(second / (1.0 - BETA_TWO**STEP)) + ADAM_EPS
    return (param - BIAS_RATE * (first / (1.0 - BETA_ONE**STEP)) / denom, first, second)


def local(
    token_ids,
    lengths,
    top_ids,
    aux_ids,
    dead_set,
    token_table,
    position_table,
    ln_gains,
    frozen_bias,
    w_qkv,
    w_proj,
    w_fc,
    w_out,
    enc_weight,
    enc_bias,
    dec_weight,
    decoder_bias,
    enc_moment,
    dec_moment,
    encb_first,
    encb_second,
    decb_first,
    decb_second,
):
    chips = lax.axis_size("chip")
    narrow_count = lax.axis_size("narrow")
    wide_count = 2 * chips
    wide = ("chip", "core")
    chip_pos = lax.axis_index("chip")
    core_pos = lax.axis_index("core")
    wide_pos = 2 * chip_pos + core_pos
    narrow_pos = lax.axis_index("narrow")
    row_count = token_ids.shape[0]
    model_width = token_table.shape[1]
    wide_latents = enc_weight.shape[1]
    own_latents = wide_latents // narrow_count
    half_latents = own_latents // 2
    latent_count = chips * own_latents
    core_rows = narrow_count * row_count
    bf16, f32 = jnp.bfloat16, jnp.float32
    to_latents = (((1,), (1,)), ((), ()))
    over_rows = (((0,), (0,)), ((), ()))
    place = jnp.stack([chip_pos, core_pos, narrow_pos]).astype(jnp.int32)
    bits = [1 << bit for bit in range(chips.bit_length() - 1)]
    orders = (bits, bits[::-1])

    tie = lambda *values: lax.optimization_barrier(values)

    def swap(value, axis, offset):
        count = lax.axis_size(axis)
        return lax.ppermute(value, axis, [(spot, spot ^ offset) for spot in range(count)])

    def spread_narrow(value):
        parts = [value] + [swap(value, "narrow", k) for k in range(1, narrow_count)]
        return jnp.concatenate(parts, 0)

    def rows_to_latents(value):
        return lax.all_to_all(value, "narrow", split_axis=1, concat_axis=0, tiled=True)

    def gather_start(own, axis):
        halves = []
        for part, order in enumerate(orders):
            held = lax.slice_in_dim(own, part * half_latents, (part + 1) * half_latents, axis=axis)
            for bit in order[:-1]:
                held = jnp.concatenate([held, swap(held, "chip", bit)], axis)
            halves.append(held)
        return halves

    def gather_end(halves):
        pieces = []
        for held, order in zip(halves, orders):
            pieces += [held, swap(held, "chip", order[-1])]
        return pieces

    def scatter_chips(keeps, gots):
        results, sums = [], []
        for order, held, got in zip(orders, keeps, gots):
            held = held + got.astype(f32)
            for bit in reversed(order[:-1]):
                lower, upper = jnp.split(held, 2, 1)
                sent = upper[:model_width].astype(bf16)
                if held.shape[0] > model_width:
                    lines = split_bf(upper[model_width] + upper[model_width + 1])
                    spare = jnp.zeros((14, upper.shape[1]), bf16)
                    sent = jnp.concatenate([sent, *(line[None] for line in lines), spare], 0)
                held = lower + swap(sent, "chip", bit).astype(f32)
            results.append(held[:model_width])
            if held.shape[0] > model_width:
                sums.append(held[model_width] + held[model_width + 1])
        return jnp.concatenate(results, 1), jnp.concatenate(sums) if sums else None

    vocab_dev = token_table.shape[0]
    every_ids = lax.all_gather(token_ids, wide, axis=0, tiled=False).reshape(wide_count, row_count)
    every_ids = jnp.concatenate(
        [
            lax.dynamic_slice_in_dim(every_ids, wide_pos ^ offset, 1, 0)
            for offset in range(wide_count)
        ],
        1,
    )[0]
    local_ids = every_ids - wide_pos * vocab_dev
    inside = (local_ids >= 0) & (local_ids < vocab_dev)
    looked = jnp.take(token_table, jnp.clip(local_ids, 0, vocab_dev - 1), axis=0)
    looked = jnp.where(inside[:, None], looked, jnp.zeros((), bf16))
    dec_weight_t, dec_moment_t = dec_weight.T, dec_moment.T
    rows_each = enc_weight.shape[0]
    enc_own = rows_to_latents(enc_weight.astype(bf16))
    picks = jnp.concatenate([top_ids, aux_ids], 1)
    near_picks = spread_narrow(picks)
    far_picks = swap(near_picks, "core", 1)

    looked = looked.reshape(chips, 2, row_count, model_width)
    looked = looked[:, 0] + swap(looked[:, 1], "core", 1)
    embedded = looked[0].astype(f32)
    for k in range(1, chips):
        embedded = embedded + swap(looked[k], "chip", k).astype(f32)

    bias_rows = jnp.concatenate(
        [enc_bias.astype(bf16)[None], jnp.zeros((15, own_latents), bf16)], 0
    )
    enc_own, embedded = tie(enc_own, embedded)
    dec_cast, enc_own = tie(dec_weight_t.astype(bf16), enc_own)
    dec_own = rows_to_latents(dec_cast)
    enc_halves = gather_start(jnp.concatenate([enc_own, bias_rows], 0), 1)

    dead_here = jnp.stack(
        [
            lax.dynamic_slice_in_dim(
                dead_set,
                (2 * (chip_pos ^ offset) + core_pos) * wide_latents + narrow_pos * own_latents,
                own_latents,
            )
            for offset in range(chips)
        ]
    )
    places = [0]
    dead_parts = []
    for part, order in enumerate(orders):
        places = [0]
        for bit in order:
            places = places + [spot ^ bit for spot in places]
        for spot in places:
            dead_parts.append(dead_here[spot, part * half_latents : (part + 1) * half_latents])
    dead_here = jnp.concatenate(dead_parts)[None]
    sizes = (wide_latents, own_latents, top_ids.shape[1], orders)
    start = embedded + position_table[:row_count].astype(f32)
    ctx_length = lengths[0]
    inputs = frozen_block(start, ctx_length, ln_gains, frozen_bias, w_qkv, w_proj, w_fc, w_out)
    counted = (jnp.arange(row_count) < ctx_length).astype(f32)
    dec_own, near_picks, inputs, enc_halves = tie(dec_own, near_picks, inputs, enc_halves)
    enc_parts = gather_end(enc_halves)
    got_inputs = [swap(inputs, "narrow", k) for k in range(1, narrow_count)]
    dec_halves = gather_start(dec_own, 1)
    moments = jnp.concatenate([enc_moment.astype(bf16), dec_moment_t.astype(bf16)], 0)
    moments, dec_own = tie(moments, dec_own)
    moments = rows_to_latents(moments)
    near_codes = kind_codes(place, near_picks, dead_here, sizes, 0, 2)
    enc_lasts = [enc_parts[1], enc_parts[3]]
    dec_halves, got_inputs, near_codes, enc_lasts = tie(
        dec_halves, got_inputs, near_codes, enc_lasts
    )
    enc_parts = [enc_parts[0], enc_lasts[0], enc_parts[2], enc_lasts[1]]
    dec_parts = gather_end(dec_halves)
    near_inputs = jnp.concatenate([inputs, *got_inputs], 0)
    codes = kind_codes(place, far_picks, dead_here, sizes, 1, 2, near_codes)
    far_inputs, codes = tie(swap(near_inputs, "core", 1), codes)
    all_inputs = jnp.concatenate([near_inputs, far_inputs], 0)
    encoder_in = (all_inputs.astype(f32) - decoder_bias).astype(bf16)
    top_acts, aux_acts, far, near = forward(encoder_in, codes, enc_parts, dec_parts)
    far, moments = tie(far, moments)
    moments = moments.reshape(narrow_count, 2, rows_each, own_latents)
    enc_moment_own = moments[:, 0].reshape(model_width, own_latents)
    dec_moment_own = moments[:, 1].reshape(model_width, own_latents)
    encoder_t = encoder_in.T
    far_got, encoder_t = tie(swap(far, "core", 1), encoder_t)
    rebuilt = near + far_got.astype(f32)
    rounded = rebuilt.astype(bf16)
    rebuilt = rebuilt[:row_count]
    for k in range(1, narrow_count):
        part = rounded[k * row_count : (k + 1) * row_count]
        rebuilt = rebuilt + swap(part, "narrow", k).astype(f32)
    target = inputs.astype(f32)
    reconstructed_input = rebuilt[:, :model_width] + decoder_bias
    auxiliary_reconstruction = rebuilt[:, model_width:]
    recon_error = target - reconstructed_input
    aux_gap = auxiliary_reconstruction - recon_error
    token_loss = (
        counted
        * (jnp.sum(recon_error * recon_error, 1) + AUX_COEF * jnp.sum(aux_gap * aux_gap, 1))
        / model_width
    )
    back_recon = 2.0 / model_width * counted[:, None] * (reconstructed_input - target)
    back_aux = 2.0 * AUX_COEF / model_width * counted[:, None] * aux_gap
    back_rows = jnp.concatenate([back_recon, back_aux], 1).astype(bf16)
    near_back = spread_narrow(back_rows)
    shard_rows = jnp.concatenate([near_back, swap(near_back, "core", 1)], 0)
    back_t = shard_rows.T
    dec_sent = dec_grads(back_t, top_acts, aux_acts, (1, 3), bf16)
    back_t, dec_sent = tie(back_t, dec_sent)
    dec_keep = dec_grads(back_t, top_acts, aux_acts, (0, 2), f32)
    shard_rows, dec_keep = tie(shard_rows, dec_keep)
    enc_sent = enc_grads(encoder_t, shard_rows, codes, dec_parts[1::2], (1, 3), bf16)
    shard_rows, enc_sent = tie(shard_rows, enc_sent)
    enc_keep = enc_grads(encoder_t, shard_rows, codes, dec_parts[::2], (0, 2), f32)
    dec_gots = [swap(sent, "chip", order[-1]) for order, sent in zip(orders, dec_sent)]
    dec_gots, enc_sent = tie(dec_gots, enc_sent)
    enc_gots = [swap(sent, "chip", order[-1]) for order, sent in zip(orders, enc_sent)]
    dec_grad, _ = scatter_chips(dec_keep, dec_gots)
    dec_grad, enc_keep = tie(dec_grad, enc_keep)
    def sum_gram(part, vector, fill):
        half = model_width // 2
        rows = half // chips
        spare = jnp.zeros((14, model_width), bf16)

        def pack(block, vector):
            lines = [line[None] for line in split_bf(vector)]
            return jnp.concatenate([block.astype(bf16), *lines, spare], 0)

        def unpack(got):
            got = got.astype(f32)
            return got[:-16], got[-16] + got[-15]

        def block_of(value, index, count):
            return lax.dynamic_slice_in_dim(value, index * count, count, 0)

        def exchange(sents, axis):
            got = [swap(sent, axis, k + 1) for k, sent in enumerate(sents)]
            return fill(sents, got)

        sent = pack(block_of(part, 1 - core_pos, half), vector)
        (got,) = exchange([sent], "core")
        got, more = unpack(got)
        part, vector = block_of(part, core_pos, half) + got, vector + more
        total = block_of(part, chip_pos, rows)
        sents = [pack(block_of(part, chip_pos ^ k, rows), vector) for k in range(1, chips)]
        for got in exchange(sents, "chip"):
            got, more = unpack(got)
            total, vector = total + got, vector + more
        for got in exchange([pack(total, vector)] * (narrow_count - 1), "narrow"):
            got, more = unpack(got)
            total, vector = total + got, vector + more
        total = total.astype(bf16)
        near = jnp.stack([total, *exchange([total] * (chips - 1), "chip")])
        (far,) = exchange([near], "core")
        return near, far, vector

    dec_own_next = (MOMENTUM * dec_moment_own.astype(f32) + dec_grad).astype(bf16)
    dec_momenta = lax.all_gather(dec_own_next, "narrow")
    stages = []
    enc_grad = encb_grad = None

    def dec_note(sents, got):
        nonlocal enc_grad, encb_grad
        if not stages:
            got, gots = tie(got, enc_gots)
            enc_grad, encb_grad = scatter_chips(enc_keep, gots)
        if len(stages) == 2:
            got, enc_grad = tie(got, enc_grad)
        stages.append(got)
        return got

    dec_near, dec_far, _ = sum_gram(
        lax.dot_general(dec_own_next, dec_own_next, to_latents, preferred_element_type=f32),
        jnp.zeros((model_width,), f32),
        dec_note,
    )
    bias_term = jnp.sum(back_rows[:, :model_width], 0, dtype=f32) - jnp.dot(
        enc_own.astype(f32),
        encb_grad,
        precision=HIGH_PRECISION,
    )

    enc_own_next = (MOMENTUM * enc_moment_own.astype(f32) + enc_grad).astype(bf16)
    enc_gram = lax.dot_general(
        enc_own_next, enc_own_next, to_latents, preferred_element_type=f32
    )
    enc_gram, dec_near = lax.optimization_barrier((enc_gram, dec_near))
    enc_momenta = lax.all_gather(enc_own_next, "narrow")
    progress = []

    def dec_fill(sents, got):
        step = len(progress)
        if step == 0:
            early, _ = tie(dec_near, sents)
            state = series_start(place, early, dec_far)
        else:
            state = series_next(step, progress[-1])
        got, state = lax.optimization_barrier((got, state))
        progress.append(state)
        return got

    enc_near, enc_far, grad_decb = sum_gram(enc_gram, bias_term, dec_fill)
    dec_factor = progress[-1][0]
    dec_new, dec_next, dec_copy = finish(
        place, dec_factor, dec_momenta, dec_weight_t
    )
    state = series_start(place, enc_near, enc_far)
    for step in range(1, NS_STEPS):
        state = series_next(step, state)
    enc_new, enc_next, enc_copy = finish(place, state[0], enc_momenta, enc_weight)
    encb_new, encb_one, encb_two = adam_update(enc_bias, encb_grad, encb_first, encb_second)
    decb_new, decb_one, decb_two = adam_update(decoder_bias, grad_decb, decb_first, decb_second)
    return (
        token_loss,
        enc_new,
        enc_next,
        enc_copy,
        dec_new.T,
        dec_next.T,
        dec_copy.T,
        encb_new,
        encb_one,
        encb_two,
        decb_new,
        decb_one,
        decb_two,
    )


def solution(mesh):
    wide, narrow = mesh.devices.shape
    fine = Mesh(mesh.devices.reshape(wide // 2, 2, narrow), ("chip", "core", "narrow"))
    placed = (
        P(("chip", "core", "narrow")),
        P(("chip", "core", "narrow")),
        P(("chip", "core", "narrow"), None),
        P(("chip", "core", "narrow"), None),
        P(),
        P(("chip", "core"), None),
        P(),
        P(),
        P(),
        P(),
        P(),
        P(),
        P(),
        P("narrow", ("chip", "core")),
        P(("chip", "core", "narrow")),
        P(("chip", "core"), "narrow"),
        P(),
        P("narrow", ("chip", "core")),
        P(("chip", "core"), "narrow"),
        P(("chip", "core", "narrow")),
        P(("chip", "core", "narrow")),
        P(),
        P(),
    )
    return jax.shard_map(
        local,
        mesh=fine,
        in_specs=placed,
        out_specs=(
            P(("chip", "core", "narrow")),
            P("narrow", ("chip", "core")),
            P("narrow", ("chip", "core")),
            P("narrow", ("chip", "core")),
            P(("chip", "core"), "narrow"),
            P(("chip", "core"), "narrow"),
            P(("chip", "core"), "narrow"),
            P(("chip", "core", "narrow")),
            P(("chip", "core", "narrow")),
            P(("chip", "core", "narrow")),
            P(),
            P(),
            P(),
        ),
        check_vma=False,
    )
```

```python
import functools
import math

import jax
import jax.numpy as jnp
from jax import lax
from jax.experimental import pallas as pl
from jax.experimental.pallas import tpu as pltpu
from jax.sharding import Mesh
from jax.sharding import PartitionSpec as P

D = 768
HEAD_DIM = 64
L = 32768
NS_STEPS = 5
STEP = 10


HIGH_PRECISION = lax.Precision.HIGHEST
AUX_COEF = 1.0 / 32.0
EPS_NORM = 1e-05
NS_EPS = 1e-07
QA = 3.4445
QB = -4.775
QC = 2.0315
MOMENTUM = 0.95
MUON_RATE = 0.1
DECAY = 0.1
BIAS_RATE = 0.3
BETA_ONE = 0.9
BETA_TWO = 0.999
ADAM_EPS = 1e-08


def layer_norm(value, gain, shift):
    row_mean = jnp.mean(value, -1, keepdims=True)
    centred = value - row_mean
    row_var = jnp.mean(centred * centred, -1, keepdims=True)
    return centred * lax.rsqrt(row_var + EPS_NORM) * gain + shift


def frozen_block(start, ctx_length, ln_gains, frozen_bias, w_qkv, w_proj, w_fc, w_out):
    row_count, model_width = start.shape
    head_count = model_width // HEAD_DIM
    ff_width = w_fc.shape[1]
    shifts = frozen_bias[: 2 * model_width].reshape(2, model_width)
    b_qkv = frozen_bias[2 * model_width : 5 * model_width]
    b_proj = frozen_bias[5 * model_width : 6 * model_width]
    b_fc = frozen_bias[6 * model_width : 6 * model_width + ff_width]
    b_out = frozen_bias[6 * model_width + ff_width :]
    normed = layer_norm(start, ln_gains[0], shifts[0]).astype(jnp.bfloat16)
    qkv_rows = (jnp.dot(normed, w_qkv, preferred_element_type=jnp.float32) + b_qkv).astype(
        jnp.bfloat16
    )
    head_split = qkv_rows.reshape(row_count, 3, head_count, HEAD_DIM)
    scores = jnp.einsum(
        "qhd,khd->hqk", head_split[:, 0], head_split[:, 1], preferred_element_type=jnp.float32
    ) * HEAD_DIM ** (-0.5)
    positions = jnp.arange(row_count)
    allowed = (positions[None, :] <= positions[:, None]) & (positions[None, :] < ctx_length)
    attn_probs = jax.nn.softmax(jnp.where(allowed[None], scores, -1e30), axis=-1).astype(
        jnp.bfloat16
    )
    mixed = jnp.einsum(
        "hqk,khd->qhd", attn_probs, head_split[:, 2], preferred_element_type=jnp.float32
    )
    mixed = mixed.reshape(row_count, model_width).astype(jnp.bfloat16)
    hidden = start + jnp.dot(mixed, w_proj, preferred_element_type=jnp.float32) + b_proj
    normed_two = layer_norm(hidden, ln_gains[1], shifts[1]).astype(jnp.bfloat16)
    inner_acts = jax.nn.gelu(
        jnp.dot(normed_two, w_fc, preferred_element_type=jnp.float32) + b_fc, approximate=True
    ).astype(jnp.bfloat16)
    return (hidden + jnp.dot(inner_acts, w_out, preferred_element_type=jnp.float32) + b_out).astype(
        jnp.bfloat16
    )


def split_bf(value):
    high = value.astype(jnp.bfloat16)
    return high, (value - high.astype(jnp.float32)).astype(jnp.bfloat16)


def row_blocks(size, body):
    block = 256

    def step(index, carry):
        body(pl.ds(pl.multiple_of(index * block, block), block), index * block)
        return carry

    lax.fori_loop(0, size // block, step, 0)


def eye_rows(start, size):
    rows = lax.broadcasted_iota(jnp.int32, (256, size), 0) + start
    cols = lax.broadcasted_iota(jnp.int32, (256, size), 1)
    return (rows == cols).astype(jnp.float32)


def dot_f32(a, b):
    return jnp.dot(a, b, preferred_element_type=jnp.float32)


def store_split(pair, rows, value):
    pair[0][rows, :], pair[1][rows, :] = split_bf(value)


def three(left, right, rows):
    high, low = left[0][rows, :], left[1][rows, :]
    return dot_f32(high, right[0][...]) + (
        dot_f32(high, right[1][...]) + dot_f32(low, right[0][...])
    )


def series_step(gram, poly, half, out, old, new, step):
    size = gram[0].shape[0]
    last = step == NS_STEPS - 1
    exact_square = step >= 3

    def poly_rows(rows, start):
        here = gram[0][rows, :].astype(jnp.float32) + gram[1][rows, :].astype(jnp.float32)
        if exact_square:
            square = three(gram, gram, rows)
        else:
            square = dot_f32(gram[0][rows, :], gram[0][...])
        store_split(poly, rows, QA * eye_rows(start, size) + QB * here + QC * square)

    def half_rows(rows, start):
        store_split(half, rows, three(gram, poly, rows))

    def gram_rows(rows, start):
        store_split(out, rows, three(poly, half, rows))

    def product_rows(rows, start):
        new[rows, :] = dot_f32(poly[0][rows, :], old[...]).astype(jnp.bfloat16)

    row_blocks(size, poly_rows)
    if not last:
        row_blocks(size, half_rows)
        row_blocks(size, gram_rows)
    if step > 0:
        row_blocks(size, product_rows)


def first_kernel(place_ref, near_ref, far_ref, o_hi, o_lo, q_ref, total, *scratch):
    size = total.shape[0]
    chips, rows_each = near_ref.shape[:2]
    chip, core = place_ref[0], place_ref[1]
    gram, poly, half = scratch[:2], scratch[2:4], scratch[4:6]
    for offset in range(chips):
        for side, source in enumerate((near_ref, far_ref)):
            first = jnp.bitwise_xor(core, side) * (size // 2)
            first = first + jnp.bitwise_xor(chip, offset) * rows_each
            total[pl.ds(pl.multiple_of(first, 8), rows_each), :] = source[offset].astype(
                jnp.float32
            )

    def trace_part(index, value):
        start = pl.multiple_of(index * 256, 256)
        return value + jnp.sum(total[pl.ds(start, 256), :] * eye_rows(start, size))

    trace_sum = lax.fori_loop(0, size // 256, trace_part, jnp.zeros((), jnp.float32))
    scale = 1.0 / (jnp.sqrt(jnp.full((1, 1), trace_sum)) + NS_EPS)

    def load_rows(rows, start):
        store_split(gram, rows, total[rows, :] * (scale * scale))

    row_blocks(size, load_rows)
    series_step(gram, poly, half, (o_hi, o_lo), None, None, 0)

    def product_rows(rows, start):
        value = poly[0][rows, :].astype(jnp.float32) + poly[1][rows, :].astype(jnp.float32)
        q_ref[rows, :] = (value * scale).astype(jnp.bfloat16)

    row_blocks(size, product_rows)


def middle_kernel(step, g_hi, g_lo, q_ref, o_hi, o_lo, out_ref, *scratch):
    series_step(
        (g_hi, g_lo), scratch[:2], scratch[2:4], (o_hi, o_lo), q_ref, out_ref, step
    )


def last_kernel(g_hi, g_lo, q_ref, out_ref, *scratch):
    series_step((g_hi, g_lo), scratch[:2], None, None, q_ref, out_ref, NS_STEPS - 1)


def square_call(kernel, outs, scratch, passes, *operands):
    size = operands[-1].shape[-1]
    whole = pl.BlockSpec(memory_space=pltpu.VMEM)
    specs = [whole] * len(operands)
    if operands[0].ndim == 1:
        specs[0] = pl.BlockSpec(memory_space=pltpu.SMEM)
    square = jax.ShapeDtypeStruct((size, size), jnp.bfloat16)
    return pl.pallas_call(
        kernel,
        out_shape=[square] * outs,
        in_specs=specs,
        out_specs=[whole] * outs,
        scratch_shapes=[pltpu.VMEM((size, size), kind) for kind in scratch],
        compiler_params=pltpu.CompilerParams(vmem_limit_bytes=40 * 2**20),
        cost_estimate=pl.CostEstimate(
            flops=passes * size**3 // 16, bytes_accessed=size * size // 2, transcendentals=0
        ),
    )(*operands)


def series_start(place, near, far):
    bf16 = jnp.bfloat16
    return square_call(first_kernel, 3, [jnp.float32] + [bf16] * 6, 8, place, near, far)


def series_next(step, state):
    bf16 = jnp.bfloat16
    if step == NS_STEPS - 1:
        return square_call(last_kernel, 1, [bf16] * 2, 4, *state)
    kernel = functools.partial(middle_kernel, step)
    return square_call(kernel, 3, [bf16] * 4, 8 if step < 3 else 10, *state)


def code_kernel(shifts, place_ref, ids_ref, dead_ref, out_ref, high, low, stage):
    wide_shift, own_shift, top_count, orders = shifts
    batch, groups = stage.shape[:2]
    rows, picks = ids_ref.shape
    bf16, f32 = jnp.bfloat16, jnp.float32
    chip, core, narrow = place_ref[0], place_ref[1], place_ref[2]
    latent_count = dead_ref.shape[1]
    half_shift = own_shift - 1

    ids = ids_ref[...]
    owner = lax.shift_right_logical(ids, wide_shift)
    within = jnp.bitwise_and(ids, (1 << wide_shift) - 1)
    mine = (lax.shift_right_logical(within, own_shift) == narrow) & (
        jnp.bitwise_and(owner, 1) == core
    )
    inner = jnp.bitwise_and(within, (1 << own_shift) - 1)
    offset = jnp.bitwise_xor(lax.shift_right_logical(owner, 1), chip)
    half = lax.shift_right_logical(inner, half_shift)
    spots = []
    for order in orders:
        spot = jnp.zeros_like(offset)
        for index, bit in enumerate(order[:-1]):
            spot = spot + jnp.where(jnp.bitwise_and(offset, bit) != 0, 1 << index, 0)
        sent = jnp.where(jnp.bitwise_and(offset, order[-1]) != 0, latent_count // 4, 0)
        spots.append(sent + lax.shift_left(spot, half_shift))
    column = (
        half * (latent_count // 2)
        + jnp.where(half == 0, spots[0], spots[1])
        + jnp.bitwise_and(inner, (1 << half_shift) - 1)
    )
    high[...] = jnp.where(mine, lax.shift_right_logical(column, 7), -1).astype(f32)
    low[...] = jnp.bitwise_and(column, 127).astype(f32)

    one, zero = jnp.ones((16, picks), bf16), jnp.zeros((16, picks), bf16)
    places = lax.broadcasted_iota(jnp.int32, (16, picks), 1)
    kinds = jnp.where(places < top_count, 1.0, 2.0).astype(bf16)
    steps = lax.broadcasted_iota(jnp.int32, (16, picks), 0).astype(f32).astype(bf16)

    def hot(row, count, value):
        row = jnp.broadcast_to(row, (16, picks)).astype(bf16)
        parts = [
            jnp.where(steps + jnp.asarray(16 * part, bf16) == row, value, zero)
            for part in range(max(1, count // 16))
        ]
        return jnp.concatenate(parts, 0).astype(jnp.float8_e4m3fn)

    def one_batch(index, carry):
        first = pl.multiple_of(index * batch, batch)
        for token in range(batch):
            row = pl.ds(first + token, 1)
            codes = lax.dot_general(
                hot(high[row, :], groups, kinds),
                hot(low[row, :], 128, one),
                (((1,), (1,)), ((), ())),
                preferred_element_type=f32,
            )
            stage[token] = codes[:groups]
        for group in range(groups):
            lanes = slice(group * 128, (group + 1) * 128)
            codes = stage[:, group, :]
            live = (codes != 2.0) | (dead_ref[:, lanes] == 1)
            out_ref[pl.ds(first, batch), lanes] = jnp.where(live, codes, 0.0).astype(bf16)
        return carry

    lax.fori_loop(0, rows // batch, one_batch, 0)


def kind_codes(place, ids, dead_here, sizes, part, parts, held=None):
    wide_latents, own_latents, top_count, orders = sizes
    row_total, pick_total = ids.shape
    latent_count = dead_here.shape[1]
    rows = min(128, row_total)
    first = part * (row_total // rows)
    shifts = (wide_latents.bit_length() - 1, own_latents.bit_length() - 1, top_count, orders)
    kernel = functools.partial(code_kernel, shifts)
    operands, specs, aliases = [place, ids, dead_here], [], {}
    if held is not None:
        operands, specs, aliases = operands + [held], [pl.BlockSpec(memory_space=pl.ANY)], {3: 0}

    def body(place_ref, ids_ref, dead_ref, *refs):
        kernel(place_ref, ids_ref, dead_ref, *refs[len(specs) :])

    return pl.pallas_call(
        body,
        grid=(row_total // rows,),
        out_shape=jax.ShapeDtypeStruct((parts * row_total, latent_count), jnp.bfloat16),
        in_specs=[
            pl.BlockSpec(memory_space=pltpu.SMEM),
            pl.BlockSpec((rows, pick_total), lambda i: (i, 0)),
            pl.BlockSpec((1, latent_count), lambda i: (0, 0)),
        ]
        + specs,
        out_specs=pl.BlockSpec((rows, latent_count), lambda i: (i + first, 0)),
        input_output_aliases=aliases,
        scratch_shapes=[
            pltpu.VMEM((rows, pick_total), jnp.float32),
            pltpu.VMEM((rows, pick_total), jnp.float32),
            pltpu.VMEM((32, latent_count // 128, 128), jnp.float32),
        ],
        compiler_params=pltpu.CompilerParams(vmem_limit_bytes=40 * 2**20),
        cost_estimate=pl.CostEstimate(
            flops=row_total * latent_count,
            bytes_accessed=row_total * pick_total,
            transcendentals=0,
        ),
    )(*operands)


def pick_copy(step, count, sources, target):
    for index, source in enumerate(sources):

        @pl.when(step // count == index)
        def _(source=source):
            target[...] = source[...]


def forward_kernel(count, x_ref, codes_ref, *refs):
    encs, decs = refs[:4], refs[4:8]
    top_ref, aux_ref, far_ref, near_ref = refs[8:12]
    enc, dec, acc_top, acc_aux = refs[12:]
    step = pl.program_id(0)
    rows_all, width = x_ref.shape
    block = min(1024, rows_all)
    pick_copy(step, count, encs, enc)
    pick_copy(step, count, decs, dec)

    @pl.when(step == 0)
    def _():
        acc_top[...] = jnp.zeros_like(acc_top)
        acc_aux[...] = jnp.zeros_like(acc_aux)

    bias = enc[pl.ds(width, 16), :].astype(jnp.float32)[:1]
    to_features = (((1,), (1,)), ((), ()))

    def one(index, carry):
        rows = pl.ds(pl.multiple_of(index * block, block), block)
        pre = (dot_f32(x_ref[rows, :], enc[pl.ds(0, width), :]) + bias).astype(jnp.bfloat16)
        codes = codes_ref[rows, :]
        zero = jnp.zeros_like(pre)
        top = jnp.where(codes == 1.0, pre, zero)
        aux = jnp.where(codes == 2.0, pre, zero)
        top_ref[rows, :] = top
        aux_ref[rows, :] = aux
        acc_top[rows, :] += lax.dot_general(
            top, dec[...], to_features, preferred_element_type=jnp.float32
        )
        acc_aux[rows, :] += lax.dot_general(
            aux, dec[...], to_features, preferred_element_type=jnp.float32
        )
        return carry

    lax.fori_loop(0, rows_all // block, one, 0)

    @pl.when(step == pl.num_programs(0) - 1)
    def _():
        half = rows_all // 2
        for first, acc in ((0, acc_top), (width, acc_aux)):
            near_ref[:, first : first + width] = acc[pl.ds(0, half), :]
            far_ref[:, first : first + width] = acc[pl.ds(half, half), :].astype(jnp.bfloat16)


def part_specs(shape, axis, block, count, starts):
    specs = []
    for index, first in enumerate(starts):

        def place(step, index=index, first=first):
            spot = jnp.clip(step - index * count, 0, count - 1)
            return (spot + first, 0) if axis == 0 else (0, spot + first)

        size = (block, shape[1]) if axis == 0 else (shape[0], block)
        specs.append(pl.BlockSpec(size, place))
    return specs


def forward(x, codes, encs, decs):
    rows, width = x.shape
    quarter = encs[0].shape[1]
    block = min(512, quarter)
    count = quarter // block
    lanes = pl.BlockSpec((rows, block), lambda step: (0, step))
    fixed = lambda shape: pl.BlockSpec(shape, lambda step: (0, 0))
    bf16, f32 = jnp.bfloat16, jnp.float32
    half_shape = (rows // 2, 2 * width)
    return pl.pallas_call(
        functools.partial(forward_kernel, count),
        grid=(4 * count,),
        out_shape=[
            jax.ShapeDtypeStruct(codes.shape, bf16),
            jax.ShapeDtypeStruct(codes.shape, bf16),
            jax.ShapeDtypeStruct(half_shape, bf16),
            jax.ShapeDtypeStruct(half_shape, f32),
        ],
        in_specs=[fixed(x.shape), lanes]
        + part_specs(encs[0].shape, 1, block, count, (0, 0, 0, 0))
        + part_specs(decs[0].shape, 1, block, count, (0, 0, 0, 0)),
        out_specs=[lanes, lanes, fixed(half_shape), fixed(half_shape)],
        scratch_shapes=[
            pltpu.VMEM((width + 16, block), bf16),
            pltpu.VMEM((width, block), bf16),
            pltpu.VMEM((rows, width), f32),
            pltpu.VMEM((rows, width), f32),
        ],
        compiler_params=pltpu.CompilerParams(vmem_limit_bytes=58 * 2**20),
        cost_estimate=pl.CostEstimate(
            flops=2 * rows * width * codes.shape[1],
            bytes_accessed=6 * rows * codes.shape[1],
            transcendentals=0,
        ),
    )(x, codes, *encs, *decs)


def store_part(count, refs, rows, value):
    step = pl.program_id(0)
    for index, ref in enumerate(refs):

        @pl.when(step // count == index)
        def _(ref=ref):
            ref[rows, :] = value.astype(ref.dtype)


def dec_grad_kernel(count, recon_ref, aux_back_ref, top_ref, aux_ref, *outs):
    def one(index, carry):
        rows = pl.ds(pl.multiple_of(index * 384, 384), 384)
        value = dot_f32(recon_ref[rows, :], top_ref[...]) + dot_f32(
            aux_back_ref[rows, :], aux_ref[...]
        )
        store_part(count, outs, rows, value)
        return carry

    lax.fori_loop(0, recon_ref.shape[0] // 384, one, 0)


def dec_grads(back_t, top_acts, aux_acts, quarters, kind):
    width = back_t.shape[0] // 2
    rows, latents = top_acts.shape
    quarter = latents // 4
    block = min(512, quarter)
    count = quarter // block

    def lanes(step):
        return (0, jnp.where(step < count, quarters[0], quarters[1] - 1) * count + step)

    acts = pl.BlockSpec((rows, block), lanes)
    shape = (width, quarter)
    return pl.pallas_call(
        functools.partial(dec_grad_kernel, count),
        grid=(2 * count,),
        out_shape=[jax.ShapeDtypeStruct(shape, kind)] * 2,
        in_specs=[
            pl.BlockSpec((width, rows), lambda step: (0, 0)),
            pl.BlockSpec((width, rows), lambda step: (1, 0)),
            acts,
            acts,
        ],
        out_specs=part_specs(shape, 1, block, count, (0, 0)),
        compiler_params=pltpu.CompilerParams(vmem_limit_bytes=58 * 2**20),
        cost_estimate=pl.CostEstimate(
            flops=rows * width * quarter // 8, bytes_accessed=rows * quarter // 4, transcendentals=0
        ),
    )(back_t, back_t, top_acts, aux_acts)


def enc_grad_kernel(count, x_ref, back_ref, codes_ref, dec_a, dec_b, out_a, out_b, dec, grads):
    step = pl.program_id(0)
    pick_copy(step, count, (dec_a, dec_b), dec)
    width, latents = dec.shape
    block = min(1024, back_ref.shape[0])

    def one(index, total):
        rows = pl.ds(pl.multiple_of(index * block, block), block)
        codes = codes_ref[rows, :].astype(jnp.float32)
        top = dot_f32(back_ref[rows, :width], dec[...])
        aux = dot_f32(back_ref[rows, width:], dec[...])
        value = jnp.where(codes == 1.0, top, jnp.where(codes == 2.0, aux, 0.0))
        value = value.astype(jnp.bfloat16)
        grads[rows, :] = value
        return total + jnp.sum(value.astype(jnp.float32), 0, keepdims=True)

    total = lax.fori_loop(
        0, back_ref.shape[0] // block, one, jnp.zeros((1, latents), jnp.float32)
    )

    def two(index, carry):
        rows = pl.ds(pl.multiple_of(index * 384, 384), 384)
        store_part(count, (out_a, out_b), rows, dot_f32(x_ref[rows, :], grads[...]))
        return carry

    lax.fori_loop(0, width // 384, two, 0)
    lines = lax.broadcasted_iota(jnp.int32, (16, latents), 0)
    if out_a.dtype == jnp.bfloat16:
        high = total.astype(jnp.bfloat16).astype(jnp.float32)
        lines = jnp.where(lines == 0, high, jnp.where(lines == 1, total - high, 0.0))
    else:
        lines = jnp.where(lines == 0, total, 0.0)
    store_part(count, (out_a, out_b), pl.ds(width, 16), lines)


def enc_grads(x_t, back, codes, parts, quarters, kind):
    width, rows = x_t.shape
    quarter = codes.shape[1] // 4
    block = min(512, quarter)
    count = quarter // block

    def lanes(step):
        return (0, jnp.where(step < count, quarters[0], quarters[1] - 1) * count + step)

    shape = (width + 16, quarter)
    return pl.pallas_call(
        functools.partial(enc_grad_kernel, count),
        grid=(2 * count,),
        out_shape=[jax.ShapeDtypeStruct(shape, kind)] * 2,
        in_specs=[
            pl.BlockSpec(x_t.shape, lambda step: (0, 0)),
            pl.BlockSpec(back.shape, lambda step: (0, 0)),
            pl.BlockSpec((rows, block), lanes),
        ]
        + part_specs(parts[0].shape, 1, block, count, (0, 0)),
        out_specs=part_specs(shape, 1, block, count, (0, 0)),
        scratch_shapes=[
            pltpu.VMEM((width, block), jnp.bfloat16),
            pltpu.VMEM((rows, block), jnp.bfloat16),
        ],
        compiler_params=pltpu.CompilerParams(vmem_limit_bytes=58 * 2**20),
        cost_estimate=pl.CostEstimate(
            flops=rows * width * quarter // 8, bytes_accessed=rows * quarter // 4, transcendentals=0
        ),
    )(x_t, back, codes, *parts)


def finish_kernel(place_ref, factor_ref, momentum_ref, weight_ref, *outs):
    new_ref, next_ref, copy_ref = outs
    rows = factor_ref.shape[0]
    f32 = jnp.float32
    momentum = momentum_ref[0]
    kept = momentum_ref[0, pl.ds(pl.multiple_of(place_ref[2] * rows, 16), rows), :].astype(f32)
    ortho = dot_f32(factor_ref[...], momentum)
    next_ref[...] = kept
    step_scale = MUON_RATE * 0.2 * math.sqrt(max(D, L))
    value = weight_ref[...] * (1.0 - MUON_RATE * DECAY) - step_scale * ortho
    new_ref[...] = value
    copy_ref[...] = value.astype(jnp.bfloat16)


def finish(place, factor, momenta, weight):
    count, width, block = momenta.shape
    rows = weight.shape[0]
    part = pl.BlockSpec((rows, block), lambda step, place: (0, step))
    return pl.pallas_call(
        finish_kernel,
        grid_spec=pltpu.PrefetchScalarGridSpec(
            num_scalar_prefetch=1,
            grid=(count,),
            in_specs=[
                pl.BlockSpec((rows, width), lambda step, place: (place[2], 0)),
                pl.BlockSpec((1, width, block), lambda step, place: (step, 0, 0)),
                part,
            ],
            out_specs=[part] * 3,
        ),
        out_shape=[
            jax.ShapeDtypeStruct(weight.shape, jnp.float32),
            jax.ShapeDtypeStruct(weight.shape, jnp.float32),
            jax.ShapeDtypeStruct(weight.shape, jnp.bfloat16),
        ],
        compiler_params=pltpu.CompilerParams(vmem_limit_bytes=58 * 2**20),
        cost_estimate=pl.CostEstimate(
            flops=2 * rows * width * block * count,
            bytes_accessed=8 * rows * block * count,
            transcendentals=0,
        ),
    )(place, factor, momenta, weight)


def adam_update(param, grad, first, second):
    first = BETA_ONE * first + (1.0 - BETA_ONE) * grad
    second = BETA_TWO * second + (1.0 - BETA_TWO) * grad * grad
    denom = jnp.sqrt(second / (1.0 - BETA_TWO**STEP)) + ADAM_EPS
    return (param - BIAS_RATE * (first / (1.0 - BETA_ONE**STEP)) / denom, first, second)


def local(
    token_ids,
    lengths,
    top_ids,
    aux_ids,
    dead_set,
    token_table,
    position_table,
    ln_gains,
    frozen_bias,
    w_qkv,
    w_proj,
    w_fc,
    w_out,
    enc_weight,
    enc_bias,
    dec_weight,
    decoder_bias,
    enc_moment,
    dec_moment,
    encb_first,
    encb_second,
    decb_first,
    decb_second,
):
    chips = lax.axis_size("chip")
    narrow_count = lax.axis_size("narrow")
    wide_count = 2 * chips
    wide = ("chip", "core")
    chip_pos = lax.axis_index("chip")
    core_pos = lax.axis_index("core")
    wide_pos = 2 * chip_pos + core_pos
    narrow_pos = lax.axis_index("narrow")
    row_count = token_ids.shape[0]
    model_width = token_table.shape[1]
    wide_latents = enc_weight.shape[1]
    own_latents = wide_latents // narrow_count
    half_latents = own_latents // 2
    latent_count = chips * own_latents
    core_rows = narrow_count * row_count
    bf16, f32 = jnp.bfloat16, jnp.float32
    to_latents = (((1,), (1,)), ((), ()))
    over_rows = (((0,), (0,)), ((), ()))
    place = jnp.stack([chip_pos, core_pos, narrow_pos]).astype(jnp.int32)
    bits = [1 << bit for bit in range(chips.bit_length() - 1)]
    orders = (bits, bits[::-1])

    tie = lambda *values: lax.optimization_barrier(values)

    def swap(value, axis, offset):
        count = lax.axis_size(axis)
        return lax.ppermute(value, axis, [(spot, spot ^ offset) for spot in range(count)])

    def spread_narrow(value):
        parts = [value] + [swap(value, "narrow", k) for k in range(1, narrow_count)]
        return jnp.concatenate(parts, 0)

    def rows_to_latents(value):
        return lax.all_to_all(value, "narrow", split_axis=1, concat_axis=0, tiled=True)

    def rows_of(value):
        return lax.all_to_all(value, "narrow", split_axis=0, concat_axis=1, tiled=True)

    def gather_start(own, axis):
        halves = []
        for part, order in enumerate(orders):
            held = lax.slice_in_dim(own, part * half_latents, (part + 1) * half_latents, axis=axis)
            for bit in order[:-1]:
                held = jnp.concatenate([held, swap(held, "chip", bit)], axis)
            halves.append(held)
        return halves

    def gather_end(halves):
        pieces = []
        for held, order in zip(halves, orders):
            pieces += [held, swap(held, "chip", order[-1])]
        return pieces

    def scatter_chips(keeps, gots):
        results, sums = [], []
        for order, held, got in zip(orders, keeps, gots):
            held = held + got.astype(f32)
            for bit in reversed(order[:-1]):
                lower, upper = jnp.split(held, 2, 1)
                sent = upper[:model_width].astype(bf16)
                if held.shape[0] > model_width:
                    lines = split_bf(upper[model_width] + upper[model_width + 1])
                    spare = jnp.zeros((14, upper.shape[1]), bf16)
                    sent = jnp.concatenate([sent, *(line[None] for line in lines), spare], 0)
                held = lower + swap(sent, "chip", bit).astype(f32)
            results.append(held[:model_width])
            if held.shape[0] > model_width:
                sums.append(held[model_width] + held[model_width + 1])
        return jnp.concatenate(results, 1), jnp.concatenate(sums) if sums else None

    vocab_dev = token_table.shape[0]
    every_ids = lax.all_gather(token_ids, wide, axis=0, tiled=False).reshape(wide_count, row_count)
    every_ids = jnp.concatenate(
        [
            lax.dynamic_slice_in_dim(every_ids, wide_pos ^ offset, 1, 0)
            for offset in range(wide_count)
        ],
        1,
    )[0]
    local_ids = every_ids - wide_pos * vocab_dev
    inside = (local_ids >= 0) & (local_ids < vocab_dev)
    looked = jnp.take(token_table, jnp.clip(local_ids, 0, vocab_dev - 1), axis=0)
    looked = jnp.where(inside[:, None], looked, jnp.zeros((), bf16))
    dec_weight_t, dec_moment_t = dec_weight.T, dec_moment.T
    rows_each = enc_weight.shape[0]
    enc_own = rows_to_latents(enc_weight.astype(bf16))
    picks = jnp.concatenate([top_ids, aux_ids], 1)
    near_picks = spread_narrow(picks)
    far_picks = swap(near_picks, "core", 1)

    looked = looked.reshape(chips, 2, row_count, model_width)
    looked = looked[:, 0] + swap(looked[:, 1], "core", 1)
    embedded = looked[0].astype(f32)
    for k in range(1, chips):
        embedded = embedded + swap(looked[k], "chip", k).astype(f32)

    bias_rows = jnp.concatenate(
        [enc_bias.astype(bf16)[None], jnp.zeros((15, own_latents), bf16)], 0
    )
    enc_own, embedded = tie(enc_own, embedded)
    dec_cast, enc_own = tie(dec_weight_t.astype(bf16), enc_own)
    dec_own = rows_to_latents(dec_cast)
    enc_halves = gather_start(jnp.concatenate([enc_own, bias_rows], 0), 1)

    dead_here = jnp.stack(
        [
            lax.dynamic_slice_in_dim(
                dead_set,
                (2 * (chip_pos ^ offset) + core_pos) * wide_latents + narrow_pos * own_latents,
                own_latents,
            )
            for offset in range(chips)
        ]
    )
    places = [0]
    dead_parts = []
    for part, order in enumerate(orders):
        places = [0]
        for bit in order:
            places = places + [spot ^ bit for spot in places]
        for spot in places:
            dead_parts.append(dead_here[spot, part * half_latents : (part + 1) * half_latents])
    dead_here = jnp.concatenate(dead_parts)[None]
    sizes = (wide_latents, own_latents, top_ids.shape[1], orders)
    start = embedded + position_table[:row_count].astype(f32)
    ctx_length = lengths[0]
    inputs = frozen_block(start, ctx_length, ln_gains, frozen_bias, w_qkv, w_proj, w_fc, w_out)
    counted = (jnp.arange(row_count) < ctx_length).astype(f32)
    near_picks, inputs, enc_halves = tie(near_picks, inputs, enc_halves)
    enc_parts = gather_end(enc_halves)
    got_inputs = [swap(inputs, "narrow", k) for k in range(1, narrow_count)]
    half_rows = core_rows // 2
    codes = kind_codes(place, near_picks[:half_rows], dead_here, sizes, 0, 4)
    dec_own, codes, got_inputs = tie(dec_own, codes, got_inputs)
    dec_halves = gather_start(dec_own, 1)
    codes = kind_codes(place, near_picks[half_rows:], dead_here, sizes, 1, 4, codes)
    enc_lasts = [enc_parts[1], enc_parts[3]]
    dec_halves, codes, enc_lasts = tie(dec_halves, codes, enc_lasts)
    enc_parts = [enc_parts[0], enc_lasts[0], enc_parts[2], enc_lasts[1]]
    dec_parts = gather_end(dec_halves)
    moments = jnp.concatenate([enc_moment.astype(bf16), dec_moment_t.astype(bf16)], 0)
    moments, got_inputs = tie(moments, got_inputs)
    moments = rows_to_latents(moments)
    near_inputs = jnp.concatenate([inputs, *got_inputs], 0)
    codes = kind_codes(place, far_picks[:half_rows], dead_here, sizes, 2, 4, codes)
    far_inputs, codes = tie(swap(near_inputs, "core", 1), codes)
    codes = kind_codes(place, far_picks[half_rows:], dead_here, sizes, 3, 4, codes)
    all_inputs = jnp.concatenate([near_inputs, far_inputs], 0)
    encoder_in = (all_inputs.astype(f32) - decoder_bias).astype(bf16)
    top_acts, aux_acts, far, near = forward(encoder_in, codes, enc_parts, dec_parts)
    encoder_t = encoder_in.T
    far_got, encoder_t = tie(swap(far, "core", 1), encoder_t)
    rebuilt = near + far_got.astype(f32)
    rounded = rebuilt.astype(bf16)
    rebuilt = rebuilt[:row_count]
    for k in range(1, narrow_count):
        part = rounded[k * row_count : (k + 1) * row_count]
        rebuilt = rebuilt + swap(part, "narrow", k).astype(f32)
    target = inputs.astype(f32)
    reconstructed_input = rebuilt[:, :model_width] + decoder_bias
    auxiliary_reconstruction = rebuilt[:, model_width:]
    recon_error = target - reconstructed_input
    aux_gap = auxiliary_reconstruction - recon_error
    token_loss = (
        counted
        * (jnp.sum(recon_error * recon_error, 1) + AUX_COEF * jnp.sum(aux_gap * aux_gap, 1))
        / model_width
    )
    back_recon = 2.0 / model_width * counted[:, None] * (reconstructed_input - target)
    back_aux = 2.0 * AUX_COEF / model_width * counted[:, None] * aux_gap
    back_rows = jnp.concatenate([back_recon, back_aux], 1).astype(bf16)
    back_rows, moments = tie(back_rows, moments)
    near_back = spread_narrow(back_rows)
    shard_rows = jnp.concatenate([near_back, swap(near_back, "core", 1)], 0)
    back_t = shard_rows.T
    dec_sent = dec_grads(back_t, top_acts, aux_acts, (1, 3), bf16)
    moments = moments.reshape(narrow_count, 2, rows_each, own_latents)
    enc_moment_own = moments[:, 0].reshape(model_width, own_latents)
    dec_moment_own = moments[:, 1].reshape(model_width, own_latents)
    top_acts, dec_sent = tie(top_acts, dec_sent)
    dec_keep = dec_grads(back_t, top_acts, aux_acts, (0, 2), f32)
    shard_rows, dec_keep = tie(shard_rows, dec_keep)
    enc_sent = enc_grads(encoder_t, shard_rows, codes, dec_parts[1::2], (1, 3), bf16)
    shard_rows, enc_sent = tie(shard_rows, enc_sent)
    enc_keep = enc_grads(encoder_t, shard_rows, codes, dec_parts[::2], (0, 2), f32)
    dec_gots = [swap(sent, "chip", order[-1]) for order, sent in zip(orders, dec_sent)]
    dec_gots, enc_sent = tie(dec_gots, enc_sent)
    enc_gots = [swap(sent, "chip", order[-1]) for order, sent in zip(orders, enc_sent)]
    dec_grad, _ = scatter_chips(dec_keep, dec_gots)
    def sum_gram(part, vector, fill):
        half = model_width // 2
        rows = half // chips
        spare = jnp.zeros((14, model_width), bf16)

        def pack(block, vector):
            lines = [line[None] for line in split_bf(vector)]
            return jnp.concatenate([block.astype(bf16), *lines, spare], 0)

        def unpack(got):
            got = got.astype(f32)
            return got[:-16], got[-16] + got[-15]

        def block_of(value, index, count):
            return lax.dynamic_slice_in_dim(value, index * count, count, 0)

        def exchange(sents, axis):
            got = [swap(sent, axis, k + 1) for k, sent in enumerate(sents)]
            return fill(sents, got)

        sent = pack(block_of(part, 1 - core_pos, half), vector)
        (got,) = exchange([sent], "core")
        got, more = unpack(got)
        part, vector = block_of(part, core_pos, half) + got, vector + more
        total = block_of(part, chip_pos, rows)
        sents = [pack(block_of(part, chip_pos ^ k, rows), vector) for k in range(1, chips)]
        for got in exchange(sents, "chip"):
            got, more = unpack(got)
            total, vector = total + got, vector + more
        for got in exchange([pack(total, vector)] * (narrow_count - 1), "narrow"):
            got, more = unpack(got)
            total, vector = total + got, vector + more
        total = total.astype(bf16)
        near = jnp.stack([total, *exchange([total] * (chips - 1), "chip")])
        (far,) = exchange([near], "core")
        return near, far, vector

    dec_own_next = (MOMENTUM * dec_moment_own.astype(f32) + dec_grad).astype(bf16)
    dec_rows, dec_own_next = tie(dec_grad.astype(bf16), dec_own_next)
    dec_rows = rows_of(dec_rows)
    dec_gram = lax.dot_general(
        dec_own_next, dec_own_next, to_latents, preferred_element_type=f32
    )
    dec_gram, enc_gots, enc_keep = tie(dec_gram, enc_gots, enc_keep)
    stages = []
    enc_grad = encb_grad = None

    def dec_note(sents, got):
        nonlocal enc_grad, encb_grad, dec_rows
        if not stages:
            enc_grad, encb_grad = scatter_chips(enc_keep, enc_gots)
        if len(stages) == 2:
            got, enc_grad, dec_rows = tie(got, enc_grad, dec_rows)
        stages.append(got)
        return got

    dec_near, dec_far, _ = sum_gram(
        dec_gram,
        jnp.zeros((model_width,), f32),
        dec_note,
    )
    bias_term = jnp.sum(back_rows[:, :model_width], 0, dtype=f32) - jnp.dot(
        enc_own.astype(f32),
        encb_grad,
        precision=HIGH_PRECISION,
    )

    enc_own_next = (MOMENTUM * enc_moment_own.astype(f32) + enc_grad).astype(bf16)
    enc_gram = lax.dot_general(
        enc_own_next, enc_own_next, to_latents, preferred_element_type=f32
    )
    enc_gram, dec_near = lax.optimization_barrier((enc_gram, dec_near))
    enc_momenta = lax.all_gather(enc_own_next, "narrow")
    progress = []

    def dec_fill(sents, got):
        step = len(progress)
        if step == 0:
            early, _ = tie(dec_near, sents)
            state = series_start(place, early, dec_far)
        else:
            state = series_next(step, progress[-1])
        got, state = lax.optimization_barrier((got, state))
        progress.append(state)
        return got

    enc_near, enc_far, grad_decb = sum_gram(enc_gram, bias_term, dec_fill)
    dec_factor = progress[-1][0]
    dec_ortho = rows_of(
        jnp.dot(dec_factor, dec_own_next, preferred_element_type=f32).astype(bf16)
    )
    step_scale = MUON_RATE * 0.2 * math.sqrt(max(D, L))
    dec_next = MOMENTUM * dec_moment_t + dec_rows.astype(f32)
    dec_new = dec_weight_t * (1.0 - MUON_RATE * DECAY) - step_scale * dec_ortho.astype(f32)
    dec_copy = dec_new.astype(bf16)
    state = series_start(place, enc_near, enc_far)
    for step in range(1, NS_STEPS):
        state = series_next(step, state)
    enc_new, enc_next, enc_copy = finish(place, state[0], enc_momenta, enc_weight)
    encb_new, encb_one, encb_two = adam_update(enc_bias, encb_grad, encb_first, encb_second)
    decb_new, decb_one, decb_two = adam_update(decoder_bias, grad_decb, decb_first, decb_second)
    return (
        token_loss,
        enc_new,
        enc_next,
        enc_copy,
        dec_new.T,
        dec_next.T,
        dec_copy.T,
        encb_new,
        encb_one,
        encb_two,
        decb_new,
        decb_one,
        decb_two,
    )


def solution(mesh):
    wide, narrow = mesh.devices.shape
    fine = Mesh(mesh.devices.reshape(wide // 2, 2, narrow), ("chip", "core", "narrow"))
    placed = (
        P(("chip", "core", "narrow")),
        P(("chip", "core", "narrow")),
        P(("chip", "core", "narrow"), None),
        P(("chip", "core", "narrow"), None),
        P(),
        P(("chip", "core"), None),
        P(),
        P(),
        P(),
        P(),
        P(),
        P(),
        P(),
        P("narrow", ("chip", "core")),
        P(("chip", "core", "narrow")),
        P(("chip", "core"), "narrow"),
        P(),
        P("narrow", ("chip", "core")),
        P(("chip", "core"), "narrow"),
        P(("chip", "core", "narrow")),
        P(("chip", "core", "narrow")),
        P(),
        P(),
    )
    return jax.shard_map(
        local,
        mesh=fine,
        in_specs=placed,
        out_specs=(
            P(("chip", "core", "narrow")),
            P("narrow", ("chip", "core")),
            P("narrow", ("chip", "core")),
            P("narrow", ("chip", "core")),
            P(("chip", "core"), "narrow"),
            P(("chip", "core"), "narrow"),
            P(("chip", "core"), "narrow"),
            P(("chip", "core", "narrow")),
            P(("chip", "core", "narrow")),
            P(("chip", "core", "narrow")),
            P(),
            P(),
            P(),
        ),
        check_vma=False,
    )
```

```python
import functools
import math

import jax
import jax.numpy as jnp
from jax import lax
from jax.experimental import pallas as pl
from jax.experimental.pallas import tpu as pltpu
from jax.sharding import Mesh
from jax.sharding import PartitionSpec as P

D = 768
HEAD_DIM = 64
L = 32768
NS_STEPS = 5
STEP = 10


HIGH_PRECISION = lax.Precision.HIGHEST
AUX_COEF = 1.0 / 32.0
EPS_NORM = 1e-05
NS_EPS = 1e-07
QA = 3.4445
QB = -4.775
QC = 2.0315
MOMENTUM = 0.95
MUON_RATE = 0.1
DECAY = 0.1
BIAS_RATE = 0.3
BETA_ONE = 0.9
BETA_TWO = 0.999
ADAM_EPS = 1e-08


def layer_norm(value, gain, shift):
    row_mean = jnp.mean(value, -1, keepdims=True)
    centred = value - row_mean
    row_var = jnp.mean(centred * centred, -1, keepdims=True)
    return centred * lax.rsqrt(row_var + EPS_NORM) * gain + shift


def frozen_block(start, ctx_length, ln_gains, frozen_bias, w_qkv, w_proj, w_fc, w_out):
    row_count, model_width = start.shape
    head_count = model_width // HEAD_DIM
    ff_width = w_fc.shape[1]
    shifts = frozen_bias[: 2 * model_width].reshape(2, model_width)
    b_qkv = frozen_bias[2 * model_width : 5 * model_width]
    b_proj = frozen_bias[5 * model_width : 6 * model_width]
    b_fc = frozen_bias[6 * model_width : 6 * model_width + ff_width]
    b_out = frozen_bias[6 * model_width + ff_width :]
    normed = layer_norm(start, ln_gains[0], shifts[0]).astype(jnp.bfloat16)
    qkv_rows = (jnp.dot(normed, w_qkv, preferred_element_type=jnp.float32) + b_qkv).astype(
        jnp.bfloat16
    )
    head_split = qkv_rows.reshape(row_count, 3, head_count, HEAD_DIM)
    scores = jnp.einsum(
        "qhd,khd->hqk", head_split[:, 0], head_split[:, 1], preferred_element_type=jnp.float32
    ) * HEAD_DIM ** (-0.5)
    positions = jnp.arange(row_count)
    allowed = (positions[None, :] <= positions[:, None]) & (positions[None, :] < ctx_length)
    attn_probs = jax.nn.softmax(jnp.where(allowed[None], scores, -1e30), axis=-1).astype(
        jnp.bfloat16
    )
    mixed = jnp.einsum(
        "hqk,khd->qhd", attn_probs, head_split[:, 2], preferred_element_type=jnp.float32
    )
    mixed = mixed.reshape(row_count, model_width).astype(jnp.bfloat16)
    hidden = start + jnp.dot(mixed, w_proj, preferred_element_type=jnp.float32) + b_proj
    normed_two = layer_norm(hidden, ln_gains[1], shifts[1]).astype(jnp.bfloat16)
    inner_acts = jax.nn.gelu(
        jnp.dot(normed_two, w_fc, preferred_element_type=jnp.float32) + b_fc, approximate=True
    ).astype(jnp.bfloat16)
    return (hidden + jnp.dot(inner_acts, w_out, preferred_element_type=jnp.float32) + b_out).astype(
        jnp.bfloat16
    )


def split_bf(value):
    high = value.astype(jnp.bfloat16)
    return high, (value - high.astype(jnp.float32)).astype(jnp.bfloat16)


def row_blocks(size, body):
    block = 256

    def step(index, carry):
        body(pl.ds(pl.multiple_of(index * block, block), block), index * block)
        return carry

    lax.fori_loop(0, size // block, step, 0)


def eye_rows(start, size):
    rows = lax.broadcasted_iota(jnp.int32, (256, size), 0) + start
    cols = lax.broadcasted_iota(jnp.int32, (256, size), 1)
    return (rows == cols).astype(jnp.float32)


def dot_f32(a, b):
    return jnp.dot(a, b, preferred_element_type=jnp.float32)


def store_split(pair, rows, value):
    pair[0][rows, :], pair[1][rows, :] = split_bf(value)


def three(left, right, rows):
    high, low = left[0][rows, :], left[1][rows, :]
    return dot_f32(high, right[0][...]) + (
        dot_f32(high, right[1][...]) + dot_f32(low, right[0][...])
    )


def series_step(gram, poly, half, out, old, new, step):
    size = gram[0].shape[0]
    last = step == NS_STEPS - 1
    exact_square = step >= 3

    def poly_rows(rows, start):
        here = gram[0][rows, :].astype(jnp.float32) + gram[1][rows, :].astype(jnp.float32)
        if exact_square:
            square = three(gram, gram, rows)
        else:
            square = dot_f32(gram[0][rows, :], gram[0][...])
        store_split(poly, rows, QA * eye_rows(start, size) + QB * here + QC * square)

    def half_rows(rows, start):
        store_split(half, rows, three(gram, poly, rows))

    def gram_rows(rows, start):
        store_split(out, rows, three(poly, half, rows))

    def product_rows(rows, start):
        new[rows, :] = dot_f32(poly[0][rows, :], old[...]).astype(jnp.bfloat16)

    row_blocks(size, poly_rows)
    if not last:
        row_blocks(size, half_rows)
        row_blocks(size, gram_rows)
    if step > 0:
        row_blocks(size, product_rows)


def first_kernel(place_ref, near_ref, far_ref, o_hi, o_lo, q_ref, total, *scratch):
    size = total.shape[0]
    chips, rows_each = near_ref.shape[:2]
    chip, core = place_ref[0], place_ref[1]
    gram, poly, half = scratch[:2], scratch[2:4], scratch[4:6]
    for offset in range(chips):
        for side, source in enumerate((near_ref, far_ref)):
            first = jnp.bitwise_xor(core, side) * (size // 2)
            first = first + jnp.bitwise_xor(chip, offset) * rows_each
            total[pl.ds(pl.multiple_of(first, 8), rows_each), :] = source[offset].astype(
                jnp.float32
            )

    def trace_part(index, value):
        start = pl.multiple_of(index * 256, 256)
        return value + jnp.sum(total[pl.ds(start, 256), :] * eye_rows(start, size))

    trace_sum = lax.fori_loop(0, size // 256, trace_part, jnp.zeros((), jnp.float32))
    scale = 1.0 / (jnp.sqrt(jnp.full((1, 1), trace_sum)) + NS_EPS)

    def load_rows(rows, start):
        store_split(gram, rows, total[rows, :] * (scale * scale))

    row_blocks(size, load_rows)
    series_step(gram, poly, half, (o_hi, o_lo), None, None, 0)

    def product_rows(rows, start):
        value = poly[0][rows, :].astype(jnp.float32) + poly[1][rows, :].astype(jnp.float32)
        q_ref[rows, :] = (value * scale).astype(jnp.bfloat16)

    row_blocks(size, product_rows)


def middle_kernel(step, g_hi, g_lo, q_ref, o_hi, o_lo, out_ref, *scratch):
    series_step(
        (g_hi, g_lo), scratch[:2], scratch[2:4], (o_hi, o_lo), q_ref, out_ref, step
    )


def last_kernel(g_hi, g_lo, q_ref, out_ref, *scratch):
    series_step((g_hi, g_lo), scratch[:2], None, None, q_ref, out_ref, NS_STEPS - 1)


def square_call(kernel, outs, scratch, passes, *operands):
    size = operands[-1].shape[-1]
    whole = pl.BlockSpec(memory_space=pltpu.VMEM)
    specs = [whole] * len(operands)
    if operands[0].ndim == 1:
        specs[0] = pl.BlockSpec(memory_space=pltpu.SMEM)
    square = jax.ShapeDtypeStruct((size, size), jnp.bfloat16)
    return pl.pallas_call(
        kernel,
        out_shape=[square] * outs,
        in_specs=specs,
        out_specs=[whole] * outs,
        scratch_shapes=[pltpu.VMEM((size, size), kind) for kind in scratch],
        compiler_params=pltpu.CompilerParams(vmem_limit_bytes=40 * 2**20),
        cost_estimate=pl.CostEstimate(
            flops=passes * size**3 // 16, bytes_accessed=size * size // 2, transcendentals=0
        ),
    )(*operands)


def series_start(place, near, far):
    bf16 = jnp.bfloat16
    return square_call(first_kernel, 3, [jnp.float32] + [bf16] * 6, 8, place, near, far)


def series_next(step, state):
    bf16 = jnp.bfloat16
    if step == NS_STEPS - 1:
        return square_call(last_kernel, 1, [bf16] * 2, 4, *state)
    kernel = functools.partial(middle_kernel, step)
    return square_call(kernel, 3, [bf16] * 4, 8 if step < 3 else 10, *state)


def code_kernel(shifts, place_ref, ids_ref, out_ref, high, low, stage):
    wide_shift, own_shift, top_count, orders = shifts
    batch, groups = stage.shape[:2]
    rows, picks = ids_ref.shape
    bf16, f32 = jnp.bfloat16, jnp.float32
    chip, core, narrow = place_ref[0], place_ref[1], place_ref[2]
    latent_count = out_ref.shape[1]
    half_shift = own_shift - 1

    ids = ids_ref[...]
    owner = lax.shift_right_logical(ids, wide_shift)
    within = jnp.bitwise_and(ids, (1 << wide_shift) - 1)
    mine = (lax.shift_right_logical(within, own_shift) == narrow) & (
        jnp.bitwise_and(owner, 1) == core
    )
    inner = jnp.bitwise_and(within, (1 << own_shift) - 1)
    offset = jnp.bitwise_xor(lax.shift_right_logical(owner, 1), chip)
    half = lax.shift_right_logical(inner, half_shift)
    spots = []
    for order in orders:
        spot = jnp.zeros_like(offset)
        for index, bit in enumerate(order[:-1]):
            spot = spot + jnp.where(jnp.bitwise_and(offset, bit) != 0, 1 << index, 0)
        sent = jnp.where(jnp.bitwise_and(offset, order[-1]) != 0, latent_count // 4, 0)
        spots.append(sent + lax.shift_left(spot, half_shift))
    column = (
        half * (latent_count // 2)
        + jnp.where(half == 0, spots[0], spots[1])
        + jnp.bitwise_and(inner, (1 << half_shift) - 1)
    )
    high[...] = jnp.where(mine, lax.shift_right_logical(column, 7), -1).astype(f32)
    low[...] = jnp.bitwise_and(column, 127).astype(f32)

    one, zero = jnp.ones((16, picks), bf16), jnp.zeros((16, picks), bf16)
    places = lax.broadcasted_iota(jnp.int32, (16, picks), 1)
    kinds = jnp.where(places < top_count, 1.0, 2.0).astype(bf16)
    steps = lax.broadcasted_iota(jnp.int32, (16, picks), 0).astype(f32).astype(bf16)

    def hot(row, count, value):
        row = jnp.broadcast_to(row, (16, picks)).astype(bf16)
        parts = [
            jnp.where(steps + jnp.asarray(16 * part, bf16) == row, value, zero)
            for part in range(max(1, count // 16))
        ]
        return jnp.concatenate(parts, 0).astype(jnp.float8_e4m3fn)

    def one_batch(index, carry):
        first = pl.multiple_of(index * batch, batch)
        for token in range(batch):
            row = pl.ds(first + token, 1)
            codes = lax.dot_general(
                hot(high[row, :], groups, kinds),
                hot(low[row, :], 128, one),
                (((1,), (1,)), ((), ())),
                preferred_element_type=f32,
            )
            stage[token] = codes[:groups]
        for group in range(groups):
            lanes = slice(group * 128, (group + 1) * 128)
            out_ref[pl.ds(first, batch), lanes] = stage[:, group, :].astype(bf16)
        return carry

    lax.fori_loop(0, rows // batch, one_batch, 0)


def kind_codes(place, ids, latent_count, sizes):
    wide_latents, own_latents, top_count, orders = sizes
    row_total, pick_total = ids.shape
    rows = min(128, row_total)
    shifts = (wide_latents.bit_length() - 1, own_latents.bit_length() - 1, top_count, orders)
    return pl.pallas_call(
        functools.partial(code_kernel, shifts),
        grid=(row_total // rows,),
        out_shape=jax.ShapeDtypeStruct((row_total, latent_count), jnp.bfloat16),
        in_specs=[
            pl.BlockSpec(memory_space=pltpu.SMEM),
            pl.BlockSpec((rows, pick_total), lambda i: (i, 0)),
        ],
        out_specs=pl.BlockSpec((rows, latent_count), lambda i: (i, 0)),
        scratch_shapes=[
            pltpu.VMEM((rows, pick_total), jnp.float32),
            pltpu.VMEM((rows, pick_total), jnp.float32),
            pltpu.VMEM((32, latent_count // 128, 128), jnp.float32),
        ],
        compiler_params=pltpu.CompilerParams(vmem_limit_bytes=40 * 2**20),
        cost_estimate=pl.CostEstimate(
            flops=row_total * latent_count,
            bytes_accessed=row_total * pick_total,
            transcendentals=0,
        ),
    )(place, ids)


def join_rows(sources, target):
    rows = sources[0].shape[0]
    for index, source in enumerate(sources):
        target[index * rows : (index + 1) * rows, :] = source[...]


def pick_copy(step, count, sources, target):
    for index, source in enumerate(sources):

        @pl.when(step // count == index)
        def _(source=source):
            target[...] = source[...]


def forward_kernel(count, x_ref, dead_ref, *refs):
    code_parts, encs, decs = refs[:4], refs[4:8], refs[8:12]
    top_ref, aux_ref, far_ref, near_ref = refs[12:16]
    codes_ref, enc, dec, acc_top, acc_aux = refs[16:]
    join_rows(code_parts, codes_ref)
    step = pl.program_id(0)
    rows_all, width = x_ref.shape
    block = min(1024, rows_all)
    pick_copy(step, count, encs, enc)
    pick_copy(step, count, decs, dec)

    @pl.when(step == 0)
    def _():
        acc_top[...] = jnp.zeros_like(acc_top)
        acc_aux[...] = jnp.zeros_like(acc_aux)

    bias = enc[pl.ds(width, 16), :].astype(jnp.float32)[:1]
    to_features = (((1,), (1,)), ((), ()))

    def one(index, carry):
        rows = pl.ds(pl.multiple_of(index * block, block), block)
        pre = dot_f32(x_ref[rows, :], enc[pl.ds(0, width), :]) + bias
        codes = codes_ref[rows, :]
        zero = jnp.zeros(codes.shape, jnp.bfloat16)
        top = jnp.where(codes == 1.0, pre.astype(jnp.bfloat16), zero)
        aux = jnp.where(codes == 2.0, (pre * dead_ref[...]).astype(jnp.bfloat16), zero)
        top_ref[rows, :] = top
        aux_ref[rows, :] = aux
        acc_top[rows, :] += lax.dot_general(
            top, dec[...], to_features, preferred_element_type=jnp.float32
        )
        acc_aux[rows, :] += lax.dot_general(
            aux, dec[...], to_features, preferred_element_type=jnp.float32
        )
        return carry

    lax.fori_loop(0, rows_all // block, one, 0)

    @pl.when(step == pl.num_programs(0) - 1)
    def _():
        half = rows_all // 2
        for first, acc in ((0, acc_top), (width, acc_aux)):
            near_ref[:, first : first + width] = acc[pl.ds(0, half), :]
            far_ref[:, first : first + width] = acc[pl.ds(half, half), :].astype(jnp.bfloat16)


def part_specs(shape, axis, block, count, starts):
    specs = []
    for index, first in enumerate(starts):

        def place(step, index=index, first=first):
            spot = jnp.clip(step - index * count, 0, count - 1)
            return (spot + first, 0) if axis == 0 else (0, spot + first)

        size = (block, shape[1]) if axis == 0 else (shape[0], block)
        specs.append(pl.BlockSpec(size, place))
    return specs


def forward(x, codes, dead, encs, decs):
    rows, width = x.shape
    acts_shape = (rows, dead.shape[1])
    quarter = encs[0].shape[1]
    block = min(512, quarter)
    count = quarter // block
    lanes = pl.BlockSpec((rows, block), lambda step: (0, step))
    fixed = lambda shape: pl.BlockSpec(shape, lambda step: (0, 0))
    bf16, f32 = jnp.bfloat16, jnp.float32
    half_shape = (rows // 2, 2 * width)
    return pl.pallas_call(
        functools.partial(forward_kernel, count),
        grid=(4 * count,),
        out_shape=[
            jax.ShapeDtypeStruct(acts_shape, bf16),
            jax.ShapeDtypeStruct(acts_shape, bf16),
            jax.ShapeDtypeStruct(half_shape, bf16),
            jax.ShapeDtypeStruct(half_shape, f32),
        ],
        in_specs=[fixed(x.shape), pl.BlockSpec((1, block), lambda step: (0, step))]
        + [pl.BlockSpec((rows // 4, block), lambda step: (0, step))] * 4
        + part_specs(encs[0].shape, 1, block, count, (0, 0, 0, 0))
        + part_specs(decs[0].shape, 1, block, count, (0, 0, 0, 0)),
        out_specs=[lanes, lanes, fixed(half_shape), fixed(half_shape)],
        scratch_shapes=[
            pltpu.VMEM((rows, block), bf16),
            pltpu.VMEM((width + 16, block), bf16),
            pltpu.VMEM((width, block), bf16),
            pltpu.VMEM((rows, width), f32),
            pltpu.VMEM((rows, width), f32),
        ],
        compiler_params=pltpu.CompilerParams(vmem_limit_bytes=58 * 2**20),
        cost_estimate=pl.CostEstimate(
            flops=2 * rows * width * dead.shape[1],
            bytes_accessed=6 * rows * dead.shape[1],
            transcendentals=0,
        ),
    )(x, dead, *codes, *encs, *decs)


def store_part(count, refs, rows, value):
    step = pl.program_id(0)
    for index, ref in enumerate(refs):

        @pl.when(step // count == index)
        def _(ref=ref):
            ref[rows, :] = value.astype(ref.dtype)


def dec_grad_kernel(count, near_r, near_a, far_r, far_a, top_ref, aux_ref, *outs):
    half = near_r.shape[1]

    def one(index, carry):
        rows = pl.ds(pl.multiple_of(index * 384, 384), 384)
        value = dot_f32(near_r[rows, :], top_ref[:half, :])
        value = value + dot_f32(near_a[rows, :], aux_ref[:half, :])
        value = value + dot_f32(far_r[rows, :], top_ref[half:, :])
        value = value + dot_f32(far_a[rows, :], aux_ref[half:, :])
        store_part(count, outs, rows, value)
        return carry

    lax.fori_loop(0, near_r.shape[0] // 384, one, 0)


def dec_grads(near_t, far_t, top_acts, aux_acts, quarters, kind):
    width = near_t.shape[0] // 2
    rows, latents = top_acts.shape
    quarter = latents // 4
    block = min(512, quarter)
    count = quarter // block

    def lanes(step):
        return (0, jnp.where(step < count, quarters[0], quarters[1] - 1) * count + step)

    acts = pl.BlockSpec((rows, block), lanes)
    shape = (width, quarter)
    return pl.pallas_call(
        functools.partial(dec_grad_kernel, count),
        grid=(2 * count,),
        out_shape=[jax.ShapeDtypeStruct(shape, kind)] * 2,
        in_specs=[
            pl.BlockSpec((width, rows // 2), lambda step: (0, 0)),
            pl.BlockSpec((width, rows // 2), lambda step: (1, 0)),
            pl.BlockSpec((width, rows // 2), lambda step: (0, 0)),
            pl.BlockSpec((width, rows // 2), lambda step: (1, 0)),
            acts,
            acts,
        ],
        out_specs=part_specs(shape, 1, block, count, (0, 0)),
        compiler_params=pltpu.CompilerParams(vmem_limit_bytes=58 * 2**20),
        cost_estimate=pl.CostEstimate(
            flops=rows * width * quarter // 8, bytes_accessed=rows * quarter // 4, transcendentals=0
        ),
    )(near_t, near_t, far_t, far_t, top_acts, aux_acts)


def enc_grad_kernel(count, x_ref, near_ref, far_ref, dead_ref, *refs):
    code_parts, (dec_a, dec_b, out_a, out_b, dec, grads) = refs[:4], refs[4:]
    step = pl.program_id(0)
    pick_copy(step, count, (dec_a, dec_b), dec)
    width, latents = dec.shape
    quarter = code_parts[0].shape[0]
    total = jnp.zeros((1, latents), jnp.float32)
    for index, back_ref in enumerate((near_ref, far_ref)):
        top = dot_f32(back_ref[:, :width], dec[...])
        aux = dot_f32(back_ref[:, width:], dec[...]) * dead_ref[...]
        for part in range(2):
            codes = code_parts[2 * index + part][...].astype(jnp.float32)
            lines = slice(part * quarter, (part + 1) * quarter)
            value = jnp.where(codes == 2.0, aux[lines], 0.0)
            value = jnp.where(codes == 1.0, top[lines], value).astype(jnp.bfloat16)
            first = (2 * index + part) * quarter
            grads[first : first + quarter, :] = value
            total = total + jnp.sum(value.astype(jnp.float32), 0, keepdims=True)

    def two(index, carry):
        rows = pl.ds(pl.multiple_of(index * 384, 384), 384)
        store_part(count, (out_a, out_b), rows, dot_f32(x_ref[rows, :], grads[...]))
        return carry

    lax.fori_loop(0, width // 384, two, 0)
    lines = lax.broadcasted_iota(jnp.int32, (16, latents), 0)
    if out_a.dtype == jnp.bfloat16:
        high = total.astype(jnp.bfloat16).astype(jnp.float32)
        lines = jnp.where(lines == 0, high, jnp.where(lines == 1, total - high, 0.0))
    else:
        lines = jnp.where(lines == 0, total, 0.0)
    store_part(count, (out_a, out_b), pl.ds(width, 16), lines)


def enc_grads(x_t, near, far, codes, dead, parts, quarters, kind):
    width, rows = x_t.shape
    quarter = dead.shape[1] // 4
    block = min(512, quarter)
    count = quarter // block

    def lanes(step):
        return (0, jnp.where(step < count, quarters[0], quarters[1] - 1) * count + step)

    shape = (width + 16, quarter)
    return pl.pallas_call(
        functools.partial(enc_grad_kernel, count),
        grid=(2 * count,),
        out_shape=[jax.ShapeDtypeStruct(shape, kind)] * 2,
        in_specs=[
            pl.BlockSpec(x_t.shape, lambda step: (0, 0)),
            pl.BlockSpec(near.shape, lambda step: (0, 0)),
            pl.BlockSpec(far.shape, lambda step: (0, 0)),
            pl.BlockSpec((1, block), lanes),
        ]
        + [pl.BlockSpec((rows // 4, block), lanes)] * 4
        + part_specs(parts[0].shape, 1, block, count, (0, 0)),
        out_specs=part_specs(shape, 1, block, count, (0, 0)),
        scratch_shapes=[
            pltpu.VMEM((width, block), jnp.bfloat16),
            pltpu.VMEM((rows, block), jnp.bfloat16),
        ],
        compiler_params=pltpu.CompilerParams(vmem_limit_bytes=58 * 2**20),
        cost_estimate=pl.CostEstimate(
            flops=rows * width * quarter // 8, bytes_accessed=rows * quarter // 4, transcendentals=0
        ),
    )(x_t, near, far, dead, *codes, *parts)


def finish_kernel(place_ref, factor_ref, momentum_ref, weight_ref, *outs):
    new_ref, next_ref, copy_ref = outs
    rows = factor_ref.shape[0]
    f32 = jnp.float32
    momentum = momentum_ref[0]
    kept = momentum_ref[0, pl.ds(pl.multiple_of(place_ref[2] * rows, 16), rows), :].astype(f32)
    ortho = dot_f32(factor_ref[...], momentum)
    next_ref[...] = kept
    step_scale = MUON_RATE * 0.2 * math.sqrt(max(D, L))
    value = weight_ref[...] * (1.0 - MUON_RATE * DECAY) - step_scale * ortho
    new_ref[...] = value
    copy_ref[...] = value.astype(jnp.bfloat16)


def finish(place, factor, momenta, weight):
    count, width, block = momenta.shape
    rows = weight.shape[0]
    part = pl.BlockSpec((rows, block), lambda step, place: (0, step))
    return pl.pallas_call(
        finish_kernel,
        grid_spec=pltpu.PrefetchScalarGridSpec(
            num_scalar_prefetch=1,
            grid=(count,),
            in_specs=[
                pl.BlockSpec((rows, width), lambda step, place: (place[2], 0)),
                pl.BlockSpec((1, width, block), lambda step, place: (step, 0, 0)),
                part,
            ],
            out_specs=[part] * 3,
        ),
        out_shape=[
            jax.ShapeDtypeStruct(weight.shape, jnp.float32),
            jax.ShapeDtypeStruct(weight.shape, jnp.float32),
            jax.ShapeDtypeStruct(weight.shape, jnp.bfloat16),
        ],
        compiler_params=pltpu.CompilerParams(vmem_limit_bytes=58 * 2**20),
        cost_estimate=pl.CostEstimate(
            flops=2 * rows * width * block * count,
            bytes_accessed=8 * rows * block * count,
            transcendentals=0,
        ),
    )(place, factor, momenta, weight)


def adam_update(param, grad, first, second):
    first = BETA_ONE * first + (1.0 - BETA_ONE) * grad
    second = BETA_TWO * second + (1.0 - BETA_TWO) * grad * grad
    denom = jnp.sqrt(second / (1.0 - BETA_TWO**STEP)) + ADAM_EPS
    return (param - BIAS_RATE * (first / (1.0 - BETA_ONE**STEP)) / denom, first, second)


def local(
    token_ids,
    lengths,
    top_ids,
    aux_ids,
    dead_set,
    token_table,
    position_table,
    ln_gains,
    frozen_bias,
    w_qkv,
    w_proj,
    w_fc,
    w_out,
    enc_weight,
    enc_bias,
    dec_weight,
    decoder_bias,
    enc_moment,
    dec_moment,
    encb_first,
    encb_second,
    decb_first,
    decb_second,
):
    chips = lax.axis_size("chip")
    narrow_count = lax.axis_size("narrow")
    wide_count = 2 * chips
    wide = ("chip", "core")
    chip_pos = lax.axis_index("chip")
    core_pos = lax.axis_index("core")
    wide_pos = 2 * chip_pos + core_pos
    narrow_pos = lax.axis_index("narrow")
    row_count = token_ids.shape[0]
    model_width = token_table.shape[1]
    wide_latents = enc_weight.shape[1]
    own_latents = wide_latents // narrow_count
    half_latents = own_latents // 2
    latent_count = chips * own_latents
    core_rows = narrow_count * row_count
    bf16, f32 = jnp.bfloat16, jnp.float32
    to_latents = (((1,), (1,)), ((), ()))
    over_rows = (((0,), (0,)), ((), ()))
    place = jnp.stack([chip_pos, core_pos, narrow_pos]).astype(jnp.int32)
    bits = [1 << bit for bit in range(chips.bit_length() - 1)]
    orders = (bits, bits[::-1])

    tie = lambda *values: lax.optimization_barrier(values)

    def swap(value, axis, offset):
        count = lax.axis_size(axis)
        return lax.ppermute(value, axis, [(spot, spot ^ offset) for spot in range(count)])

    def spread_narrow(value):
        parts = [value] + [swap(value, "narrow", k) for k in range(1, narrow_count)]
        return jnp.concatenate(parts, 0)

    def rows_to_latents(value):
        return lax.all_to_all(value, "narrow", split_axis=1, concat_axis=0, tiled=True)

    def rows_of(value):
        return lax.all_to_all(value, "narrow", split_axis=0, concat_axis=1, tiled=True)

    def gather_start(own, axis):
        halves = []
        for part, order in enumerate(orders):
            held = lax.slice_in_dim(own, part * half_latents, (part + 1) * half_latents, axis=axis)
            for bit in order[:-1]:
                held = jnp.concatenate([held, swap(held, "chip", bit)], axis)
            halves.append(held)
        return halves

    def gather_end(halves):
        pieces = []
        for held, order in zip(halves, orders):
            pieces += [held, swap(held, "chip", order[-1])]
        return pieces

    def scatter_chips(keeps, gots):
        results, sums = [], []
        for order, held, got in zip(orders, keeps, gots):
            held = held + got.astype(f32)
            for bit in reversed(order[:-1]):
                lower, upper = jnp.split(held, 2, 1)
                sent = upper[:model_width].astype(bf16)
                if held.shape[0] > model_width:
                    lines = split_bf(upper[model_width] + upper[model_width + 1])
                    spare = jnp.zeros((14, upper.shape[1]), bf16)
                    sent = jnp.concatenate([sent, *(line[None] for line in lines), spare], 0)
                held = lower + swap(sent, "chip", bit).astype(f32)
            results.append(held[:model_width])
            if held.shape[0] > model_width:
                sums.append(held[model_width] + held[model_width + 1])
        return jnp.concatenate(results, 1), jnp.concatenate(sums) if sums else None

    vocab_dev = token_table.shape[0]
    every_ids = lax.all_gather(token_ids, wide, axis=0, tiled=False).reshape(wide_count, row_count)
    every_ids = jnp.concatenate(
        [
            lax.dynamic_slice_in_dim(every_ids, wide_pos ^ offset, 1, 0)
            for offset in range(wide_count)
        ],
        1,
    )[0]
    local_ids = every_ids - wide_pos * vocab_dev
    inside = (local_ids >= 0) & (local_ids < vocab_dev)
    looked = jnp.take(token_table, jnp.clip(local_ids, 0, vocab_dev - 1), axis=0)
    looked = jnp.where(inside[:, None], looked, jnp.zeros((), bf16))
    dec_weight_t, dec_moment_t = dec_weight.T, dec_moment.T
    rows_each = enc_weight.shape[0]
    enc_own = rows_to_latents(enc_weight.astype(bf16))
    picks = jnp.concatenate([top_ids, aux_ids], 1)
    near_picks = spread_narrow(picks)
    far_picks = swap(near_picks, "core", 1)

    looked = looked.reshape(chips, 2, row_count, model_width)
    looked = looked[:, 0] + swap(looked[:, 1], "core", 1)
    embedded = looked[0].astype(f32)
    for k in range(1, chips):
        embedded = embedded + swap(looked[k], "chip", k).astype(f32)

    bias_rows = jnp.concatenate(
        [enc_bias.astype(bf16)[None], jnp.zeros((15, own_latents), bf16)], 0
    )
    enc_own, embedded = tie(enc_own, embedded)
    dec_cast, enc_own = tie(dec_weight_t.astype(bf16), enc_own)
    dec_own = rows_to_latents(dec_cast)
    enc_halves = gather_start(jnp.concatenate([enc_own, bias_rows], 0), 1)

    dead_here = jnp.stack(
        [
            lax.dynamic_slice_in_dim(
                dead_set,
                (2 * (chip_pos ^ offset) + core_pos) * wide_latents + narrow_pos * own_latents,
                own_latents,
            )
            for offset in range(chips)
        ]
    )
    places = [0]
    dead_parts = []
    for part, order in enumerate(orders):
        places = [0]
        for bit in order:
            places = places + [spot ^ bit for spot in places]
        for spot in places:
            dead_parts.append(dead_here[spot, part * half_latents : (part + 1) * half_latents])
    dead_here = jnp.concatenate(dead_parts)[None].astype(f32)
    sizes = (wide_latents, own_latents, top_ids.shape[1], orders)
    near_picks, dead_here, embedded = tie(near_picks, dead_here, embedded)
    start = embedded + position_table[:row_count].astype(f32)
    ctx_length = lengths[0]
    inputs = frozen_block(start, ctx_length, ln_gains, frozen_bias, w_qkv, w_proj, w_fc, w_out)
    counted = (jnp.arange(row_count) < ctx_length).astype(f32)
    near_picks, inputs, enc_halves = tie(near_picks, inputs, enc_halves)
    enc_parts = gather_end(enc_halves)
    got_inputs = [swap(inputs, "narrow", k) for k in range(1, narrow_count)]
    half_rows = core_rows // 2
    codes = [kind_codes(place, near_picks[:half_rows], latent_count, sizes)]
    enc_lasts = [enc_parts[1], enc_parts[3]]
    dec_own, codes, got_inputs, enc_lasts = tie(dec_own, codes, got_inputs, enc_lasts)
    near_picks, codes = tie(near_picks, codes)
    dec_halves = gather_start(dec_own, 1)
    codes = [*codes, kind_codes(place, near_picks[half_rows:], latent_count, sizes)]
    dec_halves, codes = tie(dec_halves, codes)
    enc_parts = [enc_parts[0], enc_lasts[0], enc_parts[2], enc_lasts[1]]
    dec_parts = gather_end(dec_halves)
    moments = jnp.concatenate([enc_moment.astype(bf16), dec_moment_t.astype(bf16)], 0)
    moments, got_inputs = tie(moments, got_inputs)
    moments = rows_to_latents(moments)
    near_inputs = jnp.concatenate([inputs, *got_inputs], 0)
    far_picks, codes = tie(far_picks, codes)
    codes = [*codes, kind_codes(place, far_picks[:half_rows], latent_count, sizes)]
    far_inputs, codes = tie(swap(near_inputs, "core", 1), codes)
    far_picks, codes = tie(far_picks, codes)
    codes = [*codes, kind_codes(place, far_picks[half_rows:], latent_count, sizes)]
    all_inputs = jnp.concatenate([near_inputs, far_inputs], 0)
    encoder_in = (all_inputs.astype(f32) - decoder_bias).astype(bf16)
    encoder_in, moments = tie(encoder_in, moments)
    top_acts, aux_acts, far, near = forward(encoder_in, codes, dead_here, enc_parts, dec_parts)
    encoder_t = encoder_in.T
    far_got, encoder_t = tie(swap(far, "core", 1), encoder_t)
    rebuilt = near + far_got.astype(f32)
    rounded = rebuilt.astype(bf16)
    rebuilt = rebuilt[:row_count]
    for k in range(1, narrow_count):
        part = rounded[k * row_count : (k + 1) * row_count]
        rebuilt = rebuilt + swap(part, "narrow", k).astype(f32)
    target = inputs.astype(f32)
    reconstructed_input = rebuilt[:, :model_width] + decoder_bias
    auxiliary_reconstruction = rebuilt[:, model_width:]
    recon_error = target - reconstructed_input
    aux_gap = auxiliary_reconstruction - recon_error
    token_loss = (
        counted
        * (jnp.sum(recon_error * recon_error, 1) + AUX_COEF * jnp.sum(aux_gap * aux_gap, 1))
        / model_width
    )
    back_recon = 2.0 / model_width * counted[:, None] * (reconstructed_input - target)
    back_aux = 2.0 * AUX_COEF / model_width * counted[:, None] * aux_gap
    back_rows = jnp.concatenate([back_recon, back_aux], 1).astype(bf16)
    near_back = spread_narrow(back_rows)
    far_back = swap(near_back, "core", 1)
    near_t, far_back = tie(near_back.T, far_back)
    far_t = far_back.T
    dec_sent = dec_grads(near_t, far_t, top_acts, aux_acts, (1, 3), bf16)
    moments = moments.reshape(narrow_count, 2, rows_each, own_latents)
    enc_moment_own = moments[:, 0].reshape(model_width, own_latents)
    dec_moment_own = moments[:, 1].reshape(model_width, own_latents)
    top_acts, dec_sent = tie(top_acts, dec_sent)
    dec_keep = dec_grads(near_t, far_t, top_acts, aux_acts, (0, 2), f32)
    far_back, dec_keep = tie(far_back, dec_keep)
    enc_sent = enc_grads(
        encoder_t, near_back, far_back, codes, dead_here, dec_parts[1::2], (1, 3), bf16
    )
    far_back, enc_sent = tie(far_back, enc_sent)
    enc_keep = enc_grads(
        encoder_t, near_back, far_back, codes, dead_here, dec_parts[::2], (0, 2), f32
    )
    dec_gots = [swap(sent, "chip", order[-1]) for order, sent in zip(orders, dec_sent)]
    dec_gots, enc_sent = tie(dec_gots, enc_sent)
    enc_gots = [swap(sent, "chip", order[-1]) for order, sent in zip(orders, enc_sent)]
    dec_grad, _ = scatter_chips(dec_keep, dec_gots)
    def sum_gram(part, vector, fill):
        half = model_width // 2
        rows = half // chips
        spare = jnp.zeros((14, model_width), bf16)

        def pack(block, vector):
            lines = [line[None] for line in split_bf(vector)]
            return jnp.concatenate([block.astype(bf16), *lines, spare], 0)

        def unpack(got):
            got = got.astype(f32)
            return got[:-16], got[-16] + got[-15]

        def block_of(value, index, count):
            return lax.dynamic_slice_in_dim(value, index * count, count, 0)

        def exchange(sents, axis):
            got = [swap(sent, axis, k + 1) for k, sent in enumerate(sents)]
            return fill(sents, got)

        sent = pack(block_of(part, 1 - core_pos, half), vector)
        (got,) = exchange([sent], "core")
        got, more = unpack(got)
        part, vector = block_of(part, core_pos, half) + got, vector + more
        total = block_of(part, chip_pos, rows)
        sents = [pack(block_of(part, chip_pos ^ k, rows), vector) for k in range(1, chips)]
        for got in exchange(sents, "chip"):
            got, more = unpack(got)
            total, vector = total + got, vector + more
        for got in exchange([pack(total, vector)] * (narrow_count - 1), "narrow"):
            got, more = unpack(got)
            total, vector = total + got, vector + more
        total = total.astype(bf16)
        near = jnp.stack([total, *exchange([total] * (chips - 1), "chip")])
        (far,) = exchange([near], "core")
        return near, far, vector

    dec_own_next = (MOMENTUM * dec_moment_own.astype(f32) + dec_grad).astype(bf16)
    dec_rows, dec_own_next = tie(dec_grad.astype(bf16), dec_own_next)
    dec_rows = rows_of(dec_rows)
    dec_gram = lax.dot_general(
        dec_own_next, dec_own_next, to_latents, preferred_element_type=f32
    )
    dec_gram, enc_gots, enc_keep = tie(dec_gram, enc_gots, enc_keep)
    stages = []
    enc_grad = encb_grad = None

    def dec_note(sents, got):
        nonlocal enc_grad, encb_grad, dec_rows
        if not stages:
            enc_grad, encb_grad = scatter_chips(enc_keep, enc_gots)
        if len(stages) == 2:
            got, enc_grad, dec_rows = tie(got, enc_grad, dec_rows)
        stages.append(got)
        return got

    dec_near, dec_far, _ = sum_gram(
        dec_gram,
        jnp.zeros((model_width,), f32),
        dec_note,
    )
    bias_term = jnp.sum(back_rows[:, :model_width], 0, dtype=f32) - jnp.dot(
        enc_own.astype(f32),
        encb_grad,
        precision=HIGH_PRECISION,
    )

    enc_own_next = (MOMENTUM * enc_moment_own.astype(f32) + enc_grad).astype(bf16)
    enc_gram = lax.dot_general(
        enc_own_next, enc_own_next, to_latents, preferred_element_type=f32
    )
    enc_gram, dec_near = lax.optimization_barrier((enc_gram, dec_near))
    enc_momenta = lax.all_gather(enc_own_next, "narrow")
    progress = []

    def dec_fill(sents, got):
        step = len(progress)
        if step == 0:
            early, _ = tie(dec_near, sents)
            state = series_start(place, early, dec_far)
        else:
            state = series_next(step, progress[-1])
        got, state = lax.optimization_barrier((got, state))
        progress.append(state)
        return got

    enc_near, enc_far, grad_decb = sum_gram(enc_gram, bias_term, dec_fill)
    dec_factor = progress[-1][0]
    dec_ortho = rows_of(
        jnp.dot(dec_factor, dec_own_next, preferred_element_type=f32).astype(bf16)
    )
    step_scale = MUON_RATE * 0.2 * math.sqrt(max(D, L))
    dec_next = MOMENTUM * dec_moment_t + dec_rows.astype(f32)
    dec_new = dec_weight_t * (1.0 - MUON_RATE * DECAY) - step_scale * dec_ortho.astype(f32)
    dec_copy = dec_new.astype(bf16)
    state = series_start(place, enc_near, enc_far)
    for step in range(1, NS_STEPS):
        state = series_next(step, state)
    enc_new, enc_next, enc_copy = finish(place, state[0], enc_momenta, enc_weight)
    encb_new, encb_one, encb_two = adam_update(enc_bias, encb_grad, encb_first, encb_second)
    decb_new, decb_one, decb_two = adam_update(decoder_bias, grad_decb, decb_first, decb_second)
    return (
        token_loss,
        enc_new,
        enc_next,
        enc_copy,
        dec_new.T,
        dec_next.T,
        dec_copy.T,
        encb_new,
        encb_one,
        encb_two,
        decb_new,
        decb_one,
        decb_two,
    )


def solution(mesh):
    wide, narrow = mesh.devices.shape
    fine = Mesh(mesh.devices.reshape(wide // 2, 2, narrow), ("chip", "core", "narrow"))
    placed = (
        P(("chip", "core", "narrow")),
        P(("chip", "core", "narrow")),
        P(("chip", "core", "narrow"), None),
        P(("chip", "core", "narrow"), None),
        P(),
        P(("chip", "core"), None),
        P(),
        P(),
        P(),
        P(),
        P(),
        P(),
        P(),
        P("narrow", ("chip", "core")),
        P(("chip", "core", "narrow")),
        P(("chip", "core"), "narrow"),
        P(),
        P("narrow", ("chip", "core")),
        P(("chip", "core"), "narrow"),
        P(("chip", "core", "narrow")),
        P(("chip", "core", "narrow")),
        P(),
        P(),
    )
    return jax.shard_map(
        local,
        mesh=fine,
        in_specs=placed,
        out_specs=(
            P(("chip", "core", "narrow")),
            P("narrow", ("chip", "core")),
            P("narrow", ("chip", "core")),
            P("narrow", ("chip", "core")),
            P(("chip", "core"), "narrow"),
            P(("chip", "core"), "narrow"),
            P(("chip", "core"), "narrow"),
            P(("chip", "core", "narrow")),
            P(("chip", "core", "narrow")),
            P(("chip", "core", "narrow")),
            P(),
            P(),
            P(),
        ),
        check_vma=False,
    )
```

```python
import functools
import math

import jax
import jax.numpy as jnp
from jax import lax
from jax.experimental import pallas as pl
from jax.experimental.pallas import tpu as pltpu
from jax.sharding import Mesh
from jax.sharding import PartitionSpec as P

D = 768
HEAD_DIM = 64
L = 32768
NS_STEPS = 5
STEP = 10


HIGH_PRECISION = lax.Precision.HIGHEST
AUX_COEF = 1.0 / 32.0
EPS_NORM = 1e-05
NS_EPS = 1e-07
QA = 3.4445
QB = -4.775
QC = 2.0315
MOMENTUM = 0.95
MUON_RATE = 0.1
DECAY = 0.1
BIAS_RATE = 0.3
BETA_ONE = 0.9
BETA_TWO = 0.999
ADAM_EPS = 1e-08


def layer_norm(value, gain, shift):
    row_mean = jnp.mean(value, -1, keepdims=True)
    centred = value - row_mean
    row_var = jnp.mean(centred * centred, -1, keepdims=True)
    return centred * lax.rsqrt(row_var + EPS_NORM) * gain + shift


def frozen_block(start, ctx_length, ln_gains, frozen_bias, w_qkv, w_proj, w_fc, w_out):
    row_count, model_width = start.shape
    head_count = model_width // HEAD_DIM
    ff_width = w_fc.shape[1]
    shifts = frozen_bias[: 2 * model_width].reshape(2, model_width)
    b_qkv = frozen_bias[2 * model_width : 5 * model_width]
    b_proj = frozen_bias[5 * model_width : 6 * model_width]
    b_fc = frozen_bias[6 * model_width : 6 * model_width + ff_width]
    b_out = frozen_bias[6 * model_width + ff_width :]
    normed = layer_norm(start, ln_gains[0], shifts[0]).astype(jnp.bfloat16)
    qkv_rows = (jnp.dot(normed, w_qkv, preferred_element_type=jnp.float32) + b_qkv).astype(
        jnp.bfloat16
    )
    head_split = qkv_rows.reshape(row_count, 3, head_count, HEAD_DIM)
    scores = jnp.einsum(
        "qhd,khd->hqk", head_split[:, 0], head_split[:, 1], preferred_element_type=jnp.float32
    ) * HEAD_DIM ** (-0.5)
    positions = jnp.arange(row_count)
    allowed = (positions[None, :] <= positions[:, None]) & (positions[None, :] < ctx_length)
    attn_probs = jax.nn.softmax(jnp.where(allowed[None], scores, -1e30), axis=-1).astype(
        jnp.bfloat16
    )
    mixed = jnp.einsum(
        "hqk,khd->qhd", attn_probs, head_split[:, 2], preferred_element_type=jnp.float32
    )
    mixed = mixed.reshape(row_count, model_width).astype(jnp.bfloat16)
    hidden = start + jnp.dot(mixed, w_proj, preferred_element_type=jnp.float32) + b_proj
    normed_two = layer_norm(hidden, ln_gains[1], shifts[1]).astype(jnp.bfloat16)
    inner_acts = jax.nn.gelu(
        jnp.dot(normed_two, w_fc, preferred_element_type=jnp.float32) + b_fc, approximate=True
    ).astype(jnp.bfloat16)
    return (hidden + jnp.dot(inner_acts, w_out, preferred_element_type=jnp.float32) + b_out).astype(
        jnp.bfloat16
    )


def split_bf(value):
    high = value.astype(jnp.bfloat16)
    return high, (value - high.astype(jnp.float32)).astype(jnp.bfloat16)


def row_blocks(size, body):
    block = 256

    def step(index, carry):
        body(pl.ds(pl.multiple_of(index * block, block), block), index * block)
        return carry

    lax.fori_loop(0, size // block, step, 0)


def eye_rows(start, size):
    rows = lax.broadcasted_iota(jnp.int32, (256, size), 0) + start
    cols = lax.broadcasted_iota(jnp.int32, (256, size), 1)
    return (rows == cols).astype(jnp.float32)


def dot_f32(a, b):
    return jnp.dot(a, b, preferred_element_type=jnp.float32)


def store_split(pair, rows, value):
    pair[0][rows, :], pair[1][rows, :] = split_bf(value)


def three(left, right, rows):
    high, low = left[0][rows, :], left[1][rows, :]
    return dot_f32(high, right[0][...]) + (
        dot_f32(high, right[1][...]) + dot_f32(low, right[0][...])
    )


def series_step(gram, poly, half, out, old, new, step):
    size = gram[0].shape[0]
    last = step == NS_STEPS - 1
    exact_square = step >= 3

    def poly_rows(rows, start):
        here = gram[0][rows, :].astype(jnp.float32) + gram[1][rows, :].astype(jnp.float32)
        if exact_square:
            square = three(gram, gram, rows)
        else:
            square = dot_f32(gram[0][rows, :], gram[0][...])
        store_split(poly, rows, QA * eye_rows(start, size) + QB * here + QC * square)

    def half_rows(rows, start):
        store_split(half, rows, three(gram, poly, rows))

    def gram_rows(rows, start):
        store_split(out, rows, three(poly, half, rows))

    def product_rows(rows, start):
        new[rows, :] = dot_f32(poly[0][rows, :], old[...]).astype(jnp.bfloat16)

    row_blocks(size, poly_rows)
    if not last:
        row_blocks(size, half_rows)
        row_blocks(size, gram_rows)
    if step > 0:
        row_blocks(size, product_rows)


def first_kernel(place_ref, near_ref, far_ref, o_hi, o_lo, q_ref, total, *scratch):
    size = total.shape[0]
    chips, rows_each = near_ref.shape[:2]
    chip, core = place_ref[0], place_ref[1]
    gram, poly, half = scratch[:2], scratch[2:4], scratch[4:6]
    for offset in range(chips):
        for side, source in enumerate((near_ref, far_ref)):
            first = jnp.bitwise_xor(core, side) * (size // 2)
            first = first + jnp.bitwise_xor(chip, offset) * rows_each
            total[pl.ds(pl.multiple_of(first, 8), rows_each), :] = source[offset].astype(
                jnp.float32
            )

    def trace_part(index, value):
        start = pl.multiple_of(index * 256, 256)
        return value + jnp.sum(total[pl.ds(start, 256), :] * eye_rows(start, size))

    trace_sum = lax.fori_loop(0, size // 256, trace_part, jnp.zeros((), jnp.float32))
    scale = 1.0 / (jnp.sqrt(jnp.full((1, 1), trace_sum)) + NS_EPS)

    def load_rows(rows, start):
        store_split(gram, rows, total[rows, :] * (scale * scale))

    row_blocks(size, load_rows)
    series_step(gram, poly, half, (o_hi, o_lo), None, None, 0)

    def product_rows(rows, start):
        value = poly[0][rows, :].astype(jnp.float32) + poly[1][rows, :].astype(jnp.float32)
        q_ref[rows, :] = (value * scale).astype(jnp.bfloat16)

    row_blocks(size, product_rows)


def middle_kernel(step, g_hi, g_lo, q_ref, o_hi, o_lo, out_ref, *scratch):
    series_step(
        (g_hi, g_lo), scratch[:2], scratch[2:4], (o_hi, o_lo), q_ref, out_ref, step
    )


def last_kernel(g_hi, g_lo, q_ref, out_ref, *scratch):
    series_step((g_hi, g_lo), scratch[:2], None, None, q_ref, out_ref, NS_STEPS - 1)


def square_call(kernel, outs, scratch, passes, *operands):
    size = operands[-1].shape[-1]
    whole = pl.BlockSpec(memory_space=pltpu.VMEM)
    specs = [whole] * len(operands)
    if operands[0].ndim == 1:
        specs[0] = pl.BlockSpec(memory_space=pltpu.SMEM)
    square = jax.ShapeDtypeStruct((size, size), jnp.bfloat16)
    return pl.pallas_call(
        kernel,
        out_shape=[square] * outs,
        in_specs=specs,
        out_specs=[whole] * outs,
        scratch_shapes=[pltpu.VMEM((size, size), kind) for kind in scratch],
        compiler_params=pltpu.CompilerParams(vmem_limit_bytes=40 * 2**20),
        cost_estimate=pl.CostEstimate(
            flops=passes * size**3 // 16, bytes_accessed=size * size // 2, transcendentals=0
        ),
    )(*operands)


def series_start(place, near, far):
    bf16 = jnp.bfloat16
    return square_call(first_kernel, 3, [jnp.float32] + [bf16] * 6, 8, place, near, far)


def series_next(step, state):
    bf16 = jnp.bfloat16
    if step == NS_STEPS - 1:
        return square_call(last_kernel, 1, [bf16] * 2, 4, *state)
    kernel = functools.partial(middle_kernel, step)
    return square_call(kernel, 3, [bf16] * 4, 8 if step < 3 else 10, *state)


def code_kernel(shifts, place_ref, ids_ref, out_ref, high, low, stage):
    wide_shift, own_shift, top_count, orders = shifts
    batch, groups = stage.shape[:2]
    rows, picks = ids_ref.shape
    bf16, f32 = jnp.bfloat16, jnp.float32
    chip, core, narrow = place_ref[0], place_ref[1], place_ref[2]
    latent_count = out_ref.shape[1]
    half_shift = own_shift - 1

    ids = ids_ref[...]
    owner = lax.shift_right_logical(ids, wide_shift)
    within = jnp.bitwise_and(ids, (1 << wide_shift) - 1)
    mine = (lax.shift_right_logical(within, own_shift) == narrow) & (
        jnp.bitwise_and(owner, 1) == core
    )
    inner = jnp.bitwise_and(within, (1 << own_shift) - 1)
    offset = jnp.bitwise_xor(lax.shift_right_logical(owner, 1), chip)
    half = lax.shift_right_logical(inner, half_shift)
    spots = []
    for order in orders:
        spot = jnp.zeros_like(offset)
        for index, bit in enumerate(order[:-1]):
            spot = spot + jnp.where(jnp.bitwise_and(offset, bit) != 0, 1 << index, 0)
        sent = jnp.where(jnp.bitwise_and(offset, order[-1]) != 0, latent_count // 4, 0)
        spots.append(sent + lax.shift_left(spot, half_shift))
    column = (
        half * (latent_count // 2)
        + jnp.where(half == 0, spots[0], spots[1])
        + jnp.bitwise_and(inner, (1 << half_shift) - 1)
    )
    high[...] = jnp.where(mine, lax.shift_right_logical(column, 7), -1).astype(f32)
    low[...] = jnp.bitwise_and(column, 127).astype(f32)

    one, zero = jnp.ones((16, picks), bf16), jnp.zeros((16, picks), bf16)
    places = lax.broadcasted_iota(jnp.int32, (16, picks), 1)
    kinds = jnp.where(places < top_count, 1.0, 2.0).astype(bf16)
    steps = lax.broadcasted_iota(jnp.int32, (16, picks), 0).astype(f32).astype(bf16)

    def hot(row, count, value):
        row = jnp.broadcast_to(row, (16, picks)).astype(bf16)
        parts = [
            jnp.where(steps + jnp.asarray(16 * part, bf16) == row, value, zero)
            for part in range(max(1, count // 16))
        ]
        return jnp.concatenate(parts, 0).astype(jnp.float8_e4m3fn)

    def one_batch(index, carry):
        first = pl.multiple_of(index * batch, batch)
        for token in range(batch):
            row = pl.ds(first + token, 1)
            codes = lax.dot_general(
                hot(high[row, :], groups, kinds),
                hot(low[row, :], 128, one),
                (((1,), (1,)), ((), ())),
                preferred_element_type=f32,
            )
            stage[token] = codes[:groups]
        for group in range(groups):
            lanes = slice(group * 128, (group + 1) * 128)
            out_ref[pl.ds(first, batch), lanes] = stage[:, group, :].astype(bf16)
        return carry

    lax.fori_loop(0, rows // batch, one_batch, 0)


def kind_codes(place, ids, latent_count, sizes):
    wide_latents, own_latents, top_count, orders = sizes
    row_total, pick_total = ids.shape
    rows = min(128, row_total)
    shifts = (wide_latents.bit_length() - 1, own_latents.bit_length() - 1, top_count, orders)
    return pl.pallas_call(
        functools.partial(code_kernel, shifts),
        grid=(row_total // rows,),
        out_shape=jax.ShapeDtypeStruct((row_total, latent_count), jnp.bfloat16),
        in_specs=[
            pl.BlockSpec(memory_space=pltpu.SMEM),
            pl.BlockSpec((rows, pick_total), lambda i: (i, 0)),
        ],
        out_specs=pl.BlockSpec((rows, latent_count), lambda i: (i, 0)),
        scratch_shapes=[
            pltpu.VMEM((rows, pick_total), jnp.float32),
            pltpu.VMEM((rows, pick_total), jnp.float32),
            pltpu.VMEM((32, latent_count // 128, 128), jnp.float32),
        ],
        compiler_params=pltpu.CompilerParams(vmem_limit_bytes=40 * 2**20),
        cost_estimate=pl.CostEstimate(
            flops=row_total * latent_count,
            bytes_accessed=row_total * pick_total,
            transcendentals=0,
        ),
    )(place, ids)


def join_rows(sources, target):
    rows = sources[0].shape[0]
    for index, source in enumerate(sources):
        target[index * rows : (index + 1) * rows, :] = source[...]


def pick_copy(step, count, sources, target):
    for index, source in enumerate(sources):

        @pl.when(step // count == index)
        def _(source=source):
            target[...] = source[...]


def forward_kernel(count, x_ref, dead_ref, *refs):
    code_parts, encs, decs = refs[:4], refs[4:8], refs[8:12]
    top_ref, aux_ref, far_ref, near_ref = refs[12:16]
    codes_ref, enc, dec, acc_top, acc_aux = refs[16:]
    join_rows(code_parts, codes_ref)
    step = pl.program_id(0)
    rows_all, width = x_ref.shape
    block = min(1024, rows_all)
    pick_copy(step, count, encs, enc)
    pick_copy(step, count, decs, dec)

    @pl.when(step == 0)
    def _():
        acc_top[...] = jnp.zeros_like(acc_top)
        acc_aux[...] = jnp.zeros_like(acc_aux)

    bias = enc[pl.ds(width, 16), :].astype(jnp.float32)[:1]
    to_features = (((1,), (1,)), ((), ()))

    def one(index, carry):
        rows = pl.ds(pl.multiple_of(index * block, block), block)
        pre = dot_f32(x_ref[rows, :], enc[pl.ds(0, width), :]) + bias
        codes = codes_ref[rows, :]
        zero = jnp.zeros(codes.shape, jnp.bfloat16)
        top = jnp.where(codes == 1.0, pre.astype(jnp.bfloat16), zero)
        aux = jnp.where(codes == 2.0, (pre * dead_ref[...]).astype(jnp.bfloat16), zero)
        top_ref[rows, :] = top
        aux_ref[rows, :] = aux
        acc_top[rows, :] += lax.dot_general(
            top, dec[...], to_features, preferred_element_type=jnp.float32
        )
        acc_aux[rows, :] += lax.dot_general(
            aux, dec[...], to_features, preferred_element_type=jnp.float32
        )
        return carry

    lax.fori_loop(0, rows_all // block, one, 0)

    @pl.when(step == pl.num_programs(0) - 1)
    def _():
        half = rows_all // 2
        for first, acc in ((0, acc_top), (width, acc_aux)):
            near_ref[:, first : first + width] = acc[pl.ds(0, half), :]
            far_ref[:, first : first + width] = acc[pl.ds(half, half), :].astype(jnp.bfloat16)


def part_specs(shape, axis, block, count, starts):
    specs = []
    for index, first in enumerate(starts):

        def place(step, index=index, first=first):
            spot = jnp.clip(step - index * count, 0, count - 1)
            return (spot + first, 0) if axis == 0 else (0, spot + first)

        size = (block, shape[1]) if axis == 0 else (shape[0], block)
        specs.append(pl.BlockSpec(size, place))
    return specs


def forward(x, codes, dead, encs, decs):
    rows, width = x.shape
    acts_shape = (rows, dead.shape[1])
    quarter = encs[0].shape[1]
    block = min(512, quarter)
    count = quarter // block
    lanes = pl.BlockSpec((rows, block), lambda step: (0, step))
    fixed = lambda shape: pl.BlockSpec(shape, lambda step: (0, 0))
    bf16, f32 = jnp.bfloat16, jnp.float32
    half_shape = (rows // 2, 2 * width)
    return pl.pallas_call(
        functools.partial(forward_kernel, count),
        grid=(4 * count,),
        out_shape=[
            jax.ShapeDtypeStruct(acts_shape, bf16),
            jax.ShapeDtypeStruct(acts_shape, bf16),
            jax.ShapeDtypeStruct(half_shape, bf16),
            jax.ShapeDtypeStruct(half_shape, f32),
        ],
        in_specs=[fixed(x.shape), pl.BlockSpec((1, block), lambda step: (0, step))]
        + [pl.BlockSpec((rows // 4, block), lambda step: (0, step))] * 4
        + part_specs(encs[0].shape, 1, block, count, (0, 0, 0, 0))
        + part_specs(decs[0].shape, 1, block, count, (0, 0, 0, 0)),
        out_specs=[lanes, lanes, fixed(half_shape), fixed(half_shape)],
        scratch_shapes=[
            pltpu.VMEM((rows, block), bf16),
            pltpu.VMEM((width + 16, block), bf16),
            pltpu.VMEM((width, block), bf16),
            pltpu.VMEM((rows, width), f32),
            pltpu.VMEM((rows, width), f32),
        ],
        compiler_params=pltpu.CompilerParams(vmem_limit_bytes=58 * 2**20),
        cost_estimate=pl.CostEstimate(
            flops=2 * rows * width * dead.shape[1],
            bytes_accessed=6 * rows * dead.shape[1],
            transcendentals=0,
        ),
    )(x, dead, *codes, *encs, *decs)


def store_part(count, refs, rows, value):
    step = pl.program_id(0)
    for index, ref in enumerate(refs):

        @pl.when(step // count == index)
        def _(ref=ref):
            ref[rows, :] = value.astype(ref.dtype)


def dec_grad_kernel(count, near_r, near_a, far_r, far_a, top_ref, aux_ref, *outs):
    half = near_r.shape[1]

    def one(index, carry):
        rows = pl.ds(pl.multiple_of(index * 768, 768), 768)
        value = dot_f32(near_r[rows, :], top_ref[:half, :])
        value = value + dot_f32(near_a[rows, :], aux_ref[:half, :])
        value = value + dot_f32(far_r[rows, :], top_ref[half:, :])
        value = value + dot_f32(far_a[rows, :], aux_ref[half:, :])
        store_part(count, outs, rows, value)
        return carry

    lax.fori_loop(0, near_r.shape[0] // 768, one, 0)


def dec_grads(near_t, far_t, top_acts, aux_acts, quarters, kind):
    width = near_t.shape[0] // 2
    rows, latents = top_acts.shape
    quarter = latents // 4
    block = min(512, quarter)
    count = quarter // block

    def lanes(step):
        return (0, jnp.where(step < count, quarters[0], quarters[1] - 1) * count + step)

    acts = pl.BlockSpec((rows, block), lanes)
    shape = (width, quarter)
    return pl.pallas_call(
        functools.partial(dec_grad_kernel, count),
        grid=(2 * count,),
        out_shape=[jax.ShapeDtypeStruct(shape, kind)] * 2,
        in_specs=[
            pl.BlockSpec((width, rows // 2), lambda step: (0, 0)),
            pl.BlockSpec((width, rows // 2), lambda step: (1, 0)),
            pl.BlockSpec((width, rows // 2), lambda step: (0, 0)),
            pl.BlockSpec((width, rows // 2), lambda step: (1, 0)),
            acts,
            acts,
        ],
        out_specs=part_specs(shape, 1, block, count, (0, 0)),
        compiler_params=pltpu.CompilerParams(vmem_limit_bytes=58 * 2**20),
        cost_estimate=pl.CostEstimate(
            flops=rows * width * quarter // 8, bytes_accessed=rows * quarter // 4, transcendentals=0
        ),
    )(near_t, near_t, far_t, far_t, top_acts, aux_acts)


def enc_grad_kernel(count, x_ref, near_ref, far_ref, dead_ref, *refs):
    code_parts, (dec_a, dec_b, out_a, out_b, dec, grads) = refs[:4], refs[4:]
    step = pl.program_id(0)
    pick_copy(step, count, (dec_a, dec_b), dec)
    width, latents = dec.shape
    quarter = code_parts[0].shape[0]
    total = jnp.zeros((1, latents), jnp.float32)
    for index, back_ref in enumerate((near_ref, far_ref)):
        top = dot_f32(back_ref[:, :width], dec[...])
        aux = dot_f32(back_ref[:, width:], dec[...]) * dead_ref[...]
        for part in range(2):
            codes = code_parts[2 * index + part][...].astype(jnp.float32)
            lines = slice(part * quarter, (part + 1) * quarter)
            value = jnp.where(codes == 2.0, aux[lines], 0.0)
            value = jnp.where(codes == 1.0, top[lines], value).astype(jnp.bfloat16)
            first = (2 * index + part) * quarter
            grads[first : first + quarter, :] = value
            total = total + jnp.sum(value.astype(jnp.float32), 0, keepdims=True)

    def two(index, carry):
        rows = pl.ds(pl.multiple_of(index * 768, 768), 768)
        store_part(count, (out_a, out_b), rows, dot_f32(x_ref[rows, :], grads[...]))
        return carry

    lax.fori_loop(0, width // 768, two, 0)
    lines = lax.broadcasted_iota(jnp.int32, (16, latents), 0)
    if out_a.dtype == jnp.bfloat16:
        high = total.astype(jnp.bfloat16).astype(jnp.float32)
        lines = jnp.where(lines == 0, high, jnp.where(lines == 1, total - high, 0.0))
    else:
        lines = jnp.where(lines == 0, total, 0.0)
    store_part(count, (out_a, out_b), pl.ds(width, 16), lines)


def enc_grads(x_t, near, far, codes, dead, parts, quarters, kind):
    width, rows = x_t.shape
    quarter = dead.shape[1] // 4
    block = min(512, quarter)
    count = quarter // block

    def lanes(step):
        return (0, jnp.where(step < count, quarters[0], quarters[1] - 1) * count + step)

    shape = (width + 16, quarter)
    return pl.pallas_call(
        functools.partial(enc_grad_kernel, count),
        grid=(2 * count,),
        out_shape=[jax.ShapeDtypeStruct(shape, kind)] * 2,
        in_specs=[
            pl.BlockSpec(x_t.shape, lambda step: (0, 0)),
            pl.BlockSpec(near.shape, lambda step: (0, 0)),
            pl.BlockSpec(far.shape, lambda step: (0, 0)),
            pl.BlockSpec((1, block), lanes),
        ]
        + [pl.BlockSpec((rows // 4, block), lanes)] * 4
        + part_specs(parts[0].shape, 1, block, count, (0, 0)),
        out_specs=part_specs(shape, 1, block, count, (0, 0)),
        scratch_shapes=[
            pltpu.VMEM((width, block), jnp.bfloat16),
            pltpu.VMEM((rows, block), jnp.bfloat16),
        ],
        compiler_params=pltpu.CompilerParams(vmem_limit_bytes=58 * 2**20),
        cost_estimate=pl.CostEstimate(
            flops=rows * width * quarter // 8, bytes_accessed=rows * quarter // 4, transcendentals=0
        ),
    )(x_t, near, far, dead, *codes, *parts)


def finish_kernel(place_ref, factor_ref, momentum_ref, weight_ref, *outs):
    new_ref, next_ref, copy_ref = outs
    rows = factor_ref.shape[0]
    f32 = jnp.float32
    momentum = momentum_ref[0]
    kept = momentum_ref[0, pl.ds(pl.multiple_of(place_ref[2] * rows, 16), rows), :].astype(f32)
    ortho = dot_f32(factor_ref[...], momentum)
    next_ref[...] = kept
    step_scale = MUON_RATE * 0.2 * math.sqrt(max(D, L))
    value = weight_ref[...] * (1.0 - MUON_RATE * DECAY) - step_scale * ortho
    new_ref[...] = value
    copy_ref[...] = value.astype(jnp.bfloat16)


def finish(place, factor, momenta, weight):
    count, width, block = momenta.shape
    rows = weight.shape[0]
    part = pl.BlockSpec((rows, block), lambda step, place: (0, step))
    return pl.pallas_call(
        finish_kernel,
        grid_spec=pltpu.PrefetchScalarGridSpec(
            num_scalar_prefetch=1,
            grid=(count,),
            in_specs=[
                pl.BlockSpec((rows, width), lambda step, place: (place[2], 0)),
                pl.BlockSpec((1, width, block), lambda step, place: (step, 0, 0)),
                part,
            ],
            out_specs=[part] * 3,
        ),
        out_shape=[
            jax.ShapeDtypeStruct(weight.shape, jnp.float32),
            jax.ShapeDtypeStruct(weight.shape, jnp.float32),
            jax.ShapeDtypeStruct(weight.shape, jnp.bfloat16),
        ],
        compiler_params=pltpu.CompilerParams(vmem_limit_bytes=58 * 2**20),
        cost_estimate=pl.CostEstimate(
            flops=2 * rows * width * block * count,
            bytes_accessed=8 * rows * block * count,
            transcendentals=0,
        ),
    )(place, factor, momenta, weight)


def adam_update(param, grad, first, second):
    first = BETA_ONE * first + (1.0 - BETA_ONE) * grad
    second = BETA_TWO * second + (1.0 - BETA_TWO) * grad * grad
    denom = jnp.sqrt(second / (1.0 - BETA_TWO**STEP)) + ADAM_EPS
    return (param - BIAS_RATE * (first / (1.0 - BETA_ONE**STEP)) / denom, first, second)


def local(
    token_ids,
    lengths,
    top_ids,
    aux_ids,
    dead_set,
    token_table,
    position_table,
    ln_gains,
    frozen_bias,
    w_qkv,
    w_proj,
    w_fc,
    w_out,
    enc_weight,
    enc_bias,
    dec_weight,
    decoder_bias,
    enc_moment,
    dec_moment,
    encb_first,
    encb_second,
    decb_first,
    decb_second,
):
    chips = lax.axis_size("chip")
    narrow_count = lax.axis_size("narrow")
    wide_count = 2 * chips
    wide = ("chip", "core")
    chip_pos = lax.axis_index("chip")
    core_pos = lax.axis_index("core")
    wide_pos = 2 * chip_pos + core_pos
    narrow_pos = lax.axis_index("narrow")
    row_count = token_ids.shape[0]
    model_width = token_table.shape[1]
    wide_latents = enc_weight.shape[1]
    own_latents = wide_latents // narrow_count
    half_latents = own_latents // 2
    latent_count = chips * own_latents
    core_rows = narrow_count * row_count
    bf16, f32 = jnp.bfloat16, jnp.float32
    to_latents = (((1,), (1,)), ((), ()))
    over_rows = (((0,), (0,)), ((), ()))
    place = jnp.stack([chip_pos, core_pos, narrow_pos]).astype(jnp.int32)
    bits = [1 << bit for bit in range(chips.bit_length() - 1)]
    orders = (bits, bits[::-1])

    tie = lambda *values: lax.optimization_barrier(values)

    def swap(value, axis, offset):
        count = lax.axis_size(axis)
        return lax.ppermute(value, axis, [(spot, spot ^ offset) for spot in range(count)])

    def spread_narrow(value):
        parts = [value] + [swap(value, "narrow", k) for k in range(1, narrow_count)]
        return jnp.concatenate(parts, 0)

    def rows_to_latents(value):
        return lax.all_to_all(value, "narrow", split_axis=1, concat_axis=0, tiled=True)

    def rows_of(value):
        return lax.all_to_all(value, "narrow", split_axis=0, concat_axis=1, tiled=True)

    def gather_start(own):
        helds, gots = [], []
        for part, order in enumerate(orders):
            held = own[:, part * half_latents : (part + 1) * half_latents]
            for bit in order[:-2]:
                held = jnp.concatenate([held, swap(held, "chip", bit)], 1)
            helds.append(held)
            gots.append(swap(held, "chip", order[-2]))
        return helds, gots

    def gather_join(helds, gots):
        return [jnp.concatenate(pair, 1) for pair in zip(helds, gots)]

    def gather_end(halves):
        pieces = []
        for held, order in zip(halves, orders):
            pieces += [held, swap(held, "chip", order[-1])]
        return pieces

    def scatter_chips(keeps, gots):
        results, sums = [], []
        for order, held, got in zip(orders, keeps, gots):
            held = held + got.astype(f32)
            for bit in reversed(order[:-1]):
                lower, upper = jnp.split(held, 2, 1)
                sent = upper[:model_width].astype(bf16)
                if held.shape[0] > model_width:
                    lines = split_bf(upper[model_width] + upper[model_width + 1])
                    spare = jnp.zeros((14, upper.shape[1]), bf16)
                    sent = jnp.concatenate([sent, *(line[None] for line in lines), spare], 0)
                held = lower + swap(sent, "chip", bit).astype(f32)
            results.append(held[:model_width])
            if held.shape[0] > model_width:
                sums.append(held[model_width] + held[model_width + 1])
        return jnp.concatenate(results, 1), jnp.concatenate(sums) if sums else None

    vocab_dev = token_table.shape[0]
    every_ids = lax.all_gather(token_ids, wide, axis=0, tiled=False).reshape(wide_count, row_count)
    every_ids = jnp.concatenate(
        [
            lax.dynamic_slice_in_dim(every_ids, wide_pos ^ offset, 1, 0)
            for offset in range(wide_count)
        ],
        1,
    )[0]
    local_ids = every_ids - wide_pos * vocab_dev
    inside = (local_ids >= 0) & (local_ids < vocab_dev)
    looked = jnp.take(token_table, jnp.clip(local_ids, 0, vocab_dev - 1), axis=0)
    looked = jnp.where(inside[:, None], looked, jnp.zeros((), bf16))
    dec_weight_t, dec_moment_t = dec_weight.T, dec_moment.T
    rows_each = enc_weight.shape[0]
    enc_own = rows_to_latents(enc_weight.astype(bf16))
    picks = jnp.concatenate([top_ids, aux_ids], 1)
    near_picks = spread_narrow(picks)
    far_picks = swap(near_picks, "core", 1)

    looked = looked.reshape(chips, 2, row_count, model_width)
    looked = looked[:, 0] + swap(looked[:, 1], "core", 1)
    embedded = looked[0].astype(f32)
    for k in range(1, chips):
        embedded = embedded + swap(looked[k], "chip", k).astype(f32)

    bias_rows = jnp.concatenate(
        [enc_bias.astype(bf16)[None], jnp.zeros((15, own_latents), bf16)], 0
    )
    enc_own, embedded = tie(enc_own, embedded)
    dec_cast, enc_own = tie(dec_weight_t.astype(bf16), enc_own)
    dec_own = rows_to_latents(dec_cast)
    enc_helds, enc_halves = gather_start(jnp.concatenate([enc_own, bias_rows], 0))

    dead_here = jnp.stack(
        [
            lax.dynamic_slice_in_dim(
                dead_set,
                (2 * (chip_pos ^ offset) + core_pos) * wide_latents + narrow_pos * own_latents,
                own_latents,
            )
            for offset in range(chips)
        ]
    )
    places = [0]
    dead_parts = []
    for part, order in enumerate(orders):
        places = [0]
        for bit in order:
            places = places + [spot ^ bit for spot in places]
        for spot in places:
            dead_parts.append(dead_here[spot, part * half_latents : (part + 1) * half_latents])
    dead_here = jnp.concatenate(dead_parts)[None].astype(f32)
    sizes = (wide_latents, own_latents, top_ids.shape[1], orders)
    start = embedded + position_table[:row_count].astype(f32)
    ctx_length = lengths[0]
    inputs = frozen_block(start, ctx_length, ln_gains, frozen_bias, w_qkv, w_proj, w_fc, w_out)
    counted = (jnp.arange(row_count) < ctx_length).astype(f32)
    near_picks, inputs, enc_halves, dead_here, dec_own = tie(
        near_picks, inputs, enc_halves, dead_here, dec_own
    )
    enc_parts = gather_end(gather_join(enc_helds, enc_halves))
    got_inputs = [swap(inputs, "narrow", k) for k in range(1, narrow_count)]
    half_rows = core_rows // 2
    codes = [kind_codes(place, near_picks[:half_rows], latent_count, sizes)]
    enc_lasts = [enc_parts[1], enc_parts[3]]
    codes, got_inputs, enc_lasts = tie(codes, got_inputs, enc_lasts)
    enc_parts = [enc_parts[0], enc_lasts[0], enc_parts[2], enc_lasts[1]]
    near_picks, codes = tie(near_picks, codes)
    dec_helds, dec_halves = gather_start(dec_own)
    codes = [*codes, kind_codes(place, near_picks[half_rows:], latent_count, sizes)]
    dec_halves, codes = tie(dec_halves, codes)
    dec_parts = gather_end(gather_join(dec_helds, dec_halves))
    moments = jnp.concatenate([enc_moment.astype(bf16), dec_moment_t.astype(bf16)], 0)
    moments, got_inputs = tie(moments, got_inputs)
    moments = rows_to_latents(moments)
    near_inputs = jnp.concatenate([inputs, *got_inputs], 0)
    far_picks, codes = tie(far_picks, codes)
    codes = [*codes, kind_codes(place, far_picks[:half_rows], latent_count, sizes)]
    far_inputs, codes = tie(swap(near_inputs, "core", 1), codes)
    far_picks, codes = tie(far_picks, codes)
    codes = [*codes, kind_codes(place, far_picks[half_rows:], latent_count, sizes)]
    all_inputs = jnp.concatenate([near_inputs, far_inputs], 0)
    encoder_in = (all_inputs.astype(f32) - decoder_bias).astype(bf16)
    top_acts, aux_acts, far, near = forward(encoder_in, codes, dead_here, enc_parts, dec_parts)
    far, moments = tie(far, moments)
    encoder_t = encoder_in.T
    far_got, encoder_t = tie(swap(far, "core", 1), encoder_t)
    rebuilt = near + far_got.astype(f32)
    rounded = rebuilt.astype(bf16)
    rebuilt = rebuilt[:row_count]
    for k in range(1, narrow_count):
        part = rounded[k * row_count : (k + 1) * row_count]
        rebuilt = rebuilt + swap(part, "narrow", k).astype(f32)
    target = inputs.astype(f32)
    reconstructed_input = rebuilt[:, :model_width] + decoder_bias
    auxiliary_reconstruction = rebuilt[:, model_width:]
    recon_error = target - reconstructed_input
    aux_gap = auxiliary_reconstruction - recon_error
    token_loss = (
        counted
        * (jnp.sum(recon_error * recon_error, 1) + AUX_COEF * jnp.sum(aux_gap * aux_gap, 1))
        / model_width
    )
    back_recon = 2.0 / model_width * counted[:, None] * (reconstructed_input - target)
    back_aux = 2.0 * AUX_COEF / model_width * counted[:, None] * aux_gap
    back_rows = jnp.concatenate([back_recon, back_aux], 1).astype(bf16)
    near_back = spread_narrow(back_rows)
    far_back = swap(near_back, "core", 1)
    near_t, far_back = tie(near_back.T, far_back)
    far_t = far_back.T
    dec_sent = dec_grads(near_t, far_t, top_acts, aux_acts, (1, 3), bf16)
    moments = moments.reshape(narrow_count, 2, rows_each, own_latents)
    enc_moment_own = moments[:, 0].reshape(model_width, own_latents)
    dec_moment_own = moments[:, 1].reshape(model_width, own_latents)
    top_acts, dec_sent = tie(top_acts, dec_sent)
    dec_keep = dec_grads(near_t, far_t, top_acts, aux_acts, (0, 2), f32)
    far_back, dec_keep = tie(far_back, dec_keep)
    enc_sent = enc_grads(
        encoder_t, near_back, far_back, codes, dead_here, dec_parts[1::2], (1, 3), bf16
    )
    far_back, enc_sent = tie(far_back, enc_sent)
    enc_keep = enc_grads(
        encoder_t, near_back, far_back, codes, dead_here, dec_parts[::2], (0, 2), f32
    )
    dec_gots = [swap(sent, "chip", order[-1]) for order, sent in zip(orders, dec_sent)]
    dec_gots, enc_sent = tie(dec_gots, enc_sent)
    enc_gots = [swap(sent, "chip", order[-1]) for order, sent in zip(orders, enc_sent)]
    dec_grad, _ = scatter_chips(dec_keep, dec_gots)
    def sum_gram(part, vector, fill):
        half = model_width // 2
        rows = half // chips
        spare = jnp.zeros((14, model_width), bf16)

        def pack(block, vector):
            lines = [line[None] for line in split_bf(vector)]
            return jnp.concatenate([block.astype(bf16), *lines, spare], 0)

        def unpack(got):
            got = got.astype(f32)
            return got[:-16], got[-16] + got[-15]

        def block_of(value, index, count):
            return lax.dynamic_slice_in_dim(value, index * count, count, 0)

        def exchange(sents, axis):
            got = [swap(sent, axis, k + 1) for k, sent in enumerate(sents)]
            return fill(sents, got)

        sent = pack(block_of(part, 1 - core_pos, half), vector)
        (got,) = exchange([sent], "core")
        got, more = unpack(got)
        part, vector = block_of(part, core_pos, half) + got, vector + more
        total = block_of(part, chip_pos, rows)
        sents = [pack(block_of(part, chip_pos ^ k, rows), vector) for k in range(1, chips)]
        for got in exchange(sents, "chip"):
            got, more = unpack(got)
            total, vector = total + got, vector + more
        for got in exchange([pack(total, vector)] * (narrow_count - 1), "narrow"):
            got, more = unpack(got)
            total, vector = total + got, vector + more
        total = total.astype(bf16)
        near = jnp.stack([total, *exchange([total] * (chips - 1), "chip")])
        (far,) = exchange([near], "core")
        return near, far, vector

    dec_own_next = (MOMENTUM * dec_moment_own.astype(f32) + dec_grad).astype(bf16)
    dec_rows, dec_own_next = tie(dec_grad.astype(bf16), dec_own_next)
    dec_rows = rows_of(dec_rows)
    dec_gram = lax.dot_general(
        dec_own_next, dec_own_next, to_latents, preferred_element_type=f32
    )
    dec_gram, enc_gots, enc_keep = tie(dec_gram, enc_gots, enc_keep)
    stages = []
    enc_grad = encb_grad = None

    def dec_note(sents, got):
        nonlocal enc_grad, encb_grad, dec_rows
        if not stages:
            enc_grad, encb_grad = scatter_chips(enc_keep, enc_gots)
        if len(stages) == 2:
            got, enc_grad, dec_rows = tie(got, enc_grad, dec_rows)
        stages.append(got)
        return got

    dec_near, dec_far, _ = sum_gram(
        dec_gram,
        jnp.zeros((model_width,), f32),
        dec_note,
    )
    bias_term = jnp.sum(back_rows[:, :model_width], 0, dtype=f32) - jnp.dot(
        enc_own.astype(f32),
        encb_grad,
        precision=HIGH_PRECISION,
    )

    enc_own_next = (MOMENTUM * enc_moment_own.astype(f32) + enc_grad).astype(bf16)
    enc_gram = lax.dot_general(
        enc_own_next, enc_own_next, to_latents, preferred_element_type=f32
    )
    enc_gram, dec_near = lax.optimization_barrier((enc_gram, dec_near))
    enc_momenta = lax.all_gather(enc_own_next, "narrow")
    progress = []

    def dec_fill(sents, got):
        step = len(progress)
        if step == 0:
            early, _ = tie(dec_near, sents)
            state = series_start(place, early, dec_far)
        else:
            state = series_next(step, progress[-1])
        got, state = lax.optimization_barrier((got, state))
        progress.append(state)
        return got

    enc_near, enc_far, grad_decb = sum_gram(enc_gram, bias_term, dec_fill)
    dec_factor = progress[-1][0]
    dec_ortho = rows_of(
        jnp.dot(dec_factor, dec_own_next, preferred_element_type=f32).astype(bf16)
    )
    step_scale = MUON_RATE * 0.2 * math.sqrt(max(D, L))
    dec_next = MOMENTUM * dec_moment_t + dec_rows.astype(f32)
    dec_new = dec_weight_t * (1.0 - MUON_RATE * DECAY) - step_scale * dec_ortho.astype(f32)
    dec_copy = dec_new.astype(bf16)
    state = series_start(place, enc_near, enc_far)
    for step in range(1, NS_STEPS):
        state = series_next(step, state)
    enc_new, enc_next, enc_copy = finish(place, state[0], enc_momenta, enc_weight)
    encb_new, encb_one, encb_two = adam_update(enc_bias, encb_grad, encb_first, encb_second)
    decb_new, decb_one, decb_two = adam_update(decoder_bias, grad_decb, decb_first, decb_second)
    return (
        token_loss,
        enc_new,
        enc_next,
        enc_copy,
        dec_new.T,
        dec_next.T,
        dec_copy.T,
        encb_new,
        encb_one,
        encb_two,
        decb_new,
        decb_one,
        decb_two,
    )


def solution(mesh):
    wide, narrow = mesh.devices.shape
    fine = Mesh(mesh.devices.reshape(wide // 2, 2, narrow), ("chip", "core", "narrow"))
    placed = (
        P(("chip", "core", "narrow")),
        P(("chip", "core", "narrow")),
        P(("chip", "core", "narrow"), None),
        P(("chip", "core", "narrow"), None),
        P(),
        P(("chip", "core"), None),
        P(),
        P(),
        P(),
        P(),
        P(),
        P(),
        P(),
        P("narrow", ("chip", "core")),
        P(("chip", "core", "narrow")),
        P(("chip", "core"), "narrow"),
        P(),
        P("narrow", ("chip", "core")),
        P(("chip", "core"), "narrow"),
        P(("chip", "core", "narrow")),
        P(("chip", "core", "narrow")),
        P(),
        P(),
    )
    return jax.shard_map(
        local,
        mesh=fine,
        in_specs=placed,
        out_specs=(
            P(("chip", "core", "narrow")),
            P("narrow", ("chip", "core")),
            P("narrow", ("chip", "core")),
            P("narrow", ("chip", "core")),
            P(("chip", "core"), "narrow"),
            P(("chip", "core"), "narrow"),
            P(("chip", "core"), "narrow"),
            P(("chip", "core", "narrow")),
            P(("chip", "core", "narrow")),
            P(("chip", "core", "narrow")),
            P(),
            P(),
            P(),
        ),
        check_vma=False,
    )
```

```python
import functools
import math

import jax
import jax.numpy as jnp
from jax import lax
from jax.experimental import pallas as pl
from jax.experimental.pallas import tpu as pltpu
from jax.sharding import Mesh
from jax.sharding import PartitionSpec as P

D = 768
HEAD_DIM = 64
L = 32768
NS_STEPS = 5
STEP = 10


HIGH_PRECISION = lax.Precision.HIGHEST
AUX_COEF = 1.0 / 32.0
EPS_NORM = 1e-05
NS_EPS = 1e-07
QA = 3.4445
QB = -4.775
QC = 2.0315
MOMENTUM = 0.95
MUON_RATE = 0.1
DECAY = 0.1
BIAS_RATE = 0.3
BETA_ONE = 0.9
BETA_TWO = 0.999
ADAM_EPS = 1e-08


def layer_norm(value, gain, shift):
    row_mean = jnp.mean(value, -1, keepdims=True)
    centred = value - row_mean
    row_var = jnp.mean(centred * centred, -1, keepdims=True)
    return centred * lax.rsqrt(row_var + EPS_NORM) * gain + shift


def frozen_block(start, ctx_length, ln_gains, frozen_bias, w_qkv, w_proj, w_fc, w_out):
    row_count, model_width = start.shape
    head_count = model_width // HEAD_DIM
    ff_width = w_fc.shape[1]
    shifts = frozen_bias[: 2 * model_width].reshape(2, model_width)
    b_qkv = frozen_bias[2 * model_width : 5 * model_width]
    b_proj = frozen_bias[5 * model_width : 6 * model_width]
    b_fc = frozen_bias[6 * model_width : 6 * model_width + ff_width]
    b_out = frozen_bias[6 * model_width + ff_width :]
    normed = layer_norm(start, ln_gains[0], shifts[0]).astype(jnp.bfloat16)
    qkv_rows = (jnp.dot(normed, w_qkv, preferred_element_type=jnp.float32) + b_qkv).astype(
        jnp.bfloat16
    )
    head_split = qkv_rows.reshape(row_count, 3, head_count, HEAD_DIM)
    scores = jnp.einsum(
        "qhd,khd->hqk", head_split[:, 0], head_split[:, 1], preferred_element_type=jnp.float32
    ) * HEAD_DIM ** (-0.5)
    positions = jnp.arange(row_count)
    allowed = (positions[None, :] <= positions[:, None]) & (positions[None, :] < ctx_length)
    attn_probs = jax.nn.softmax(jnp.where(allowed[None], scores, -1e30), axis=-1).astype(
        jnp.bfloat16
    )
    mixed = jnp.einsum(
        "hqk,khd->qhd", attn_probs, head_split[:, 2], preferred_element_type=jnp.float32
    )
    mixed = mixed.reshape(row_count, model_width).astype(jnp.bfloat16)
    hidden = start + jnp.dot(mixed, w_proj, preferred_element_type=jnp.float32) + b_proj
    normed_two = layer_norm(hidden, ln_gains[1], shifts[1]).astype(jnp.bfloat16)
    inner_acts = jax.nn.gelu(
        jnp.dot(normed_two, w_fc, preferred_element_type=jnp.float32) + b_fc, approximate=True
    ).astype(jnp.bfloat16)
    return (hidden + jnp.dot(inner_acts, w_out, preferred_element_type=jnp.float32) + b_out).astype(
        jnp.bfloat16
    )


def split_bf(value):
    high = value.astype(jnp.bfloat16)
    return high, (value - high.astype(jnp.float32)).astype(jnp.bfloat16)


def row_blocks(size, body):
    block = 256

    def step(index, carry):
        body(pl.ds(pl.multiple_of(index * block, block), block), index * block)
        return carry

    lax.fori_loop(0, size // block, step, 0)


def eye_rows(start, size):
    rows = lax.broadcasted_iota(jnp.int32, (256, size), 0) + start
    cols = lax.broadcasted_iota(jnp.int32, (256, size), 1)
    return (rows == cols).astype(jnp.float32)


def dot_f32(a, b):
    return jnp.dot(a, b, preferred_element_type=jnp.float32)


def store_split(pair, rows, value):
    pair[0][rows, :], pair[1][rows, :] = split_bf(value)


def three(left, right, rows):
    high, low = left[0][rows, :], left[1][rows, :]
    return dot_f32(high, right[0][...]) + (
        dot_f32(high, right[1][...]) + dot_f32(low, right[0][...])
    )


def series_step(gram, poly, half, out, old, new, step):
    size = gram[0].shape[0]
    last = step == NS_STEPS - 1
    exact_square = step >= 3

    def poly_rows(rows, start):
        here = gram[0][rows, :].astype(jnp.float32) + gram[1][rows, :].astype(jnp.float32)
        if exact_square:
            square = three(gram, gram, rows)
        else:
            square = dot_f32(gram[0][rows, :], gram[0][...])
        store_split(poly, rows, QA * eye_rows(start, size) + QB * here + QC * square)

    def half_rows(rows, start):
        store_split(half, rows, three(gram, poly, rows))

    def gram_rows(rows, start):
        store_split(out, rows, three(poly, half, rows))

    def product_rows(rows, start):
        new[rows, :] = dot_f32(poly[0][rows, :], old[...]).astype(jnp.bfloat16)

    row_blocks(size, poly_rows)
    if not last:
        row_blocks(size, half_rows)
        row_blocks(size, gram_rows)
    if step > 0:
        row_blocks(size, product_rows)


def first_kernel(place_ref, near_ref, far_ref, o_hi, o_lo, q_ref, total, *scratch):
    size = total.shape[0]
    chips, rows_each = near_ref.shape[:2]
    chip, core = place_ref[0], place_ref[1]
    gram, poly, half = scratch[:2], scratch[2:4], scratch[4:6]
    for offset in range(chips):
        for side, source in enumerate((near_ref, far_ref)):
            first = jnp.bitwise_xor(core, side) * (size // 2)
            first = first + jnp.bitwise_xor(chip, offset) * rows_each
            total[pl.ds(pl.multiple_of(first, 8), rows_each), :] = source[offset].astype(
                jnp.float32
            )

    def trace_part(index, value):
        start = pl.multiple_of(index * 256, 256)
        return value + jnp.sum(total[pl.ds(start, 256), :] * eye_rows(start, size))

    trace_sum = lax.fori_loop(0, size // 256, trace_part, jnp.zeros((), jnp.float32))
    scale = 1.0 / (jnp.sqrt(jnp.full((1, 1), trace_sum)) + NS_EPS)

    def load_rows(rows, start):
        store_split(gram, rows, total[rows, :] * (scale * scale))

    row_blocks(size, load_rows)
    series_step(gram, poly, half, (o_hi, o_lo), None, None, 0)

    def product_rows(rows, start):
        value = poly[0][rows, :].astype(jnp.float32) + poly[1][rows, :].astype(jnp.float32)
        q_ref[rows, :] = (value * scale).astype(jnp.bfloat16)

    row_blocks(size, product_rows)


def middle_kernel(step, g_hi, g_lo, q_ref, o_hi, o_lo, out_ref, *scratch):
    series_step(
        (g_hi, g_lo), scratch[:2], scratch[2:4], (o_hi, o_lo), q_ref, out_ref, step
    )


def last_kernel(g_hi, g_lo, q_ref, out_ref, *scratch):
    series_step((g_hi, g_lo), scratch[:2], None, None, q_ref, out_ref, NS_STEPS - 1)


def square_call(kernel, outs, scratch, passes, *operands):
    size = operands[-1].shape[-1]
    whole = pl.BlockSpec(memory_space=pltpu.VMEM)
    specs = [whole] * len(operands)
    if operands[0].ndim == 1:
        specs[0] = pl.BlockSpec(memory_space=pltpu.SMEM)
    square = jax.ShapeDtypeStruct((size, size), jnp.bfloat16)
    return pl.pallas_call(
        kernel,
        out_shape=[square] * outs,
        in_specs=specs,
        out_specs=[whole] * outs,
        scratch_shapes=[pltpu.VMEM((size, size), kind) for kind in scratch],
        compiler_params=pltpu.CompilerParams(vmem_limit_bytes=40 * 2**20),
        cost_estimate=pl.CostEstimate(
            flops=passes * size**3 // 16, bytes_accessed=size * size // 2, transcendentals=0
        ),
    )(*operands)


def series_start(place, near, far):
    bf16 = jnp.bfloat16
    return square_call(first_kernel, 3, [jnp.float32] + [bf16] * 6, 8, place, near, far)


def series_next(step, state):
    bf16 = jnp.bfloat16
    if step == NS_STEPS - 1:
        return square_call(last_kernel, 1, [bf16] * 2, 4, *state)
    kernel = functools.partial(middle_kernel, step)
    return square_call(kernel, 3, [bf16] * 4, 8 if step < 3 else 10, *state)


def code_kernel(shifts, place_ref, ids_ref, out_ref, high, low, stage):
    wide_shift, own_shift, top_count, orders = shifts
    batch, groups = stage.shape[:2]
    rows, picks = ids_ref.shape
    bf16, f32 = jnp.bfloat16, jnp.float32
    chip, core, narrow = place_ref[0], place_ref[1], place_ref[2]
    latent_count = out_ref.shape[1]
    half_shift = own_shift - 1

    ids = ids_ref[...]
    owner = lax.shift_right_logical(ids, wide_shift)
    within = jnp.bitwise_and(ids, (1 << wide_shift) - 1)
    mine = (lax.shift_right_logical(within, own_shift) == narrow) & (
        jnp.bitwise_and(owner, 1) == core
    )
    inner = jnp.bitwise_and(within, (1 << own_shift) - 1)
    offset = jnp.bitwise_xor(lax.shift_right_logical(owner, 1), chip)
    half = lax.shift_right_logical(inner, half_shift)
    spots = []
    for order in orders:
        spot = jnp.zeros_like(offset)
        for index, bit in enumerate(order[:-1]):
            spot = spot + jnp.where(jnp.bitwise_and(offset, bit) != 0, 1 << index, 0)
        sent = jnp.where(jnp.bitwise_and(offset, order[-1]) != 0, latent_count // 4, 0)
        spots.append(sent + lax.shift_left(spot, half_shift))
    column = (
        half * (latent_count // 2)
        + jnp.where(half == 0, spots[0], spots[1])
        + jnp.bitwise_and(inner, (1 << half_shift) - 1)
    )
    high[...] = jnp.where(mine, lax.shift_right_logical(column, 7), -1).astype(f32)
    low[...] = jnp.bitwise_and(column, 127).astype(f32)

    one, zero = jnp.ones((16, picks), bf16), jnp.zeros((16, picks), bf16)
    places = lax.broadcasted_iota(jnp.int32, (16, picks), 1)
    kinds = jnp.where(places < top_count, 1.0, 2.0).astype(bf16)
    steps = lax.broadcasted_iota(jnp.int32, (16, picks), 0).astype(f32).astype(bf16)

    def hot(row, count, value):
        row = jnp.broadcast_to(row, (16, picks)).astype(bf16)
        parts = [
            jnp.where(steps + jnp.asarray(16 * part, bf16) == row, value, zero)
            for part in range(max(1, count // 16))
        ]
        return jnp.concatenate(parts, 0).astype(jnp.float8_e4m3fn)

    def one_batch(index, carry):
        first = pl.multiple_of(index * batch, batch)
        for token in range(batch):
            row = pl.ds(first + token, 1)
            codes = lax.dot_general(
                hot(high[row, :], groups, kinds),
                hot(low[row, :], 128, one),
                (((1,), (1,)), ((), ())),
                preferred_element_type=f32,
            )
            stage[token] = codes[:groups]
        for group in range(groups):
            lanes = slice(group * 128, (group + 1) * 128)
            out_ref[pl.ds(first, batch), lanes] = stage[:, group, :].astype(bf16)
        return carry

    lax.fori_loop(0, rows // batch, one_batch, 0)


def kind_codes(place, ids, latent_count, sizes):
    wide_latents, own_latents, top_count, orders = sizes
    row_total, pick_total = ids.shape
    rows = min(128, row_total)
    shifts = (wide_latents.bit_length() - 1, own_latents.bit_length() - 1, top_count, orders)
    return pl.pallas_call(
        functools.partial(code_kernel, shifts),
        grid=(row_total // rows,),
        out_shape=jax.ShapeDtypeStruct((row_total, latent_count), jnp.bfloat16),
        in_specs=[
            pl.BlockSpec(memory_space=pltpu.SMEM),
            pl.BlockSpec((rows, pick_total), lambda i: (i, 0)),
        ],
        out_specs=pl.BlockSpec((rows, latent_count), lambda i: (i, 0)),
        scratch_shapes=[
            pltpu.VMEM((rows, pick_total), jnp.float32),
            pltpu.VMEM((rows, pick_total), jnp.float32),
            pltpu.VMEM((32, latent_count // 128, 128), jnp.float32),
        ],
        compiler_params=pltpu.CompilerParams(vmem_limit_bytes=40 * 2**20),
        cost_estimate=pl.CostEstimate(
            flops=row_total * latent_count,
            bytes_accessed=row_total * pick_total,
            transcendentals=0,
        ),
    )(place, ids)


def join_rows(sources, target):
    rows = sources[0].shape[0]
    for index, source in enumerate(sources):
        target[index * rows : (index + 1) * rows, :] = source[...]


def pick_copy(step, count, sources, target):
    for index, source in enumerate(sources):

        @pl.when(step // count == index)
        def _(source=source):
            target[...] = source[...]


def forward_kernel(count, x_ref, dead_ref, *refs):
    code_parts, encs, decs = refs[:4], refs[4:8], refs[8:12]
    top_ref, aux_ref, far_ref, near_ref = refs[12:16]
    codes_ref, enc, dec, acc_top, acc_aux = refs[16:]
    join_rows(code_parts, codes_ref)
    step = pl.program_id(0)
    rows_all, width = x_ref.shape
    block = min(1024, rows_all)
    pick_copy(step, count, encs, enc)
    pick_copy(step, count, decs, dec)

    @pl.when(step == 0)
    def _():
        acc_top[...] = jnp.zeros_like(acc_top)
        acc_aux[...] = jnp.zeros_like(acc_aux)

    bias = enc[pl.ds(width, 16), :].astype(jnp.float32)[:1]
    to_features = (((1,), (1,)), ((), ()))

    def one(index, carry):
        rows = pl.ds(pl.multiple_of(index * block, block), block)
        pre = dot_f32(x_ref[rows, :], enc[pl.ds(0, width), :]) + bias
        codes = codes_ref[rows, :]
        zero = jnp.zeros(codes.shape, jnp.bfloat16)
        top = jnp.where(codes == 1.0, pre.astype(jnp.bfloat16), zero)
        aux = jnp.where(codes == 2.0, (pre * dead_ref[...]).astype(jnp.bfloat16), zero)
        top_ref[rows, :] = top
        aux_ref[rows, :] = aux
        acc_top[rows, :] += lax.dot_general(
            top, dec[...], to_features, preferred_element_type=jnp.float32
        )
        acc_aux[rows, :] += lax.dot_general(
            aux, dec[...], to_features, preferred_element_type=jnp.float32
        )
        return carry

    lax.fori_loop(0, rows_all // block, one, 0)

    @pl.when(step == pl.num_programs(0) - 1)
    def _():
        half = rows_all // 2
        for first, acc in ((0, acc_top), (width, acc_aux)):
            near_ref[:, first : first + width] = acc[pl.ds(0, half), :]
            far_ref[:, first : first + width] = acc[pl.ds(half, half), :].astype(jnp.bfloat16)


def part_specs(shape, axis, block, count, starts):
    specs = []
    for index, first in enumerate(starts):

        def place(step, index=index, first=first):
            spot = jnp.clip(step - index * count, 0, count - 1)
            return (spot + first, 0) if axis == 0 else (0, spot + first)

        size = (block, shape[1]) if axis == 0 else (shape[0], block)
        specs.append(pl.BlockSpec(size, place))
    return specs


def forward(x, codes, dead, encs, decs):
    rows, width = x.shape
    acts_shape = (rows, dead.shape[1])
    quarter = encs[0].shape[1]
    block = min(512, quarter)
    count = quarter // block
    lanes = pl.BlockSpec((rows, block), lambda step: (0, step))
    fixed = lambda shape: pl.BlockSpec(shape, lambda step: (0, 0))
    bf16, f32 = jnp.bfloat16, jnp.float32
    half_shape = (rows // 2, 2 * width)
    return pl.pallas_call(
        functools.partial(forward_kernel, count),
        grid=(4 * count,),
        out_shape=[
            jax.ShapeDtypeStruct(acts_shape, bf16),
            jax.ShapeDtypeStruct(acts_shape, bf16),
            jax.ShapeDtypeStruct(half_shape, bf16),
            jax.ShapeDtypeStruct(half_shape, f32),
        ],
        in_specs=[fixed(x.shape), pl.BlockSpec((1, block), lambda step: (0, step))]
        + [pl.BlockSpec((rows // 4, block), lambda step: (0, step))] * 4
        + part_specs(encs[0].shape, 1, block, count, (0, 0, 0, 0))
        + part_specs(decs[0].shape, 1, block, count, (0, 0, 0, 0)),
        out_specs=[lanes, lanes, fixed(half_shape), fixed(half_shape)],
        scratch_shapes=[
            pltpu.VMEM((rows, block), bf16),
            pltpu.VMEM((width + 16, block), bf16),
            pltpu.VMEM((width, block), bf16),
            pltpu.VMEM((rows, width), f32),
            pltpu.VMEM((rows, width), f32),
        ],
        compiler_params=pltpu.CompilerParams(vmem_limit_bytes=58 * 2**20),
        cost_estimate=pl.CostEstimate(
            flops=2 * rows * width * dead.shape[1],
            bytes_accessed=6 * rows * dead.shape[1],
            transcendentals=0,
        ),
    )(x, dead, *codes, *encs, *decs)


def store_part(count, refs, rows, value):
    step = pl.program_id(0)
    for index, ref in enumerate(refs):

        @pl.when(step // count == index)
        def _(ref=ref):
            ref[rows, :] = value.astype(ref.dtype)


def dec_grad_kernel(count, near_r, near_a, far_r, far_a, top_ref, aux_ref, *outs):
    half = near_r.shape[1]

    def one(index, carry):
        rows = pl.ds(pl.multiple_of(index * 768, 768), 768)
        value = dot_f32(near_r[rows, :], top_ref[:half, :])
        value = value + dot_f32(near_a[rows, :], aux_ref[:half, :])
        value = value + dot_f32(far_r[rows, :], top_ref[half:, :])
        value = value + dot_f32(far_a[rows, :], aux_ref[half:, :])
        store_part(count, outs, rows, value)
        return carry

    lax.fori_loop(0, near_r.shape[0] // 768, one, 0)


def dec_grads(near_t, far_t, top_acts, aux_acts, quarters, kind):
    width = near_t.shape[0] // 2
    rows, latents = top_acts.shape
    quarter = latents // 4
    block = min(512, quarter)
    count = quarter // block

    def lanes(step):
        return (0, jnp.where(step < count, quarters[0], quarters[1] - 1) * count + step)

    acts = pl.BlockSpec((rows, block), lanes)
    shape = (width, quarter)
    return pl.pallas_call(
        functools.partial(dec_grad_kernel, count),
        grid=(2 * count,),
        out_shape=[jax.ShapeDtypeStruct(shape, kind)] * 2,
        in_specs=[
            pl.BlockSpec((width, rows // 2), lambda step: (0, 0)),
            pl.BlockSpec((width, rows // 2), lambda step: (1, 0)),
            pl.BlockSpec((width, rows // 2), lambda step: (0, 0)),
            pl.BlockSpec((width, rows // 2), lambda step: (1, 0)),
            acts,
            acts,
        ],
        out_specs=part_specs(shape, 1, block, count, (0, 0)),
        compiler_params=pltpu.CompilerParams(vmem_limit_bytes=58 * 2**20),
        cost_estimate=pl.CostEstimate(
            flops=rows * width * quarter // 8, bytes_accessed=rows * quarter // 4, transcendentals=0
        ),
    )(near_t, near_t, far_t, far_t, top_acts, aux_acts)


def enc_grad_kernel(count, x_ref, near_ref, far_ref, dead_ref, *refs):
    code_parts, (dec_a, dec_b, out_a, out_b, dec, grads) = refs[:4], refs[4:]
    step = pl.program_id(0)
    pick_copy(step, count, (dec_a, dec_b), dec)
    width, latents = dec.shape
    quarter = code_parts[0].shape[0]
    total = jnp.zeros((1, latents), jnp.float32)
    for index, back_ref in enumerate((near_ref, far_ref)):
        top = dot_f32(back_ref[:, :width], dec[...])
        aux = dot_f32(back_ref[:, width:], dec[...]) * dead_ref[...]
        for part in range(2):
            codes = code_parts[2 * index + part][...].astype(jnp.float32)
            lines = slice(part * quarter, (part + 1) * quarter)
            value = jnp.where(codes == 2.0, aux[lines], 0.0)
            value = jnp.where(codes == 1.0, top[lines], value).astype(jnp.bfloat16)
            first = (2 * index + part) * quarter
            grads[first : first + quarter, :] = value
            total = total + jnp.sum(value.astype(jnp.float32), 0, keepdims=True)

    def two(index, carry):
        rows = pl.ds(pl.multiple_of(index * 768, 768), 768)
        store_part(count, (out_a, out_b), rows, dot_f32(x_ref[rows, :], grads[...]))
        return carry

    lax.fori_loop(0, width // 768, two, 0)
    lines = lax.broadcasted_iota(jnp.int32, (16, latents), 0)
    if out_a.dtype == jnp.bfloat16:
        high = total.astype(jnp.bfloat16).astype(jnp.float32)
        lines = jnp.where(lines == 0, high, jnp.where(lines == 1, total - high, 0.0))
    else:
        lines = jnp.where(lines == 0, total, 0.0)
    store_part(count, (out_a, out_b), pl.ds(width, 16), lines)


def enc_grads(x_t, near, far, codes, dead, parts, quarters, kind):
    width, rows = x_t.shape
    quarter = dead.shape[1] // 4
    block = min(512, quarter)
    count = quarter // block

    def lanes(step):
        return (0, jnp.where(step < count, quarters[0], quarters[1] - 1) * count + step)

    shape = (width + 16, quarter)
    return pl.pallas_call(
        functools.partial(enc_grad_kernel, count),
        grid=(2 * count,),
        out_shape=[jax.ShapeDtypeStruct(shape, kind)] * 2,
        in_specs=[
            pl.BlockSpec(x_t.shape, lambda step: (0, 0)),
            pl.BlockSpec(near.shape, lambda step: (0, 0)),
            pl.BlockSpec(far.shape, lambda step: (0, 0)),
            pl.BlockSpec((1, block), lanes),
        ]
        + [pl.BlockSpec((rows // 4, block), lanes)] * 4
        + part_specs(parts[0].shape, 1, block, count, (0, 0)),
        out_specs=part_specs(shape, 1, block, count, (0, 0)),
        scratch_shapes=[
            pltpu.VMEM((width, block), jnp.bfloat16),
            pltpu.VMEM((rows, block), jnp.bfloat16),
        ],
        compiler_params=pltpu.CompilerParams(vmem_limit_bytes=58 * 2**20),
        cost_estimate=pl.CostEstimate(
            flops=rows * width * quarter // 8, bytes_accessed=rows * quarter // 4, transcendentals=0
        ),
    )(x_t, near, far, dead, *codes, *parts)


def finish_kernel(place_ref, factor_ref, momentum_ref, weight_ref, *outs):
    new_ref, next_ref, copy_ref = outs
    rows = factor_ref.shape[0]
    f32 = jnp.float32
    momentum = momentum_ref[0]
    kept = momentum_ref[0, pl.ds(pl.multiple_of(place_ref[2] * rows, 16), rows), :].astype(f32)
    ortho = dot_f32(factor_ref[...], momentum)
    next_ref[...] = kept
    step_scale = MUON_RATE * 0.2 * math.sqrt(max(D, L))
    value = weight_ref[...] * (1.0 - MUON_RATE * DECAY) - step_scale * ortho
    new_ref[...] = value
    copy_ref[...] = value.astype(jnp.bfloat16)


def finish(place, factor, momenta, weight):
    count, width, block = momenta.shape
    rows = weight.shape[0]
    part = pl.BlockSpec((rows, block), lambda step, place: (0, step))
    return pl.pallas_call(
        finish_kernel,
        grid_spec=pltpu.PrefetchScalarGridSpec(
            num_scalar_prefetch=1,
            grid=(count,),
            in_specs=[
                pl.BlockSpec((rows, width), lambda step, place: (place[2], 0)),
                pl.BlockSpec((1, width, block), lambda step, place: (step, 0, 0)),
                part,
            ],
            out_specs=[part] * 3,
        ),
        out_shape=[
            jax.ShapeDtypeStruct(weight.shape, jnp.float32),
            jax.ShapeDtypeStruct(weight.shape, jnp.float32),
            jax.ShapeDtypeStruct(weight.shape, jnp.bfloat16),
        ],
        compiler_params=pltpu.CompilerParams(vmem_limit_bytes=58 * 2**20),
        cost_estimate=pl.CostEstimate(
            flops=2 * rows * width * block * count,
            bytes_accessed=8 * rows * block * count,
            transcendentals=0,
        ),
    )(place, factor, momenta, weight)


def adam_update(param, grad, first, second):
    first = BETA_ONE * first + (1.0 - BETA_ONE) * grad
    second = BETA_TWO * second + (1.0 - BETA_TWO) * grad * grad
    denom = jnp.sqrt(second / (1.0 - BETA_TWO**STEP)) + ADAM_EPS
    return (param - BIAS_RATE * (first / (1.0 - BETA_ONE**STEP)) / denom, first, second)


def local(
    token_ids,
    lengths,
    top_ids,
    aux_ids,
    dead_set,
    token_table,
    position_table,
    ln_gains,
    frozen_bias,
    w_qkv,
    w_proj,
    w_fc,
    w_out,
    enc_weight,
    enc_bias,
    dec_weight,
    decoder_bias,
    enc_moment,
    dec_moment,
    encb_first,
    encb_second,
    decb_first,
    decb_second,
):
    chips = lax.axis_size("chip")
    narrow_count = lax.axis_size("narrow")
    wide_count = 2 * chips
    wide = ("chip", "core")
    chip_pos = lax.axis_index("chip")
    core_pos = lax.axis_index("core")
    wide_pos = 2 * chip_pos + core_pos
    narrow_pos = lax.axis_index("narrow")
    row_count = token_ids.shape[0]
    model_width = token_table.shape[1]
    wide_latents = enc_weight.shape[1]
    own_latents = wide_latents // narrow_count
    half_latents = own_latents // 2
    latent_count = chips * own_latents
    core_rows = narrow_count * row_count
    bf16, f32 = jnp.bfloat16, jnp.float32
    to_latents = (((1,), (1,)), ((), ()))
    over_rows = (((0,), (0,)), ((), ()))
    place = jnp.stack([chip_pos, core_pos, narrow_pos]).astype(jnp.int32)
    bits = [1 << bit for bit in range(chips.bit_length() - 1)]
    orders = (bits, bits[::-1])

    tie = lambda *values: lax.optimization_barrier(values)

    def swap(value, axis, offset):
        count = lax.axis_size(axis)
        return lax.ppermute(value, axis, [(spot, spot ^ offset) for spot in range(count)])

    def spread_narrow(value):
        parts = [value] + [swap(value, "narrow", k) for k in range(1, narrow_count)]
        return jnp.concatenate(parts, 0)

    def rows_to_latents(value):
        return lax.all_to_all(value, "narrow", split_axis=1, concat_axis=0, tiled=True)

    def rows_of(value):
        return lax.all_to_all(value, "narrow", split_axis=0, concat_axis=1, tiled=True)

    def gather_start(own):
        helds, gots = [], []
        for part, order in enumerate(orders):
            held = own[:, part * half_latents : (part + 1) * half_latents]
            for bit in order[:-2]:
                held = jnp.concatenate([held, swap(held, "chip", bit)], 1)
            helds.append(held)
            gots.append(swap(held, "chip", order[-2]))
        return helds, gots

    def gather_join(helds, gots):
        return [jnp.concatenate(pair, 1) for pair in zip(helds, gots)]

    def gather_end(halves):
        pieces = []
        for held, order in zip(halves, orders):
            pieces += [held, swap(held, "chip", order[-1])]
        return pieces

    def scatter_chips(keeps, gots):
        results, sums = [], []
        for order, held, got in zip(orders, keeps, gots):
            held = held + got.astype(f32)
            for bit in reversed(order[:-1]):
                lower, upper = jnp.split(held, 2, 1)
                sent = upper[:model_width].astype(bf16)
                if held.shape[0] > model_width:
                    lines = split_bf(upper[model_width] + upper[model_width + 1])
                    spare = jnp.zeros((14, upper.shape[1]), bf16)
                    sent = jnp.concatenate([sent, *(line[None] for line in lines), spare], 0)
                held = lower + swap(sent, "chip", bit).astype(f32)
            results.append(held[:model_width])
            if held.shape[0] > model_width:
                sums.append(held[model_width] + held[model_width + 1])
        return jnp.concatenate(results, 1), jnp.concatenate(sums) if sums else None

    vocab_dev = token_table.shape[0]
    every_ids = lax.all_gather(token_ids, wide, axis=0, tiled=False).reshape(wide_count, row_count)
    every_ids = jnp.concatenate(
        [
            lax.dynamic_slice_in_dim(every_ids, wide_pos ^ offset, 1, 0)
            for offset in range(wide_count)
        ],
        1,
    )[0]
    local_ids = every_ids - wide_pos * vocab_dev
    inside = (local_ids >= 0) & (local_ids < vocab_dev)
    looked = jnp.take(token_table, jnp.clip(local_ids, 0, vocab_dev - 1), axis=0)
    looked = jnp.where(inside[:, None], looked, jnp.zeros((), bf16))
    dec_weight_t, dec_moment_t = dec_weight.T, dec_moment.T
    rows_each = enc_weight.shape[0]
    enc_own = rows_to_latents(enc_weight.astype(bf16))
    picks = jnp.concatenate([top_ids, aux_ids], 1)
    near_picks = spread_narrow(picks)
    far_picks = swap(near_picks, "core", 1)

    looked = looked.reshape(chips, 2, row_count, model_width)
    looked = looked[:, 0] + swap(looked[:, 1], "core", 1)
    embedded = looked[0].astype(f32)
    for k in range(1, chips):
        embedded = embedded + swap(looked[k], "chip", k).astype(f32)

    bias_rows = jnp.concatenate(
        [enc_bias.astype(bf16)[None], jnp.zeros((15, own_latents), bf16)], 0
    )
    enc_own, embedded = tie(enc_own, embedded)
    dec_cast, enc_own = tie(dec_weight_t.astype(bf16), enc_own)
    dec_own = rows_to_latents(dec_cast)
    enc_helds, enc_halves = gather_start(jnp.concatenate([enc_own, bias_rows], 0))

    dead_here = jnp.stack(
        [
            lax.dynamic_slice_in_dim(
                dead_set,
                (2 * (chip_pos ^ offset) + core_pos) * wide_latents + narrow_pos * own_latents,
                own_latents,
            )
            for offset in range(chips)
        ]
    )
    places = [0]
    dead_parts = []
    for part, order in enumerate(orders):
        places = [0]
        for bit in order:
            places = places + [spot ^ bit for spot in places]
        for spot in places:
            dead_parts.append(dead_here[spot, part * half_latents : (part + 1) * half_latents])
    dead_here = jnp.concatenate(dead_parts)[None].astype(f32)
    sizes = (wide_latents, own_latents, top_ids.shape[1], orders)
    start = embedded + position_table[:row_count].astype(f32)
    ctx_length = lengths[0]
    inputs = frozen_block(start, ctx_length, ln_gains, frozen_bias, w_qkv, w_proj, w_fc, w_out)
    counted = (jnp.arange(row_count) < ctx_length).astype(f32)
    near_picks, inputs, enc_halves, dead_here, dec_own = tie(
        near_picks, inputs, enc_halves, dead_here, dec_own
    )
    enc_parts = gather_end(gather_join(enc_helds, enc_halves))
    got_inputs = [swap(inputs, "narrow", k) for k in range(1, narrow_count)]
    half_rows = core_rows // 2
    codes = [kind_codes(place, near_picks[:half_rows], latent_count, sizes)]
    enc_lasts = [enc_parts[1], enc_parts[3]]
    codes, got_inputs, enc_lasts = tie(codes, got_inputs, enc_lasts)
    enc_parts = [enc_parts[0], enc_lasts[0], enc_parts[2], enc_lasts[1]]
    near_picks, codes = tie(near_picks, codes)
    dec_helds, dec_halves = gather_start(dec_own)
    codes = [*codes, kind_codes(place, near_picks[half_rows:], latent_count, sizes)]
    dec_halves, codes = tie(dec_halves, codes)
    dec_parts = gather_end(gather_join(dec_helds, dec_halves))
    moments = jnp.concatenate([enc_moment.astype(bf16), dec_moment_t.astype(bf16)], 0)
    moments, got_inputs = tie(moments, got_inputs)
    moments = rows_to_latents(moments)
    near_inputs = jnp.concatenate([inputs, *got_inputs], 0)
    far_picks, codes = tie(far_picks, codes)
    codes = [*codes, kind_codes(place, far_picks[:half_rows], latent_count, sizes)]
    far_inputs, codes = tie(swap(near_inputs, "core", 1), codes)
    far_picks, codes = tie(far_picks, codes)
    codes = [*codes, kind_codes(place, far_picks[half_rows:], latent_count, sizes)]
    all_inputs = jnp.concatenate([near_inputs, far_inputs], 0)
    encoder_in = (all_inputs.astype(f32) - decoder_bias).astype(bf16)
    top_acts, aux_acts, far, near = forward(encoder_in, codes, dead_here, enc_parts, dec_parts)
    encoder_t = encoder_in.T
    far_got, encoder_t = tie(swap(far, "core", 1), encoder_t)
    rebuilt = near + far_got.astype(f32)
    rounded = rebuilt.astype(bf16)
    rebuilt = rebuilt[:row_count]
    for k in range(1, narrow_count):
        part = rounded[k * row_count : (k + 1) * row_count]
        rebuilt = rebuilt + swap(part, "narrow", k).astype(f32)
    target = inputs.astype(f32)
    reconstructed_input = rebuilt[:, :model_width] + decoder_bias
    auxiliary_reconstruction = rebuilt[:, model_width:]
    recon_error = target - reconstructed_input
    aux_gap = auxiliary_reconstruction - recon_error
    token_loss = (
        counted
        * (jnp.sum(recon_error * recon_error, 1) + AUX_COEF * jnp.sum(aux_gap * aux_gap, 1))
        / model_width
    )
    back_recon = 2.0 / model_width * counted[:, None] * (reconstructed_input - target)
    back_aux = 2.0 * AUX_COEF / model_width * counted[:, None] * aux_gap
    back_rows = jnp.concatenate([back_recon, back_aux], 1).astype(bf16)
    back_rows, moments = tie(back_rows, moments)
    near_back = spread_narrow(back_rows)
    far_back = swap(near_back, "core", 1)
    near_t, far_back = tie(near_back.T, far_back)
    far_t = far_back.T
    dec_sent = dec_grads(near_t, far_t, top_acts, aux_acts, (1, 3), bf16)
    moments = moments.reshape(narrow_count, 2, rows_each, own_latents)
    enc_moment_own = moments[:, 0].reshape(model_width, own_latents)
    dec_moment_own = moments[:, 1].reshape(model_width, own_latents)
    top_acts, dec_sent = tie(top_acts, dec_sent)
    dec_keep = dec_grads(near_t, far_t, top_acts, aux_acts, (0, 2), f32)
    far_back, dec_keep = tie(far_back, dec_keep)
    enc_sent = enc_grads(
        encoder_t, near_back, far_back, codes, dead_here, dec_parts[1::2], (1, 3), bf16
    )
    far_back, enc_sent = tie(far_back, enc_sent)
    enc_keep = enc_grads(
        encoder_t, near_back, far_back, codes, dead_here, dec_parts[::2], (0, 2), f32
    )
    dec_gots = [swap(sent, "chip", order[-1]) for order, sent in zip(orders, dec_sent)]
    dec_gots, enc_sent = tie(dec_gots, enc_sent)
    enc_gots = [swap(sent, "chip", order[-1]) for order, sent in zip(orders, enc_sent)]
    dec_grad, _ = scatter_chips(dec_keep, dec_gots)
    def sum_gram(part, vector, fill):
        half = model_width // 2
        rows = half // chips
        spare = jnp.zeros((14, model_width), bf16)

        def pack(block, vector):
            lines = [line[None] for line in split_bf(vector)]
            return jnp.concatenate([block.astype(bf16), *lines, spare], 0)

        def unpack(got):
            got = got.astype(f32)
            return got[:-16], got[-16] + got[-15]

        def block_of(value, index, count):
            return lax.dynamic_slice_in_dim(value, index * count, count, 0)

        def exchange(sents, axis):
            got = [swap(sent, axis, k + 1) for k, sent in enumerate(sents)]
            return fill(sents, got)

        sent = pack(block_of(part, 1 - core_pos, half), vector)
        (got,) = exchange([sent], "core")
        got, more = unpack(got)
        part, vector = block_of(part, core_pos, half) + got, vector + more
        total = block_of(part, chip_pos, rows)
        sents = [pack(block_of(part, chip_pos ^ k, rows), vector) for k in range(1, chips)]
        for got in exchange(sents, "chip"):
            got, more = unpack(got)
            total, vector = total + got, vector + more
        for got in exchange([pack(total, vector)] * (narrow_count - 1), "narrow"):
            got, more = unpack(got)
            total, vector = total + got, vector + more
        total = total.astype(bf16)
        near = jnp.stack([total, *exchange([total] * (chips - 1), "chip")])
        (far,) = exchange([near], "core")
        return near, far, vector

    dec_own_next = (MOMENTUM * dec_moment_own.astype(f32) + dec_grad).astype(bf16)
    dec_rows, dec_own_next = tie(dec_grad.astype(bf16), dec_own_next)
    dec_rows = rows_of(dec_rows)
    dec_gram = lax.dot_general(
        dec_own_next, dec_own_next, to_latents, preferred_element_type=f32
    )
    dec_gram, enc_gots, enc_keep = tie(dec_gram, enc_gots, enc_keep)
    stages = []
    enc_grad = encb_grad = None

    def dec_note(sents, got):
        nonlocal enc_grad, encb_grad, dec_rows
        if not stages:
            enc_grad, encb_grad = scatter_chips(enc_keep, enc_gots)
        if len(stages) == 2:
            got, enc_grad, dec_rows = tie(got, enc_grad, dec_rows)
        stages.append(got)
        return got

    dec_near, dec_far, _ = sum_gram(
        dec_gram,
        jnp.zeros((model_width,), f32),
        dec_note,
    )
    bias_term = jnp.sum(back_rows[:, :model_width], 0, dtype=f32) - jnp.dot(
        enc_own.astype(f32),
        encb_grad,
        precision=HIGH_PRECISION,
    )

    enc_own_next = (MOMENTUM * enc_moment_own.astype(f32) + enc_grad).astype(bf16)
    enc_gram = lax.dot_general(
        enc_own_next, enc_own_next, to_latents, preferred_element_type=f32
    )
    enc_gram, dec_near = lax.optimization_barrier((enc_gram, dec_near))
    enc_momenta = lax.all_gather(enc_own_next, "narrow")
    progress = []

    def dec_fill(sents, got):
        step = len(progress)
        if step == 0:
            early, _ = tie(dec_near, sents)
            state = series_start(place, early, dec_far)
        else:
            state = series_next(step, progress[-1])
        got, state = lax.optimization_barrier((got, state))
        progress.append(state)
        return got

    enc_near, enc_far, grad_decb = sum_gram(enc_gram, bias_term, dec_fill)
    dec_factor = progress[-1][0]
    dec_ortho = rows_of(
        jnp.dot(dec_factor, dec_own_next, preferred_element_type=f32).astype(bf16)
    )
    step_scale = MUON_RATE * 0.2 * math.sqrt(max(D, L))
    dec_next = MOMENTUM * dec_moment_t + dec_rows.astype(f32)
    dec_new = dec_weight_t * (1.0 - MUON_RATE * DECAY) - step_scale * dec_ortho.astype(f32)
    dec_copy = dec_new.astype(bf16)
    state = series_start(place, enc_near, enc_far)
    for step in range(1, NS_STEPS):
        state = series_next(step, state)
    enc_new, enc_next, enc_copy = finish(place, state[0], enc_momenta, enc_weight)
    encb_new, encb_one, encb_two = adam_update(enc_bias, encb_grad, encb_first, encb_second)
    decb_new, decb_one, decb_two = adam_update(decoder_bias, grad_decb, decb_first, decb_second)
    return (
        token_loss,
        enc_new,
        enc_next,
        enc_copy,
        dec_new.T,
        dec_next.T,
        dec_copy.T,
        encb_new,
        encb_one,
        encb_two,
        decb_new,
        decb_one,
        decb_two,
    )


def solution(mesh):
    wide, narrow = mesh.devices.shape
    fine = Mesh(mesh.devices.reshape(wide // 2, 2, narrow), ("chip", "core", "narrow"))
    placed = (
        P(("chip", "core", "narrow")),
        P(("chip", "core", "narrow")),
        P(("chip", "core", "narrow"), None),
        P(("chip", "core", "narrow"), None),
        P(),
        P(("chip", "core"), None),
        P(),
        P(),
        P(),
        P(),
        P(),
        P(),
        P(),
        P("narrow", ("chip", "core")),
        P(("chip", "core", "narrow")),
        P(("chip", "core"), "narrow"),
        P(),
        P("narrow", ("chip", "core")),
        P(("chip", "core"), "narrow"),
        P(("chip", "core", "narrow")),
        P(("chip", "core", "narrow")),
        P(),
        P(),
    )
    return jax.shard_map(
        local,
        mesh=fine,
        in_specs=placed,
        out_specs=(
            P(("chip", "core", "narrow")),
            P("narrow", ("chip", "core")),
            P("narrow", ("chip", "core")),
            P("narrow", ("chip", "core")),
            P(("chip", "core"), "narrow"),
            P(("chip", "core"), "narrow"),
            P(("chip", "core"), "narrow"),
            P(("chip", "core", "narrow")),
            P(("chip", "core", "narrow")),
            P(("chip", "core", "narrow")),
            P(),
            P(),
            P(),
        ),
        check_vma=False,
    )
```

```python
import functools
import math

import jax
import jax.numpy as jnp
from jax import lax
from jax.experimental import pallas as pl
from jax.experimental.pallas import tpu as pltpu
from jax.sharding import Mesh
from jax.sharding import PartitionSpec as P

D = 768
HEAD_DIM = 64
L = 32768
NS_STEPS = 5
STEP = 10


HIGH_PRECISION = lax.Precision.HIGHEST
AUX_COEF = 1.0 / 32.0
EPS_NORM = 1e-05
NS_EPS = 1e-07
QA = 3.4445
QB = -4.775
QC = 2.0315
MOMENTUM = 0.95
MUON_RATE = 0.1
DECAY = 0.1
BIAS_RATE = 0.3
BETA_ONE = 0.9
BETA_TWO = 0.999
ADAM_EPS = 1e-08


def layer_norm(value, gain, shift):
    row_mean = jnp.mean(value, -1, keepdims=True)
    centred = value - row_mean
    row_var = jnp.mean(centred * centred, -1, keepdims=True)
    return centred * lax.rsqrt(row_var + EPS_NORM) * gain + shift


def frozen_block(start, ctx_length, ln_gains, frozen_bias, w_qkv, w_proj, w_fc, w_out):
    row_count, model_width = start.shape
    head_count = model_width // HEAD_DIM
    ff_width = w_fc.shape[1]
    shifts = frozen_bias[: 2 * model_width].reshape(2, model_width)
    b_qkv = frozen_bias[2 * model_width : 5 * model_width]
    b_proj = frozen_bias[5 * model_width : 6 * model_width]
    b_fc = frozen_bias[6 * model_width : 6 * model_width + ff_width]
    b_out = frozen_bias[6 * model_width + ff_width :]
    normed = layer_norm(start, ln_gains[0], shifts[0]).astype(jnp.bfloat16)
    qkv_rows = (jnp.dot(normed, w_qkv, preferred_element_type=jnp.float32) + b_qkv).astype(
        jnp.bfloat16
    )
    head_split = qkv_rows.reshape(row_count, 3, head_count, HEAD_DIM)
    scores = jnp.einsum(
        "qhd,khd->hqk", head_split[:, 0], head_split[:, 1], preferred_element_type=jnp.float32
    ) * HEAD_DIM ** (-0.5)
    positions = jnp.arange(row_count)
    allowed = (positions[None, :] <= positions[:, None]) & (positions[None, :] < ctx_length)
    attn_probs = jax.nn.softmax(jnp.where(allowed[None], scores, -1e30), axis=-1).astype(
        jnp.bfloat16
    )
    mixed = jnp.einsum(
        "hqk,khd->qhd", attn_probs, head_split[:, 2], preferred_element_type=jnp.float32
    )
    mixed = mixed.reshape(row_count, model_width).astype(jnp.bfloat16)
    hidden = start + jnp.dot(mixed, w_proj, preferred_element_type=jnp.float32) + b_proj
    normed_two = layer_norm(hidden, ln_gains[1], shifts[1]).astype(jnp.bfloat16)
    inner_acts = jax.nn.gelu(
        jnp.dot(normed_two, w_fc, preferred_element_type=jnp.float32) + b_fc, approximate=True
    ).astype(jnp.bfloat16)
    return (hidden + jnp.dot(inner_acts, w_out, preferred_element_type=jnp.float32) + b_out).astype(
        jnp.bfloat16
    )


def split_bf(value):
    high = value.astype(jnp.bfloat16)
    return high, (value - high.astype(jnp.float32)).astype(jnp.bfloat16)


def row_blocks(size, body):
    block = 256

    def step(index, carry):
        body(pl.ds(pl.multiple_of(index * block, block), block), index * block)
        return carry

    lax.fori_loop(0, size // block, step, 0)


def eye_rows(start, size):
    rows = lax.broadcasted_iota(jnp.int32, (256, size), 0) + start
    cols = lax.broadcasted_iota(jnp.int32, (256, size), 1)
    return (rows == cols).astype(jnp.float32)


def dot_f32(a, b):
    return jnp.dot(a, b, preferred_element_type=jnp.float32)


def store_split(pair, rows, value):
    pair[0][rows, :], pair[1][rows, :] = split_bf(value)


def three(left, right, rows):
    high, low = left[0][rows, :], left[1][rows, :]
    return dot_f32(high, right[0][...]) + (
        dot_f32(high, right[1][...]) + dot_f32(low, right[0][...])
    )


def series_step(gram, poly, half, out, old, new, step):
    size = gram[0].shape[0]
    last = step == NS_STEPS - 1
    exact_square = step >= 3

    def poly_rows(rows, start):
        here = gram[0][rows, :].astype(jnp.float32) + gram[1][rows, :].astype(jnp.float32)
        if exact_square:
            square = three(gram, gram, rows)
        else:
            square = dot_f32(gram[0][rows, :], gram[0][...])
        store_split(poly, rows, QA * eye_rows(start, size) + QB * here + QC * square)

    def half_rows(rows, start):
        store_split(half, rows, three(gram, poly, rows))

    def gram_rows(rows, start):
        store_split(out, rows, three(poly, half, rows))

    def product_rows(rows, start):
        new[rows, :] = dot_f32(poly[0][rows, :], old[...]).astype(jnp.bfloat16)

    row_blocks(size, poly_rows)
    if not last:
        row_blocks(size, half_rows)
        row_blocks(size, gram_rows)
    if step > 0:
        row_blocks(size, product_rows)


def first_kernel(place_ref, near_ref, far_ref, o_hi, o_lo, q_ref, total, *scratch):
    size = total.shape[0]
    chips, rows_each = near_ref.shape[:2]
    chip, core = place_ref[0], place_ref[1]
    gram, poly, half = scratch[:2], scratch[2:4], scratch[4:6]
    for offset in range(chips):
        for side, source in enumerate((near_ref, far_ref)):
            first = jnp.bitwise_xor(core, side) * (size // 2)
            first = first + jnp.bitwise_xor(chip, offset) * rows_each
            total[pl.ds(pl.multiple_of(first, 8), rows_each), :] = source[offset].astype(
                jnp.float32
            )

    def trace_part(index, value):
        start = pl.multiple_of(index * 256, 256)
        return value + jnp.sum(total[pl.ds(start, 256), :] * eye_rows(start, size))

    trace_sum = lax.fori_loop(0, size // 256, trace_part, jnp.zeros((), jnp.float32))
    scale = 1.0 / (jnp.sqrt(jnp.full((1, 1), trace_sum)) + NS_EPS)

    def load_rows(rows, start):
        store_split(gram, rows, total[rows, :] * (scale * scale))

    row_blocks(size, load_rows)
    series_step(gram, poly, half, (o_hi, o_lo), None, None, 0)

    def product_rows(rows, start):
        value = poly[0][rows, :].astype(jnp.float32) + poly[1][rows, :].astype(jnp.float32)
        q_ref[rows, :] = (value * scale).astype(jnp.bfloat16)

    row_blocks(size, product_rows)


def middle_kernel(step, g_hi, g_lo, q_ref, o_hi, o_lo, out_ref, *scratch):
    series_step(
        (g_hi, g_lo), scratch[:2], scratch[2:4], (o_hi, o_lo), q_ref, out_ref, step
    )


def last_kernel(g_hi, g_lo, q_ref, out_ref, *scratch):
    series_step((g_hi, g_lo), scratch[:2], None, None, q_ref, out_ref, NS_STEPS - 1)


def square_call(kernel, outs, scratch, passes, *operands):
    size = operands[-1].shape[-1]
    whole = pl.BlockSpec(memory_space=pltpu.VMEM)
    specs = [whole] * len(operands)
    if operands[0].ndim == 1:
        specs[0] = pl.BlockSpec(memory_space=pltpu.SMEM)
    square = jax.ShapeDtypeStruct((size, size), jnp.bfloat16)
    return pl.pallas_call(
        kernel,
        out_shape=[square] * outs,
        in_specs=specs,
        out_specs=[whole] * outs,
        scratch_shapes=[pltpu.VMEM((size, size), kind) for kind in scratch],
        compiler_params=pltpu.CompilerParams(vmem_limit_bytes=40 * 2**20),
        cost_estimate=pl.CostEstimate(
            flops=passes * size**3 // 16, bytes_accessed=size * size // 2, transcendentals=0
        ),
    )(*operands)


def series_start(place, near, far):
    bf16 = jnp.bfloat16
    return square_call(first_kernel, 3, [jnp.float32] + [bf16] * 6, 8, place, near, far)


def series_next(step, state):
    bf16 = jnp.bfloat16
    if step == NS_STEPS - 1:
        return square_call(last_kernel, 1, [bf16] * 2, 4, *state)
    kernel = functools.partial(middle_kernel, step)
    return square_call(kernel, 3, [bf16] * 4, 8 if step < 3 else 10, *state)


def code_kernel(shifts, place_ref, ids_ref, out_ref, high, low, stage):
    wide_shift, own_shift, top_count, orders = shifts
    batch, groups = stage.shape[:2]
    rows, picks = ids_ref.shape
    bf16, f32 = jnp.bfloat16, jnp.float32
    chip, core, narrow = place_ref[0], place_ref[1], place_ref[2]
    latent_count = out_ref.shape[1]
    half_shift = own_shift - 1

    ids = ids_ref[...]
    owner = lax.shift_right_logical(ids, wide_shift)
    within = jnp.bitwise_and(ids, (1 << wide_shift) - 1)
    mine = (lax.shift_right_logical(within, own_shift) == narrow) & (
        jnp.bitwise_and(owner, 1) == core
    )
    inner = jnp.bitwise_and(within, (1 << own_shift) - 1)
    offset = jnp.bitwise_xor(lax.shift_right_logical(owner, 1), chip)
    half = lax.shift_right_logical(inner, half_shift)
    spots = []
    for order in orders:
        spot = jnp.zeros_like(offset)
        for index, bit in enumerate(order[:-1]):
            spot = spot + jnp.where(jnp.bitwise_and(offset, bit) != 0, 1 << index, 0)
        sent = jnp.where(jnp.bitwise_and(offset, order[-1]) != 0, latent_count // 4, 0)
        spots.append(sent + lax.shift_left(spot, half_shift))
    column = (
        half * (latent_count // 2)
        + jnp.where(half == 0, spots[0], spots[1])
        + jnp.bitwise_and(inner, (1 << half_shift) - 1)
    )
    high[...] = jnp.where(mine, lax.shift_right_logical(column, 7), -1).astype(f32)
    low[...] = jnp.bitwise_and(column, 127).astype(f32)

    one, zero = jnp.ones((16, picks), bf16), jnp.zeros((16, picks), bf16)
    places = lax.broadcasted_iota(jnp.int32, (16, picks), 1)
    kinds = jnp.where(places < top_count, 1.0, 2.0).astype(bf16)
    steps = lax.broadcasted_iota(jnp.int32, (16, picks), 0).astype(f32).astype(bf16)

    def hot(row, count, value):
        row = jnp.broadcast_to(row, (16, picks)).astype(bf16)
        parts = [
            jnp.where(steps + jnp.asarray(16 * part, bf16) == row, value, zero)
            for part in range(max(1, count // 16))
        ]
        return jnp.concatenate(parts, 0).astype(jnp.float8_e4m3fn)

    def one_batch(index, carry):
        first = pl.multiple_of(index * batch, batch)
        for token in range(batch):
            row = pl.ds(first + token, 1)
            codes = lax.dot_general(
                hot(high[row, :], groups, kinds),
                hot(low[row, :], 128, one),
                (((1,), (1,)), ((), ())),
                preferred_element_type=f32,
            )
            stage[token] = codes[:groups]
        for group in range(groups):
            lanes = slice(group * 128, (group + 1) * 128)
            out_ref[pl.ds(first, batch), lanes] = stage[:, group, :].astype(bf16)
        return carry

    lax.fori_loop(0, rows // batch, one_batch, 0)


def kind_codes(place, ids, latent_count, sizes):
    wide_latents, own_latents, top_count, orders = sizes
    row_total, pick_total = ids.shape
    rows = min(128, row_total)
    shifts = (wide_latents.bit_length() - 1, own_latents.bit_length() - 1, top_count, orders)
    return pl.pallas_call(
        functools.partial(code_kernel, shifts),
        grid=(row_total // rows,),
        out_shape=jax.ShapeDtypeStruct((row_total, latent_count), jnp.bfloat16),
        in_specs=[
            pl.BlockSpec(memory_space=pltpu.SMEM),
            pl.BlockSpec((rows, pick_total), lambda i: (i, 0)),
        ],
        out_specs=pl.BlockSpec((rows, latent_count), lambda i: (i, 0)),
        scratch_shapes=[
            pltpu.VMEM((rows, pick_total), jnp.float32),
            pltpu.VMEM((rows, pick_total), jnp.float32),
            pltpu.VMEM((32, latent_count // 128, 128), jnp.float32),
        ],
        compiler_params=pltpu.CompilerParams(vmem_limit_bytes=40 * 2**20),
        cost_estimate=pl.CostEstimate(
            flops=row_total * latent_count,
            bytes_accessed=row_total * pick_total,
            transcendentals=0,
        ),
    )(place, ids)


def join_rows(sources, target):
    rows = sources[0].shape[0]
    for index, source in enumerate(sources):
        target[index * rows : (index + 1) * rows, :] = source[...]


def pick_copy(step, count, sources, target):
    for index, source in enumerate(sources):

        @pl.when(step // count == index)
        def _(source=source):
            target[...] = source[...]


def forward_kernel(count, x_ref, dead_ref, *refs):
    code_parts, encs, decs = refs[:4], refs[4:8], refs[8:12]
    top_ref, aux_ref, far_ref, near_ref = refs[12:16]
    codes_ref, enc, dec, acc_top, acc_aux = refs[16:]
    join_rows(code_parts, codes_ref)
    step = pl.program_id(0)
    rows_all, width = x_ref.shape
    block = min(1024, rows_all)
    pick_copy(step, count, encs, enc)
    pick_copy(step, count, decs, dec)

    @pl.when(step == 0)
    def _():
        acc_top[...] = jnp.zeros_like(acc_top)
        acc_aux[...] = jnp.zeros_like(acc_aux)

    bias = enc[pl.ds(width, 16), :].astype(jnp.float32)[:1]
    to_features = (((1,), (1,)), ((), ()))

    def one(index, carry):
        rows = pl.ds(pl.multiple_of(index * block, block), block)
        pre = dot_f32(x_ref[rows, :], enc[pl.ds(0, width), :]) + bias
        codes = codes_ref[rows, :]
        zero = jnp.zeros(codes.shape, jnp.bfloat16)
        top = jnp.where(codes == 1.0, pre.astype(jnp.bfloat16), zero)
        aux = jnp.where(codes == 2.0, (pre * dead_ref[...]).astype(jnp.bfloat16), zero)
        top_ref[rows, :] = top
        aux_ref[rows, :] = aux
        acc_top[rows, :] += lax.dot_general(
            top, dec[...], to_features, preferred_element_type=jnp.float32
        )
        acc_aux[rows, :] += lax.dot_general(
            aux, dec[...], to_features, preferred_element_type=jnp.float32
        )
        return carry

    lax.fori_loop(0, rows_all // block, one, 0)

    @pl.when(step == pl.num_programs(0) - 1)
    def _():
        half = rows_all // 2
        for first, acc in ((0, acc_top), (width, acc_aux)):
            near_ref[:, first : first + width] = acc[pl.ds(0, half), :]
            far_ref[:, first : first + width] = acc[pl.ds(half, half), :].astype(jnp.bfloat16)


def part_specs(shape, axis, block, count, starts):
    specs = []
    for index, first in enumerate(starts):

        def place(step, index=index, first=first):
            spot = jnp.clip(step - index * count, 0, count - 1)
            return (spot + first, 0) if axis == 0 else (0, spot + first)

        size = (block, shape[1]) if axis == 0 else (shape[0], block)
        specs.append(pl.BlockSpec(size, place))
    return specs


def forward(x, codes, dead, encs, decs):
    rows, width = x.shape
    acts_shape = (rows, dead.shape[1])
    quarter = encs[0].shape[1]
    block = min(512, quarter)
    count = quarter // block
    lanes = pl.BlockSpec((rows, block), lambda step: (0, step))
    fixed = lambda shape: pl.BlockSpec(shape, lambda step: (0, 0))
    bf16, f32 = jnp.bfloat16, jnp.float32
    half_shape = (rows // 2, 2 * width)
    return pl.pallas_call(
        functools.partial(forward_kernel, count),
        grid=(4 * count,),
        out_shape=[
            jax.ShapeDtypeStruct(acts_shape, bf16),
            jax.ShapeDtypeStruct(acts_shape, bf16),
            jax.ShapeDtypeStruct(half_shape, bf16),
            jax.ShapeDtypeStruct(half_shape, f32),
        ],
        in_specs=[fixed(x.shape), pl.BlockSpec((1, block), lambda step: (0, step))]
        + [pl.BlockSpec((rows // 4, block), lambda step: (0, step))] * 4
        + part_specs(encs[0].shape, 1, block, count, (0, 0, 0, 0))
        + part_specs(decs[0].shape, 1, block, count, (0, 0, 0, 0)),
        out_specs=[lanes, lanes, fixed(half_shape), fixed(half_shape)],
        scratch_shapes=[
            pltpu.VMEM((rows, block), bf16),
            pltpu.VMEM((width + 16, block), bf16),
            pltpu.VMEM((width, block), bf16),
            pltpu.VMEM((rows, width), f32),
            pltpu.VMEM((rows, width), f32),
        ],
        compiler_params=pltpu.CompilerParams(vmem_limit_bytes=58 * 2**20),
        cost_estimate=pl.CostEstimate(
            flops=2 * rows * width * dead.shape[1],
            bytes_accessed=6 * rows * dead.shape[1],
            transcendentals=0,
        ),
    )(x, dead, *codes, *encs, *decs)


def store_part(count, refs, rows, value):
    step = pl.program_id(0)
    for index, ref in enumerate(refs):

        @pl.when(step // count == index)
        def _(ref=ref):
            ref[rows, :] = value.astype(ref.dtype)


def dec_grad_kernel(count, near_r, near_a, far_r, far_a, top_ref, aux_ref, *outs):
    half = near_r.shape[1]

    def one(index, carry):
        rows = pl.ds(pl.multiple_of(index * 384, 384), 384)
        value = dot_f32(near_r[rows, :], top_ref[:half, :])
        value = value + dot_f32(near_a[rows, :], aux_ref[:half, :])
        value = value + dot_f32(far_r[rows, :], top_ref[half:, :])
        value = value + dot_f32(far_a[rows, :], aux_ref[half:, :])
        store_part(count, outs, rows, value)
        return carry

    lax.fori_loop(0, near_r.shape[0] // 384, one, 0)


def dec_grads(near_t, far_t, top_acts, aux_acts, quarters, kind):
    width = near_t.shape[0] // 2
    rows, latents = top_acts.shape
    quarter = latents // 4
    block = min(512, quarter)
    count = quarter // block

    def lanes(step):
        return (0, jnp.where(step < count, quarters[0], quarters[1] - 1) * count + step)

    acts = pl.BlockSpec((rows, block), lanes)
    shape = (width, quarter)
    return pl.pallas_call(
        functools.partial(dec_grad_kernel, count),
        grid=(2 * count,),
        out_shape=[jax.ShapeDtypeStruct(shape, kind)] * 2,
        in_specs=[
            pl.BlockSpec((width, rows // 2), lambda step: (0, 0)),
            pl.BlockSpec((width, rows // 2), lambda step: (1, 0)),
            pl.BlockSpec((width, rows // 2), lambda step: (0, 0)),
            pl.BlockSpec((width, rows // 2), lambda step: (1, 0)),
            acts,
            acts,
        ],
        out_specs=part_specs(shape, 1, block, count, (0, 0)),
        compiler_params=pltpu.CompilerParams(vmem_limit_bytes=58 * 2**20),
        cost_estimate=pl.CostEstimate(
            flops=rows * width * quarter // 8, bytes_accessed=rows * quarter // 4, transcendentals=0
        ),
    )(near_t, near_t, far_t, far_t, top_acts, aux_acts)


def enc_grad_kernel(count, x_ref, near_ref, far_ref, dead_ref, *refs):
    code_parts, (dec_a, dec_b, out_a, out_b, dec, grads) = refs[:4], refs[4:]
    step = pl.program_id(0)
    pick_copy(step, count, (dec_a, dec_b), dec)
    width, latents = dec.shape
    quarter = code_parts[0].shape[0]
    total = jnp.zeros((1, latents), jnp.float32)
    for index, back_ref in enumerate((near_ref, far_ref)):
        top = dot_f32(back_ref[:, :width], dec[...])
        aux = dot_f32(back_ref[:, width:], dec[...]) * dead_ref[...]
        for part in range(2):
            codes = code_parts[2 * index + part][...].astype(jnp.float32)
            lines = slice(part * quarter, (part + 1) * quarter)
            value = jnp.where(codes == 2.0, aux[lines], 0.0)
            value = jnp.where(codes == 1.0, top[lines], value).astype(jnp.bfloat16)
            first = (2 * index + part) * quarter
            grads[first : first + quarter, :] = value
            total = total + jnp.sum(value.astype(jnp.float32), 0, keepdims=True)

    def two(index, carry):
        rows = pl.ds(pl.multiple_of(index * 384, 384), 384)
        store_part(count, (out_a, out_b), rows, dot_f32(x_ref[rows, :], grads[...]))
        return carry

    lax.fori_loop(0, width // 384, two, 0)
    lines = lax.broadcasted_iota(jnp.int32, (16, latents), 0)
    if out_a.dtype == jnp.bfloat16:
        high = total.astype(jnp.bfloat16).astype(jnp.float32)
        lines = jnp.where(lines == 0, high, jnp.where(lines == 1, total - high, 0.0))
    else:
        lines = jnp.where(lines == 0, total, 0.0)
    store_part(count, (out_a, out_b), pl.ds(width, 16), lines)


def enc_grads(x_t, near, far, codes, dead, parts, quarters, kind):
    width, rows = x_t.shape
    quarter = dead.shape[1] // 4
    block = min(512, quarter)
    count = quarter // block

    def lanes(step):
        return (0, jnp.where(step < count, quarters[0], quarters[1] - 1) * count + step)

    shape = (width + 16, quarter)
    return pl.pallas_call(
        functools.partial(enc_grad_kernel, count),
        grid=(2 * count,),
        out_shape=[jax.ShapeDtypeStruct(shape, kind)] * 2,
        in_specs=[
            pl.BlockSpec(x_t.shape, lambda step: (0, 0)),
            pl.BlockSpec(near.shape, lambda step: (0, 0)),
            pl.BlockSpec(far.shape, lambda step: (0, 0)),
            pl.BlockSpec((1, block), lanes),
        ]
        + [pl.BlockSpec((rows // 4, block), lanes)] * 4
        + part_specs(parts[0].shape, 1, block, count, (0, 0)),
        out_specs=part_specs(shape, 1, block, count, (0, 0)),
        scratch_shapes=[
            pltpu.VMEM((width, block), jnp.bfloat16),
            pltpu.VMEM((rows, block), jnp.bfloat16),
        ],
        compiler_params=pltpu.CompilerParams(vmem_limit_bytes=58 * 2**20),
        cost_estimate=pl.CostEstimate(
            flops=rows * width * quarter // 8, bytes_accessed=rows * quarter // 4, transcendentals=0
        ),
    )(x_t, near, far, dead, *codes, *parts)


def finish_kernel(place_ref, factor_ref, momentum_ref, weight_ref, *outs):
    new_ref, next_ref, copy_ref = outs
    rows = factor_ref.shape[0]
    f32 = jnp.float32
    momentum = momentum_ref[0]
    kept = momentum_ref[0, pl.ds(pl.multiple_of(place_ref[2] * rows, 16), rows), :].astype(f32)
    ortho = dot_f32(factor_ref[...], momentum)
    next_ref[...] = kept
    step_scale = MUON_RATE * 0.2 * math.sqrt(max(D, L))
    value = weight_ref[...] * (1.0 - MUON_RATE * DECAY) - step_scale * ortho
    new_ref[...] = value
    copy_ref[...] = value.astype(jnp.bfloat16)


def finish(place, factor, momenta, weight):
    count, width, block = momenta.shape
    rows = weight.shape[0]
    part = pl.BlockSpec((rows, block), lambda step, place: (0, step))
    return pl.pallas_call(
        finish_kernel,
        grid_spec=pltpu.PrefetchScalarGridSpec(
            num_scalar_prefetch=1,
            grid=(count,),
            in_specs=[
                pl.BlockSpec((rows, width), lambda step, place: (place[2], 0)),
                pl.BlockSpec((1, width, block), lambda step, place: (step, 0, 0)),
                part,
            ],
            out_specs=[part] * 3,
        ),
        out_shape=[
            jax.ShapeDtypeStruct(weight.shape, jnp.float32),
            jax.ShapeDtypeStruct(weight.shape, jnp.float32),
            jax.ShapeDtypeStruct(weight.shape, jnp.bfloat16),
        ],
        compiler_params=pltpu.CompilerParams(vmem_limit_bytes=58 * 2**20),
        cost_estimate=pl.CostEstimate(
            flops=2 * rows * width * block * count,
            bytes_accessed=8 * rows * block * count,
            transcendentals=0,
        ),
    )(place, factor, momenta, weight)


def adam_update(param, grad, first, second):
    first = BETA_ONE * first + (1.0 - BETA_ONE) * grad
    second = BETA_TWO * second + (1.0 - BETA_TWO) * grad * grad
    denom = jnp.sqrt(second / (1.0 - BETA_TWO**STEP)) + ADAM_EPS
    return (param - BIAS_RATE * (first / (1.0 - BETA_ONE**STEP)) / denom, first, second)


def local(
    token_ids,
    lengths,
    top_ids,
    aux_ids,
    dead_set,
    token_table,
    position_table,
    ln_gains,
    frozen_bias,
    w_qkv,
    w_proj,
    w_fc,
    w_out,
    enc_weight,
    enc_bias,
    dec_weight,
    decoder_bias,
    enc_moment,
    dec_moment,
    encb_first,
    encb_second,
    decb_first,
    decb_second,
):
    chips = lax.axis_size("chip")
    narrow_count = lax.axis_size("narrow")
    wide_count = 2 * chips
    wide = ("chip", "core")
    chip_pos = lax.axis_index("chip")
    core_pos = lax.axis_index("core")
    wide_pos = 2 * chip_pos + core_pos
    narrow_pos = lax.axis_index("narrow")
    row_count = token_ids.shape[0]
    model_width = token_table.shape[1]
    wide_latents = enc_weight.shape[1]
    own_latents = wide_latents // narrow_count
    half_latents = own_latents // 2
    latent_count = chips * own_latents
    core_rows = narrow_count * row_count
    bf16, f32 = jnp.bfloat16, jnp.float32
    to_latents = (((1,), (1,)), ((), ()))
    over_rows = (((0,), (0,)), ((), ()))
    place = jnp.stack([chip_pos, core_pos, narrow_pos]).astype(jnp.int32)
    bits = [1 << bit for bit in range(chips.bit_length() - 1)]
    orders = (bits, bits[::-1])

    tie = lambda *values: lax.optimization_barrier(values)

    def swap(value, axis, offset):
        count = lax.axis_size(axis)
        return lax.ppermute(value, axis, [(spot, spot ^ offset) for spot in range(count)])

    def spread_narrow(value):
        parts = [value] + [swap(value, "narrow", k) for k in range(1, narrow_count)]
        return jnp.concatenate(parts, 0)

    def rows_to_latents(value):
        return lax.all_to_all(value, "narrow", split_axis=1, concat_axis=0, tiled=True)

    def rows_of(value):
        return lax.all_to_all(value, "narrow", split_axis=0, concat_axis=1, tiled=True)

    def gather_start(own, axis):
        halves = []
        for part, order in enumerate(orders):
            held = lax.slice_in_dim(own, part * half_latents, (part + 1) * half_latents, axis=axis)
            for bit in order[:-1]:
                held = jnp.concatenate([held, swap(held, "chip", bit)], axis)
            halves.append(held)
        return halves

    def gather_end(halves):
        pieces = []
        for held, order in zip(halves, orders):
            pieces += [held, swap(held, "chip", order[-1])]
        return pieces

    def scatter_chips(keeps, gots):
        results, sums = [], []
        for order, held, got in zip(orders, keeps, gots):
            held = held + got.astype(f32)
            for bit in reversed(order[:-1]):
                lower, upper = jnp.split(held, 2, 1)
                sent = upper[:model_width].astype(bf16)
                if held.shape[0] > model_width:
                    lines = split_bf(upper[model_width] + upper[model_width + 1])
                    spare = jnp.zeros((14, upper.shape[1]), bf16)
                    sent = jnp.concatenate([sent, *(line[None] for line in lines), spare], 0)
                held = lower + swap(sent, "chip", bit).astype(f32)
            results.append(held[:model_width])
            if held.shape[0] > model_width:
                sums.append(held[model_width] + held[model_width + 1])
        return jnp.concatenate(results, 1), jnp.concatenate(sums) if sums else None

    vocab_dev = token_table.shape[0]
    every_ids = lax.all_gather(token_ids, wide, axis=0, tiled=False).reshape(wide_count, row_count)
    every_ids = jnp.concatenate(
        [
            lax.dynamic_slice_in_dim(every_ids, wide_pos ^ offset, 1, 0)
            for offset in range(wide_count)
        ],
        1,
    )[0]
    local_ids = every_ids - wide_pos * vocab_dev
    inside = (local_ids >= 0) & (local_ids < vocab_dev)
    looked = jnp.take(token_table, jnp.clip(local_ids, 0, vocab_dev - 1), axis=0)
    looked = jnp.where(inside[:, None], looked, jnp.zeros((), bf16))
    dec_weight_t, dec_moment_t = dec_weight.T, dec_moment.T
    rows_each = enc_weight.shape[0]
    enc_own = rows_to_latents(enc_weight.astype(bf16))
    picks = jnp.concatenate([top_ids, aux_ids], 1)
    near_picks = spread_narrow(picks)
    far_picks = swap(near_picks, "core", 1)

    looked = looked.reshape(chips, 2, row_count, model_width)
    looked = looked[:, 0] + swap(looked[:, 1], "core", 1)
    embedded = looked[0].astype(f32)
    for k in range(1, chips):
        embedded = embedded + swap(looked[k], "chip", k).astype(f32)

    bias_rows = jnp.concatenate(
        [enc_bias.astype(bf16)[None], jnp.zeros((15, own_latents), bf16)], 0
    )
    enc_own, embedded = tie(enc_own, embedded)
    dec_cast, enc_own = tie(dec_weight_t.astype(bf16), enc_own)
    dec_own = rows_to_latents(dec_cast)
    enc_halves = gather_start(jnp.concatenate([enc_own, bias_rows], 0), 1)

    dead_here = jnp.stack(
        [
            lax.dynamic_slice_in_dim(
                dead_set,
                (2 * (chip_pos ^ offset) + core_pos) * wide_latents + narrow_pos * own_latents,
                own_latents,
            )
            for offset in range(chips)
        ]
    )
    places = [0]
    dead_parts = []
    for part, order in enumerate(orders):
        places = [0]
        for bit in order:
            places = places + [spot ^ bit for spot in places]
        for spot in places:
            dead_parts.append(dead_here[spot, part * half_latents : (part + 1) * half_latents])
    dead_here = jnp.concatenate(dead_parts)[None].astype(f32)
    sizes = (wide_latents, own_latents, top_ids.shape[1], orders)
    near_picks, dead_here, embedded = tie(near_picks, dead_here, embedded)
    start = embedded + position_table[:row_count].astype(f32)
    ctx_length = lengths[0]
    inputs = frozen_block(start, ctx_length, ln_gains, frozen_bias, w_qkv, w_proj, w_fc, w_out)
    counted = (jnp.arange(row_count) < ctx_length).astype(f32)
    near_picks, inputs, enc_halves = tie(near_picks, inputs, enc_halves)
    enc_parts = gather_end(enc_halves)
    got_inputs = [swap(inputs, "narrow", k) for k in range(1, narrow_count)]
    half_rows = core_rows // 2
    codes = [kind_codes(place, near_picks[:half_rows], latent_count, sizes)]
    enc_lasts = [enc_parts[1], enc_parts[3]]
    dec_own, codes, got_inputs, enc_lasts = tie(dec_own, codes, got_inputs, enc_lasts)
    near_picks, codes = tie(near_picks, codes)
    dec_halves = gather_start(dec_own, 1)
    codes = [*codes, kind_codes(place, near_picks[half_rows:], latent_count, sizes)]
    dec_halves, codes = tie(dec_halves, codes)
    enc_parts = [enc_parts[0], enc_lasts[0], enc_parts[2], enc_lasts[1]]
    dec_parts = gather_end(dec_halves)
    moments = jnp.concatenate([enc_moment.astype(bf16), dec_moment_t.astype(bf16)], 0)
    moments, got_inputs = tie(moments, got_inputs)
    moments = rows_to_latents(moments)
    near_inputs = jnp.concatenate([inputs, *got_inputs], 0)
    far_picks, codes = tie(far_picks, codes)
    codes = [*codes, kind_codes(place, far_picks[:half_rows], latent_count, sizes)]
    far_inputs, codes = tie(swap(near_inputs, "core", 1), codes)
    far_picks, codes = tie(far_picks, codes)
    codes = [*codes, kind_codes(place, far_picks[half_rows:], latent_count, sizes)]
    all_inputs = jnp.concatenate([near_inputs, far_inputs], 0)
    encoder_in = (all_inputs.astype(f32) - decoder_bias).astype(bf16)
    top_acts, aux_acts, far, near = forward(encoder_in, codes, dead_here, enc_parts, dec_parts)
    encoder_t = encoder_in.T
    far_got, encoder_t = tie(swap(far, "core", 1), encoder_t)
    rebuilt = near + far_got.astype(f32)
    rounded = rebuilt.astype(bf16)
    rebuilt = rebuilt[:row_count]
    for k in range(1, narrow_count):
        part = rounded[k * row_count : (k + 1) * row_count]
        rebuilt = rebuilt + swap(part, "narrow", k).astype(f32)
    target = inputs.astype(f32)
    reconstructed_input = rebuilt[:, :model_width] + decoder_bias
    auxiliary_reconstruction = rebuilt[:, model_width:]
    recon_error = target - reconstructed_input
    aux_gap = auxiliary_reconstruction - recon_error
    token_loss = (
        counted
        * (jnp.sum(recon_error * recon_error, 1) + AUX_COEF * jnp.sum(aux_gap * aux_gap, 1))
        / model_width
    )
    back_recon = 2.0 / model_width * counted[:, None] * (reconstructed_input - target)
    back_aux = 2.0 * AUX_COEF / model_width * counted[:, None] * aux_gap
    back_rows = jnp.concatenate([back_recon, back_aux], 1).astype(bf16)
    back_rows, moments = tie(back_rows, moments)
    near_back = spread_narrow(back_rows)
    far_back = swap(near_back, "core", 1)
    near_t, far_back = tie(near_back.T, far_back)
    far_t = far_back.T
    dec_sent = dec_grads(near_t, far_t, top_acts, aux_acts, (1, 3), bf16)
    moments = moments.reshape(narrow_count, 2, rows_each, own_latents)
    enc_moment_own = moments[:, 0].reshape(model_width, own_latents)
    dec_moment_own = moments[:, 1].reshape(model_width, own_latents)
    top_acts, dec_sent = tie(top_acts, dec_sent)
    dec_keep = dec_grads(near_t, far_t, top_acts, aux_acts, (0, 2), f32)
    far_back, dec_keep = tie(far_back, dec_keep)
    enc_sent = enc_grads(
        encoder_t, near_back, far_back, codes, dead_here, dec_parts[1::2], (1, 3), bf16
    )
    far_back, enc_sent = tie(far_back, enc_sent)
    enc_keep = enc_grads(
        encoder_t, near_back, far_back, codes, dead_here, dec_parts[::2], (0, 2), f32
    )
    dec_gots = [swap(sent, "chip", order[-1]) for order, sent in zip(orders, dec_sent)]
    dec_gots, enc_sent = tie(dec_gots, enc_sent)
    enc_gots = [swap(sent, "chip", order[-1]) for order, sent in zip(orders, enc_sent)]
    dec_grad, _ = scatter_chips(dec_keep, dec_gots)
    def sum_gram(part, vector, fill):
        half = model_width // 2
        rows = half // chips
        spare = jnp.zeros((14, model_width), bf16)

        def pack(block, vector):
            lines = [line[None] for line in split_bf(vector)]
            return jnp.concatenate([block.astype(bf16), *lines, spare], 0)

        def unpack(got):
            got = got.astype(f32)
            return got[:-16], got[-16] + got[-15]

        def block_of(value, index, count):
            return lax.dynamic_slice_in_dim(value, index * count, count, 0)

        def exchange(sents, axis):
            got = [swap(sent, axis, k + 1) for k, sent in enumerate(sents)]
            return fill(sents, got)

        sent = pack(block_of(part, 1 - core_pos, half), vector)
        (got,) = exchange([sent], "core")
        got, more = unpack(got)
        part, vector = block_of(part, core_pos, half) + got, vector + more
        total = block_of(part, chip_pos, rows)
        sents = [pack(block_of(part, chip_pos ^ k, rows), vector) for k in range(1, chips)]
        for got in exchange(sents, "chip"):
            got, more = unpack(got)
            total, vector = total + got, vector + more
        for got in exchange([pack(total, vector)] * (narrow_count - 1), "narrow"):
            got, more = unpack(got)
            total, vector = total + got, vector + more
        total = total.astype(bf16)
        near = jnp.stack([total, *exchange([total] * (chips - 1), "chip")])
        (far,) = exchange([near], "core")
        return near, far, vector

    dec_own_next = (MOMENTUM * dec_moment_own.astype(f32) + dec_grad).astype(bf16)
    dec_rows, dec_own_next = tie(dec_grad.astype(bf16), dec_own_next)
    dec_rows = rows_of(dec_rows)
    dec_gram = lax.dot_general(
        dec_own_next, dec_own_next, to_latents, preferred_element_type=f32
    )
    dec_gram, enc_gots, enc_keep = tie(dec_gram, enc_gots, enc_keep)
    stages = []
    enc_grad = encb_grad = None

    def dec_note(sents, got):
        nonlocal enc_grad, encb_grad, dec_rows
        if not stages:
            enc_grad, encb_grad = scatter_chips(enc_keep, enc_gots)
        if len(stages) == 2:
            got, enc_grad, dec_rows = tie(got, enc_grad, dec_rows)
        stages.append(got)
        return got

    dec_near, dec_far, _ = sum_gram(
        dec_gram,
        jnp.zeros((model_width,), f32),
        dec_note,
    )
    bias_term = jnp.sum(back_rows[:, :model_width], 0, dtype=f32) - jnp.dot(
        enc_own.astype(f32),
        encb_grad,
        precision=HIGH_PRECISION,
    )

    enc_own_next = (MOMENTUM * enc_moment_own.astype(f32) + enc_grad).astype(bf16)
    enc_gram = lax.dot_general(
        enc_own_next, enc_own_next, to_latents, preferred_element_type=f32
    )
    enc_gram, dec_near = lax.optimization_barrier((enc_gram, dec_near))
    enc_momenta = lax.all_gather(enc_own_next, "narrow")
    progress = []

    def dec_fill(sents, got):
        step = len(progress)
        if step == 0:
            early, _ = tie(dec_near, sents)
            state = series_start(place, early, dec_far)
        else:
            state = series_next(step, progress[-1])
        got, state = lax.optimization_barrier((got, state))
        progress.append(state)
        return got

    enc_near, enc_far, grad_decb = sum_gram(enc_gram, bias_term, dec_fill)
    dec_factor = progress[-1][0]
    dec_ortho = rows_of(
        jnp.dot(dec_factor, dec_own_next, preferred_element_type=f32).astype(bf16)
    )
    step_scale = MUON_RATE * 0.2 * math.sqrt(max(D, L))
    dec_next = MOMENTUM * dec_moment_t + dec_rows.astype(f32)
    dec_new = dec_weight_t * (1.0 - MUON_RATE * DECAY) - step_scale * dec_ortho.astype(f32)
    dec_copy = dec_new.astype(bf16)
    state = series_start(place, enc_near, enc_far)
    for step in range(1, NS_STEPS):
        state = series_next(step, state)
    enc_new, enc_next, enc_copy = finish(place, state[0], enc_momenta, enc_weight)
    encb_new, encb_one, encb_two = adam_update(enc_bias, encb_grad, encb_first, encb_second)
    decb_new, decb_one, decb_two = adam_update(decoder_bias, grad_decb, decb_first, decb_second)
    return (
        token_loss,
        enc_new,
        enc_next,
        enc_copy,
        dec_new.T,
        dec_next.T,
        dec_copy.T,
        encb_new,
        encb_one,
        encb_two,
        decb_new,
        decb_one,
        decb_two,
    )


def solution(mesh):
    wide, narrow = mesh.devices.shape
    fine = Mesh(mesh.devices.reshape(wide // 2, 2, narrow), ("chip", "core", "narrow"))
    placed = (
        P(("chip", "core", "narrow")),
        P(("chip", "core", "narrow")),
        P(("chip", "core", "narrow"), None),
        P(("chip", "core", "narrow"), None),
        P(),
        P(("chip", "core"), None),
        P(),
        P(),
        P(),
        P(),
        P(),
        P(),
        P(),
        P("narrow", ("chip", "core")),
        P(("chip", "core", "narrow")),
        P(("chip", "core"), "narrow"),
        P(),
        P("narrow", ("chip", "core")),
        P(("chip", "core"), "narrow"),
        P(("chip", "core", "narrow")),
        P(("chip", "core", "narrow")),
        P(),
        P(),
    )
    return jax.shard_map(
        local,
        mesh=fine,
        in_specs=placed,
        out_specs=(
            P(("chip", "core", "narrow")),
            P("narrow", ("chip", "core")),
            P("narrow", ("chip", "core")),
            P("narrow", ("chip", "core")),
            P(("chip", "core"), "narrow"),
            P(("chip", "core"), "narrow"),
            P(("chip", "core"), "narrow"),
            P(("chip", "core", "narrow")),
            P(("chip", "core", "narrow")),
            P(("chip", "core", "narrow")),
            P(),
            P(),
            P(),
        ),
        check_vma=False,
    )
```
